32 devices in a mesh: pair: 8 (over y, x, core), slab: 4 (over z).
Axes of the slice: x: 2, y: 2, z: 4, core: 2. Of those that a mesh axis runs over, the one named last changes fastest.
Arguments:
- amplitudes: bfloat16 [1536, 9216], P('pair', 'slab'), may hold values from -6 to 6
- integrals: bfloat16 [9216, 9216], P('slab', 'pair'), may hold values from -0.09375 to 0.09375
- pair_index: int32 [1536, 2], P('pair'), may hold values from 0 to 159, as said below
- eps_occ: float32 [160], replicated, may hold values from -2 to -0.5
- eps_vir: float32 [96], replicated, may hold values from 0.5 to 3
Outputs:
- update: float32 [1536, 9216], P('pair', 'slab')
The draws below stay inside these ranges and needn't reach their ends.
Inputs may be any that keep to these rules, and one draw needn't show every extreme that they name: `pair_index`: each row holds i < j; pairs may repeat; pair 0 is (0, 159).
All inputs are finite; a program needn't handle non-finite values.
Results may differ from the reference program's by a relative error of at most 0.0003.
Values may be sent and summed in bfloat16 or wider, within the bound.
No kernel may reach another device: no remote copies, remote signals or barrier semaphores. Data moves between devices by JAX's collectives and lax.ppermute only.
A program may use at most 128 MiB of HBM per device.

```python
import jax
import jax.numpy as jnp

NOCC = 160
NA = 96
PAIRS = 1536
VV = 9216


def draw_pair_index(key, part):
    key_one, key_two = jax.random.split(jax.random.fold_in(key, 7))
    first = jax.random.randint(key_one, (PAIRS,), 0, NOCC - 1)
    second = jax.random.randint(key_two, (PAIRS,), first + 1, NOCC)
    first = first.at[0].set(0)
    second = second.at[0].set(NOCC - 1)
    return jnp.stack([first, second], axis=1).astype(jnp.int32)


def spiked(values, key, source, target, shards_of, factor):
    def block_of(position):
        return (jnp.arange(values.shape[position]) // (values.shape[position] // shards_of)).reshape((-1,) + (1,) * (values.ndim - 1 - position))

    one_side = jax.random.permutation(key, shards_of)[block_of(target)]
    other_side = (block_of(target) + shards_of // 2) % shards_of
    return jnp.where((block_of(source) == one_side) | (block_of(source) == other_side), factor * values, values)


def block_levels(key, shape, pieces, low, largest):
    factor_of = 1.0
    for position, parts in pieces:
        draws = jax.random.uniform(jax.random.fold_in(jax.random.fold_in(key, 6), position), (parts,), jnp.float32, low / len(pieces), largest / len(pieces))
        factor_of = factor_of * jnp.repeat(jnp.exp(draws), shape[position] // parts).reshape((-1,) + (1,) * (len(shape) - 1 - position))
    return factor_of


def scatter_about(stream_key, extent, spread, reach, cuts=(), dtype=jnp.bfloat16):
    values = jax.random.normal(stream_key, extent, jnp.float32) * spread
    if len(cuts) > 0:
        values = block_levels(stream_key, extent, cuts, -0.22, 0.18) * values
    return jnp.clip(values, min=-reach, max=reach).astype(dtype)


def gaussian_with(own_key, shape, scale, reach, pieces, heavy, held_as=jnp.bfloat16):
    values = scale * jax.random.normal(own_key, shape, jnp.float32)
    if pieces:
        values = values * block_levels(own_key, shape, pieces, -0.22, 0.18)
    return jnp.clip(spiked(values, jax.random.fold_in(own_key, 3), *heavy), -reach, reach).astype(held_as)


def setup_inputs(seed: int = 0) -> dict:
    seeds = jax.random.split(jax.random.key(seed), 6)
    return {
        "amplitudes": scatter_about(seeds[0], (PAIRS, VV), 1.0, 6.0, ((0, 8), (1, 4))),
        "integrals": gaussian_with(seeds[1], (VV, VV), VV ** -0.5, 0.09375, ((0, 4), (1, 8)), (0, 1, 8, 2.0)),
        "pair_index": draw_pair_index(jax.random.fold_in(seeds[5], 71), 0),
        "eps_occ": jnp.clip(jax.random.uniform(seeds[3], (NOCC,), jnp.float32, -2.0, -0.5), -2.0, -0.5),
        "eps_vir": jnp.clip(jax.random.uniform(seeds[4], (NA,), jnp.float32, 0.5, 3.0), 0.5, 3.0),
    }


def reference(amplitudes, integrals, pair_index, eps_occ, eps_vir):
    ladder = jnp.dot(amplitudes, integrals, preferred_element_type=jnp.float32)
    ladder_cube = ladder.reshape(PAIRS, NA, NA)
    antisym = (ladder_cube - jnp.swapaxes(ladder_cube, 1, 2)).reshape(PAIRS, NA * NA)
    e_pair = eps_occ[pair_index[:, 0]] + eps_occ[pair_index[:, 1]]
    e_virt = (eps_vir[:, None] + eps_vir[None, :]).reshape(NA * NA)
    return antisym / (e_pair[:, None] - e_virt[None, :])
```

```python
import functools

import jax
import jax.numpy as jnp
from jax import lax
from jax.experimental import pallas as pl
from jax.experimental.pallas import tpu as pltpu
from jax.sharding import PartitionSpec as P

CORES = 2
WIDTH = 64
TAIL = 16
VMEM = 48 * 1024 * 1024
NT = (((1,), (1,)), ((), ()))


def tile_of(rows, most):
    return max(t for t in range(16, most + 1, 16) if rows % t == 0)


def power_of(peak):
    return jnp.ceil(jnp.log2(jnp.maximum(peak, 1e-30) * (1.0 / 32760.0)))


def to_codes(values, inverse):
    return jnp.round(values * inverse).astype(jnp.int32).astype(jnp.int16)


def from_codes(codes):
    return codes.astype(jnp.int32).astype(jnp.float32)


def put_power(out_ref, rows, power):
    wide = jnp.broadcast_to(power.astype(jnp.int32), (TAIL, power.shape[1]))
    out_ref[pl.ds(rows, TAIL), :] = wide.astype(jnp.int16)


def scale_in(ref, rows):
    return jnp.exp2(from_codes(ref[pl.ds(rows, TAIL), :])[0:1, :])


def rows_at(i, tile):
    return pl.ds(pl.multiple_of(i * tile, tile), tile)


def ladder_kernel(chips, it_ref, *refs):
    own, sib = refs[:chips], refs[chips : 2 * chips]
    outs = refs[2 * chips : 3 * chips]
    rhs, acc = refs[3 * chips :]
    rows = it_ref.shape[0]
    width = own[0].shape[0]
    lanes = 2 * width
    tile = tile_of(rows, 384)
    small = tile_of(rows, 96)
    for d in range(0, chips, 2):
        for k, ref in enumerate((own[d], sib[d], own[d + 1], sib[d + 1])):
            rhs[pl.ds(k * width, width), :] = ref[...]

        def multiply(i, peak):
            part = lax.dot_general(
                it_ref[rows_at(i, tile), :], rhs[...], NT, preferred_element_type=jnp.float32
            )
            acc[rows_at(i, tile), :] = part
            return jnp.maximum(peak, jnp.max(jnp.abs(part), axis=0, keepdims=True))

        peak = lax.fori_loop(0, rows // tile, multiply, jnp.zeros((1, 2 * lanes), jnp.float32))
        power = power_of(peak)
        inverse = jnp.exp2(-power)

        def code(i, carry):
            at = rows_at(i, small)
            codes = to_codes(acc[at, :], inverse)
            outs[d][at, :] = codes[:, :lanes]
            outs[d + 1][at, :] = codes[:, lanes:]
            return carry

        lax.fori_loop(0, rows // small, code, 0)
        put_power(outs[d], rows, power[:, :lanes])
        put_power(outs[d + 1], rows, power[:, lanes:])


def antisym_kernel(chips, slabs, vir, place_ref, *refs):
    own, sib = refs[:chips], refs[chips : 2 * chips]
    anti, right, left, cube = refs[2 * chips :]
    chip, core = place_ref[0], place_ref[1]
    lanes = cube.shape[1]
    rows = own[0].shape[0] - TAIL
    held = rows // vir
    small = tile_of(rows, 96)
    for d in range(chips):
        block = (chip ^ d) * CORES
        for ref, owner, turned in ((own[d], block + core, False), (sib[d], block + 1 - core, True)):
            scale = scale_in(ref, rows)
            base = owner * rows

            def spread(i, carry, ref=ref, base=base, scale=scale, turned=turned):
                values = from_codes(ref[rows_at(i, small), :]) * scale
                if turned:
                    values = pltpu.roll(values, lanes // 2, 1)
                cube[pl.ds(pl.multiple_of(base + i * small, small), small), :] = values
                return carry

            lax.fori_loop(0, rows // small, spread, 0)
    blocks = vir // slabs // (CORES * held)
    for s in range(slabs):
        peak = jnp.zeros((1, lanes), jnp.float32)
        for blk in range(blocks):
            first = s * (vir // slabs) + blk * CORES * held + core * held

            def subtract(k, peak, s=s, blk=blk, first=first):
                a = first + k
                here = cube[pl.ds(pl.multiple_of(a * vir, vir), vir), :]
                there = cube[pl.ds(a, vir, stride=vir), :]
                both = here - there
                anti[s, pl.ds(pl.multiple_of((blk * held + k) * vir, vir), vir), :] = both
                return jnp.maximum(peak, jnp.max(jnp.abs(both), axis=0, keepdims=True))

            peak = lax.fori_loop(0, held, subtract, peak)
        for out, which in ((right, slabs - 1), (left, 0)):
            if s == which:
                code_rows(lambda at: anti[which, at, :], out, peak, anti.shape[1])


def code_rows(read, out, peak, rows):
    small = tile_of(rows, 96)
    power = power_of(peak)
    inverse = jnp.exp2(-power)

    def code(i, carry):
        at = rows_at(i, small)
        out[at, :] = to_codes(read(at), inverse)
        return carry

    lax.fori_loop(0, rows // small, code, 0)
    put_power(out, rows, power)


def hop_kernel(place_ref, anti_r, anti_l, got_r, got_l, out_r, out_l, total):
    rows, lanes = total.shape
    small = tile_of(rows, 96)
    for anti, got, out in ((anti_r, got_r, out_r), (anti_l, got_l, out_l)):
        scale = scale_in(got, rows)

        def add(i, peak, anti=anti, got=got, scale=scale):
            at = rows_at(i, small)
            values = anti[0, at, :] + from_codes(got[at, :]) * scale
            total[at, :] = values
            return jnp.maximum(peak, jnp.max(jnp.abs(values), axis=0, keepdims=True))

        peak = lax.fori_loop(0, rows // small, add, jnp.zeros((1, lanes), jnp.float32))
        code_rows(lambda at: total[at, :], out, peak, rows)


def finish_kernel(place_ref, anti, got_r, got_l, pair_ref, vir_ref, own_ref, sib_ref):
    rows = vir_ref.shape[0]
    width = own_ref.shape[0]
    total = anti[0] + (
        from_codes(got_r[pl.ds(0, rows), :]) * scale_in(got_r, rows)
        + from_codes(got_l[pl.ds(0, rows), :]) * scale_in(got_l, rows)
    )
    update = (total / (pair_ref[...] - vir_ref[...])).T
    own_ref[...] = update[:width]
    sib_ref[...] = update[width:]


def whole(shape):
    return pl.BlockSpec(shape, lambda i, place: (0,) * len(shape))


def on_device(mesh, amplitudes, integrals, pair_index, eps_occ, eps_vir):
    devices, slabs = mesh.shape["pair"], mesh.shape["slab"]
    chips = devices // CORES
    num_pairs, depth = amplitudes.shape
    rows = integrals.shape[1]
    vir = eps_vir.shape[0]
    held = rows // vir
    lanes = CORES * WIDTH
    chunks = num_pairs // WIDTH
    part_rows = vir // slabs // CORES * vir
    me, z = lax.axis_index("pair"), lax.axis_index("slab")
    chip, core = me // CORES, me % CORES

    def to_chip(x, d):
        return lax.ppermute(x, "pair", [(i, i ^ (d * CORES)) for i in range(devices)])

    def to_core(x):
        return lax.ppermute(x, "pair", [(i, i ^ 1) for i in range(devices)])

    params = pltpu.CompilerParams(vmem_limit_bytes=VMEM)
    message = jax.ShapeDtypeStruct((rows + TAIL, lanes), jnp.int16)
    part_message = jax.ShapeDtypeStruct((part_rows + TAIL, lanes), jnp.int16)
    part_shape = (part_rows + TAIL, lanes)
    smem = pl.BlockSpec(memory_space=pltpu.SMEM)

    ladder = pl.pallas_call(
        functools.partial(ladder_kernel, chips),
        out_shape=[message] * chips,
        scratch_shapes=[
            pltpu.VMEM((2 * lanes, depth), jnp.bfloat16),
            pltpu.VMEM((rows, 2 * lanes), jnp.float32),
        ],
        compiler_params=params,
        cost_estimate=pl.CostEstimate(
            flops=2 * rows * depth * chips * lanes,
            bytes_accessed=2 * (rows + chips * lanes) * depth + 2 * chips * rows * lanes,
            transcendentals=0,
        ),
        name="ladder",
    )
    antisym = pl.pallas_call(
        functools.partial(antisym_kernel, chips, slabs, vir),
        in_specs=[smem] + [pl.BlockSpec(memory_space=pltpu.VMEM)] * (2 * chips),
        out_shape=[
            jax.ShapeDtypeStruct((slabs, part_rows, lanes), jnp.float32),
            part_message,
            part_message,
        ],
        scratch_shapes=[pltpu.VMEM((vir * vir, lanes), jnp.float32)],
        compiler_params=params,
        cost_estimate=pl.CostEstimate(
            flops=8 * vir * vir * lanes, bytes_accessed=8 * vir * vir * lanes, transcendentals=0
        ),
        name="antisym",
    )

    def slab_block(k):
        return pl.BlockSpec((1, part_rows, lanes), lambda i, place: (place[k], 0, 0))

    hop = pl.pallas_call(
        hop_kernel,
        grid_spec=pltpu.PrefetchScalarGridSpec(
            num_scalar_prefetch=1,
            grid=(1,),
            in_specs=[slab_block(0), slab_block(1), whole(part_shape), whole(part_shape)],
            out_specs=[whole(part_shape), whole(part_shape)],
            scratch_shapes=[pltpu.VMEM((part_rows, lanes), jnp.float32)],
        ),
        out_shape=[part_message, part_message],
        compiler_params=params,
        cost_estimate=pl.CostEstimate(
            flops=16 * part_rows * lanes, bytes_accessed=16 * part_rows * lanes, transcendentals=0
        ),
        name="hop",
    )
    finish = pl.pallas_call(
        finish_kernel,
        grid_spec=pltpu.PrefetchScalarGridSpec(
            num_scalar_prefetch=1,
            grid=(1,),
            in_specs=[
                slab_block(0),
                whole(part_shape),
                whole(part_shape),
                whole((1, lanes)),
                whole((part_rows, 1)),
            ],
            out_specs=[whole((WIDTH, part_rows))] * 2,
        ),
        out_shape=[jax.ShapeDtypeStruct((WIDTH, part_rows), jnp.float32)] * 2,
        compiler_params=params,
        cost_estimate=pl.CostEstimate(
            flops=16 * part_rows * lanes, bytes_accessed=12 * part_rows * lanes, transcendentals=0
        ),
        name="finish",
    )

    integrals_t = integrals.T

    occ_ids = jnp.arange(eps_occ.shape[0], dtype=jnp.int32)

    def pick(ids):
        return jnp.sum(jnp.where(ids[:, None] == occ_ids[None, :], eps_occ[None, :], 0.0), axis=1)

    eps_pair = pick(pair_index[:, 0]) + pick(pair_index[:, 1])
    eps_pair = eps_pair.reshape(chunks, 1, WIDTH)
    eps_pair = jnp.concatenate([eps_pair, to_core(eps_pair)], axis=2)
    blocks = vir // slabs // (CORES * held)
    eps_grid = eps_vir.reshape(slabs, blocks, CORES, held)
    eps_mine = lax.dynamic_slice(eps_grid, (z, 0, core, 0), (1, blocks, 1, held)).reshape(-1)
    eps_virt = (eps_mine[:, None] + eps_vir[None, :]).reshape(part_rows, 1)

    place = jnp.stack([chip, core]).astype(jnp.int32)

    gathered = []
    last = None
    for r in range(chunks):
        mine = amplitudes[r * WIDTH : (r + 1) * WIDTH]
        if last is not None:
            mine, last = lax.optimization_barrier((mine, last))
            gathered[-1] = gathered[-1][:1] + list(last)
        got = [to_chip(mine, d) for d in range(1, chips)]
        last = tuple(got)
        gathered.append([mine] + got)

    halves = []
    for r in range(chunks):
        sib = [to_core(x) for x in gathered[r]]
        sums = ladder(integrals_t, *gathered[r], *sib)
        arrived = [sums[0]] + [to_chip(sums[d], d) for d in range(1, chips)]
        twins = [to_core(x) for x in arrived]
        anti, right, left = antisym(place, *arrived, *twins)
        for step in range(1, slabs):
            ahead = slabs - step
            if step > 1:
                targets = jnp.clip(jnp.stack([z + ahead, z - ahead]), 0, slabs - 1)
                right, left = hop(targets.astype(jnp.int32), anti, anti, right, left)
            right, left = (
                lax.ppermute(right, "slab", [(i, i + 1) for i in range(step)]),
                lax.ppermute(
                    left, "slab", [(i, i - 1) for i in range(slabs - step, slabs)]
                ),
            )
        own, other = finish(z[None].astype(jnp.int32), anti, right, left, eps_pair[r], eps_virt)
        other = to_core(other)
        first = jnp.where(core == 0, own, other).reshape(WIDTH, blocks, 1, held * vir)
        second = jnp.where(core == 0, other, own).reshape(WIDTH, blocks, 1, held * vir)
        halves.append(jnp.concatenate([first, second], axis=2).reshape(WIDTH, CORES * part_rows))
    return jnp.concatenate(halves, axis=0)


def solution(mesh):
    in_specs = (P("pair", "slab"), P("slab", "pair"), P("pair", None), P(), P())
    out_specs = P("pair", "slab")
    return jax.shard_map(
        functools.partial(on_device, mesh),
        mesh=mesh,
        in_specs=in_specs,
        out_specs=out_specs,
        check_vma=False,
    )
```

```python
import functools

import jax
import jax.numpy as jnp
from jax import lax
from jax.experimental import pallas as pl
from jax.experimental.pallas import tpu as pltpu
from jax.sharding import PartitionSpec as P

CORES = 2
WIDTH = 64
LANES = 2 * WIDTH
TAIL = 16
NT = (((1,), (1,)), ((), ()))


def tile_of(rows, most):
    return max(t for t in range(16, most + 1, 16) if rows % t == 0)


def is_low(shape):
    return lax.broadcasted_iota(jnp.int32, shape, len(shape) - 1) < WIDTH


def turn(values):
    return pltpu.roll(values, WIDTH, 1)


def encode(values, out_ref):
    tile = values.shape[0]
    peak = jnp.max(jnp.abs(values), axis=0, keepdims=True)
    power = jnp.ceil(jnp.log2(jnp.maximum(peak, 1e-30) * (1.0 / 32760.0)))
    codes = jnp.round(values * jnp.exp2(-power)).astype(jnp.int32)
    out_ref[pl.ds(0, tile), :] = codes.astype(jnp.int16)
    wide = jnp.broadcast_to(power.astype(jnp.int32), (TAIL, LANES))
    out_ref[pl.ds(tile, TAIL), :] = wide.astype(jnp.int16)


def decode(ref):
    tile = ref.shape[0] - TAIL
    power = ref[pl.ds(tile, TAIL), :].astype(jnp.int32).astype(jnp.float32)[0:1, :]
    return ref[pl.ds(0, tile), :].astype(jnp.int32).astype(jnp.float32) * jnp.exp2(power)


def ladder_kernel(chips, own_ref, sib_ref, *refs):
    rows_in, outs, rhs = refs[:chips], refs[chips : 2 * chips], refs[-1]

    @pl.when(pl.program_id(0) == 0)
    def _():
        for d in range(chips):
            rhs[pl.ds(d * WIDTH, WIDTH), :] = rows_in[d][...]

    low = is_low((own_ref.shape[0], LANES))
    group = min(4, chips)
    for first in range(0, chips, group):
        right = rhs[pl.ds(first * WIDTH, group * WIDTH), :]
        own = lax.dot_general(own_ref[...], right, NT, preferred_element_type=jnp.float32)
        sib = lax.dot_general(sib_ref[...], right, NT, preferred_element_type=jnp.float32)
        for k in range(0, group, 2):
            u = own[:, k * WIDTH : k * WIDTH + LANES]
            v = sib[:, k * WIDTH : k * WIDTH + LANES]
            encode(jnp.where(low, u, turn(v)), outs[first + k].at[0])
            encode(jnp.where(low, turn(u), v), outs[first + k + 1].at[0])


def antisym_kernel(chips, slabs, vir, place_ref, *refs):
    arrived, (anti, first_out, cube) = refs[:chips], refs[chips:]
    chip, core, z = place_ref[0], place_ref[1], place_ref[2]
    tiles, tile = arrived[0].shape[0], arrived[0].shape[1] - TAIL
    rows = tiles * tile
    s = pl.program_id(0)

    @pl.when(s == 0)
    def _():
        low = is_low((tile, LANES))
        for d in range(chips):
            base = (chip ^ d) * (CORES * rows)
            for t in range(tiles):
                values = decode(arrived[d].at[t])
                turned = turn(values)
                at_own = pl.multiple_of(base + core * rows + t * tile, tile)
                at_sib = pl.multiple_of(base + (1 - core) * rows + t * tile, tile)
                cube[pl.ds(at_own, tile), :] = jnp.where(low, values, turned)
                cube[pl.ds(at_sib, tile), :] = jnp.where(low, turned, values)

    half = vir // slabs // 2
    low = is_low((vir, LANES))

    def subtract(k, carry):
        a = s * (2 * half) + k
        b = a + half
        here = cube[pl.ds(pl.multiple_of(a * vir, vir), vir), :]
        other = cube[pl.ds(pl.multiple_of(b * vir, vir), vir), :]
        lower = here - cube[pl.ds(a, vir, stride=vir), :]
        upper = other - cube[pl.ds(b, vir, stride=vir), :]
        anti[0, pl.ds(pl.multiple_of(k * vir, vir), vir), :] = jnp.where(low, lower, upper)
        return carry

    lax.fori_loop(0, half, subtract, 0)
    part_tile = first_out.shape[1] - TAIL

    @pl.when(s == jnp.where(z == 0, slabs - 1, 0))
    def _():
        for t in range(first_out.shape[0]):
            encode(anti[0, pl.ds(t * part_tile, part_tile), :], first_out.at[t])


def hop_kernel(count, place_ref, *refs):
    for k in range(count):
        anti, got, out = refs[k], refs[count + k], refs[2 * count + k]
        encode(anti[0] + decode(got.at[0]), out.at[0])


def finish_kernel(place_ref, anti, got_r, got_l, pair_ref, vir_ref, *refs):
    out_ref = refs[-1]
    tiles, tile = got_r.shape[0], got_r.shape[1] - TAIL
    low = is_low((tile, LANES))
    pair = pair_ref[0]
    half = tiles * tile
    for t in range(tiles):
        at = pl.ds(t * tile, tile)
        total = anti[0, at, :] + (decode(got_r.at[t]) + decode(got_l.at[t]))
        virt = jnp.where(low, vir_ref[at, 0:1], vir_ref[at, 1:2])
        update = (total / (pair - virt)).T
        out_ref[:, pl.ds(t * tile, tile)] = update[:WIDTH]
        out_ref[:, pl.ds(half + t * tile, tile)] = update[WIDTH:]


def on_device(mesh, amplitudes, integrals, pair_index, eps_occ, eps_vir):
    devices, slabs = mesh.shape["pair"], mesh.shape["slab"]
    chips = devices // CORES
    num_pairs, depth = amplitudes.shape
    rows = integrals.shape[1]
    vir = eps_vir.shape[0]
    chunks = num_pairs // WIDTH
    half = vir // slabs // 2
    part_rows = half * vir
    tile, part_tile = tile_of(rows, 384), tile_of(part_rows, 384)
    tiles, part_tiles = rows // tile, part_rows // part_tile
    me, z = lax.axis_index("pair"), lax.axis_index("slab")
    chip, core = me // CORES, me % CORES

    def to_chip(x, d):
        return lax.ppermute(x, "pair", [(i, i ^ (d * CORES)) for i in range(devices)])

    def limit(mib):
        return pltpu.CompilerParams(vmem_limit_bytes=mib * 1024 * 1024)

    def cost(flops, moved):
        return pl.CostEstimate(flops=flops, bytes_accessed=moved, transcendentals=0)

    message = jax.ShapeDtypeStruct((tiles, tile + TAIL, LANES), jnp.int16)
    part_message = jax.ShapeDtypeStruct((part_tiles, part_tile + TAIL, LANES), jnp.int16)
    smem = pl.BlockSpec(memory_space=pltpu.SMEM)

    ladder = pl.pallas_call(
        functools.partial(ladder_kernel, chips),
        grid=(tiles,),
        in_specs=[pl.BlockSpec((tile, depth), lambda i: (i, 0))] * 2
        + [pl.BlockSpec((WIDTH, depth), lambda i: (0, 0))] * chips,
        out_specs=[pl.BlockSpec((1, tile + TAIL, LANES), lambda i: (i, 0, 0))] * chips,
        out_shape=[message] * chips,
        scratch_shapes=[pltpu.VMEM((chips * WIDTH, depth), jnp.bfloat16)],
        compiler_params=limit(24),
        cost_estimate=cost(
            4 * rows * depth * chips * WIDTH,
            4 * rows * depth + 2 * chips * WIDTH * depth + 2 * chips * rows * LANES,
        ),
        name="ladder",
    )
    antisym = pl.pallas_call(
        functools.partial(antisym_kernel, chips, slabs, vir),
        grid=(slabs,),
        in_specs=[smem] + [pl.BlockSpec(message.shape, lambda s: (0, 0, 0))] * chips,
        out_specs=[
            pl.BlockSpec((1, part_rows, LANES), lambda s: (s, 0, 0)),
            pl.BlockSpec(part_message.shape, lambda s: (0, 0, 0)),
        ],
        out_shape=[
            jax.ShapeDtypeStruct((slabs, part_rows, LANES), jnp.float32),
            part_message,
        ],
        scratch_shapes=[pltpu.VMEM((vir * vir, LANES), jnp.float32)],
        compiler_params=limit(24),
        cost_estimate=cost(8 * vir * vir * LANES, 4 * vir * vir * LANES),
        name="antisym",
    )
    part_spec = pl.BlockSpec((1, part_tile + TAIL, LANES), lambda i, place: (i, 0, 0))

    def hop(count):
        def anti_spec(k):
            return pl.BlockSpec((1, part_tile, LANES), lambda i, place: (place[k], i, 0))

        return pl.pallas_call(
            functools.partial(hop_kernel, count),
            grid_spec=pltpu.PrefetchScalarGridSpec(
                num_scalar_prefetch=1,
                grid=(part_tiles,),
                in_specs=[anti_spec(k) for k in range(count)] + [part_spec] * count,
                out_specs=[part_spec] * count,
            ),
            out_shape=[part_message] * count,
            compiler_params=limit(12),
            cost_estimate=cost(8 * count * part_rows * LANES, 8 * count * part_rows * LANES),
            name="hop",
        )

    def finish(r, anti, got_r, got_l, pair, virt, place, so_far):
        given = [] if so_far is None else [so_far]
        whole_part = pl.BlockSpec(part_message.shape, lambda i, place: (0, 0, 0))
        return pl.pallas_call(
            finish_kernel,
            grid_spec=pltpu.PrefetchScalarGridSpec(
                num_scalar_prefetch=1,
                grid=(1,),
                in_specs=[
                    pl.BlockSpec((1, part_rows, LANES), lambda i, place: (place[0], 0, 0)),
                    whole_part,
                    whole_part,
                    pl.BlockSpec((1, 1, LANES), lambda i, place: (r, 0, 0)),
                    pl.BlockSpec((part_rows, 2), lambda i, place: (0, 0)),
                ]
                + [pl.BlockSpec(memory_space=pl.ANY)] * len(given),
                out_specs=pl.BlockSpec((WIDTH, 2 * part_rows), lambda i, place: (r, 0)),
            ),
            out_shape=jax.ShapeDtypeStruct((num_pairs, 2 * part_rows), jnp.float32),
            input_output_aliases={6: 0} if given else {},
            compiler_params=limit(16),
            cost_estimate=cost(16 * part_rows * LANES, 16 * part_rows * LANES),
            name="finish",
        )(place, anti, got_r, got_l, pair, virt, *given)

    own_t = integrals.T
    sib_t = lax.ppermute(own_t, "pair", [(i, i ^ 1) for i in range(devices)])

    occ_ids = jnp.arange(eps_occ.shape[0], dtype=jnp.int32)

    def pick(ids):
        return jnp.sum(jnp.where(ids[:, None] == occ_ids[None, :], eps_occ[None, :], 0.0), axis=1)

    eps_pair = (pick(pair_index[:, 0]) + pick(pair_index[:, 1])).reshape(chunks, 1, WIDTH)
    eps_pair = jnp.concatenate([eps_pair, eps_pair], axis=2)
    eps_mine = lax.dynamic_slice(eps_vir.reshape(slabs, 2, half), (z, 0, 0), (1, 2, half))[0]
    eps_virt = (eps_mine[:, :, None] + eps_vir[None, None, :]).reshape(2, part_rows).T

    place = jnp.stack([chip, core, z]).astype(jnp.int32)

    gathered = []
    for r in range(chunks):
        mine = amplitudes[r * WIDTH : (r + 1) * WIDTH]
        if gathered:
            mine, *last = lax.optimization_barrier((mine, *gathered[-1]))
            gathered[-1] = last
        gathered.append([mine] + [to_chip(mine, d) for d in range(1, chips)])

    update = None
    for r in range(chunks):
        sums = ladder(own_t, sib_t, *gathered[r])
        arrived = [sums[0]] + [to_chip(sums[d], d) for d in range(1, chips)]
        anti, one = antisym(place, *arrived)
        for step in range(1, slabs):
            ahead = slabs - step
            rightward = [(i, i + 1) for i in range(step)]
            leftward = [(i, i - 1) for i in range(ahead, slabs)]
            targets = jnp.stack([z + ahead, z - ahead])
            if step <= slabs // 2:
                if step > 1:
                    target = jnp.where(z < slabs // 2, targets[0:1], targets[1:2])
                    target = jnp.clip(target, 0, slabs - 1).astype(jnp.int32)
                    (one,) = hop(1)(target, anti, one)
                if step < slabs // 2:
                    one = lax.ppermute(one, "slab", rightward + leftward)
                    continue
                right = left = one
            else:
                targets = jnp.clip(targets, 0, slabs - 1).astype(jnp.int32)
                right, left = hop(2)(targets, anti, anti, right, left)
            right = lax.ppermute(right, "slab", rightward)
            left = lax.ppermute(left, "slab", leftward)
        here = z[None].astype(jnp.int32)
        update = finish(r, anti, right, left, eps_pair, eps_virt, here, update)
    return update


def solution(mesh):
    in_specs = (P("pair", "slab"), P("slab", "pair"), P("pair", None), P(), P())
    out_specs = P("pair", "slab")
    return jax.shard_map(
        functools.partial(on_device, mesh),
        mesh=mesh,
        in_specs=in_specs,
        out_specs=out_specs,
        check_vma=False,
    )
```

```python
import functools

import jax
import jax.numpy as jnp
from jax import lax
from jax.experimental import pallas as pl
from jax.experimental.pallas import tpu as pltpu
from jax.sharding import PartitionSpec as P

CORES = 2
WIDTH = 64
LANES = 2 * WIDTH
TAIL = 16
NT = (((1,), (1,)), ((), ()))


def tile_of(rows, most):
    return max(t for t in range(16, most + 1, 16) if rows % t == 0)


def is_low(shape):
    return lax.broadcasted_iota(jnp.int32, shape, len(shape) - 1) < WIDTH


def turn(values):
    return pltpu.roll(values, WIDTH, 1)


def encode(values, out_ref):
    tile = values.shape[0]
    peak = jnp.max(jnp.abs(values), axis=0, keepdims=True)
    power = jnp.ceil(jnp.log2(jnp.maximum(peak, 1e-30) * (1.0 / 32760.0)))
    codes = jnp.round(values * jnp.exp2(-power)).astype(jnp.int32)
    out_ref[pl.ds(0, tile), :] = codes.astype(jnp.int16)
    wide = jnp.broadcast_to(power.astype(jnp.int32), (TAIL, LANES))
    out_ref[pl.ds(tile, TAIL), :] = wide.astype(jnp.int16)


def decode(ref):
    tile = ref.shape[0] - TAIL
    power = ref[pl.ds(tile, TAIL), :].astype(jnp.int32).astype(jnp.float32)[0:1, :]
    return ref[pl.ds(0, tile), :].astype(jnp.int32).astype(jnp.float32) * jnp.exp2(power)


def ladder_kernel(chips, place_ref, own_ref, sib_ref, rows_in, *refs):
    outs, rhs = refs[:chips], refs[-1]

    @pl.when(pl.program_id(0) == 0)
    def _():
        for d in range(chips):
            rhs[pl.ds(d * WIDTH, WIDTH), :] = rows_in[place_ref[0] ^ d]

    low = is_low((own_ref.shape[0], LANES))
    group = min(4, chips)
    for first in range(0, chips, group):
        right = rhs[pl.ds(first * WIDTH, group * WIDTH), :]
        own = lax.dot_general(own_ref[...], right, NT, preferred_element_type=jnp.float32)
        sib = lax.dot_general(sib_ref[...], right, NT, preferred_element_type=jnp.float32)
        for k in range(0, group, 2):
            u = own[:, k * WIDTH : k * WIDTH + LANES]
            v = sib[:, k * WIDTH : k * WIDTH + LANES]
            encode(jnp.where(low, u, turn(v)), outs[first + k].at[0])
            encode(jnp.where(low, turn(u), v), outs[first + k + 1].at[0])


def antisym_kernel(chips, slabs, vir, place_ref, *refs):
    arrived, (kept, away, cube, sent) = refs[:chips], refs[chips:]
    chip, core, z = place_ref[0], place_ref[1], place_ref[2]
    tiles, tile = arrived[0].shape[0], arrived[0].shape[1] - TAIL
    rows = tiles * tile
    s = pl.program_id(0)

    @pl.when(s == 0)
    def _():
        low = is_low((tile, LANES))
        for d in range(chips):
            base = (chip ^ d) * (CORES * rows)
            for t in range(tiles):
                values = decode(arrived[d].at[t])
                turned = turn(values)
                at_own = pl.multiple_of(base + core * rows + t * tile, tile)
                at_sib = pl.multiple_of(base + (1 - core) * rows + t * tile, tile)
                cube[pl.ds(at_own, tile), :] = jnp.where(low, values, turned)
                cube[pl.ds(at_sib, tile), :] = jnp.where(low, turned, values)

    half = vir // slabs // 2
    low = is_low((vir, LANES))
    part_tile = away.shape[2] - TAIL
    keep = ((s ^ z) & 1) == 0

    def subtract(k):
        a = s * (2 * half) + k
        b = a + half
        here = cube[pl.ds(pl.multiple_of(a * vir, vir), vir), :]
        other = cube[pl.ds(pl.multiple_of(b * vir, vir), vir), :]
        lower = here - cube[pl.ds(a, vir, stride=vir), :]
        upper = other - cube[pl.ds(b, vir, stride=vir), :]
        return jnp.where(low, lower, upper)

    def into(out):
        def body(k, carry):
            out[pl.ds(pl.multiple_of(k * vir, vir), vir), :] = subtract(k)
            return carry

        lax.fori_loop(0, half, body, 0)

    @pl.when(keep)
    def _():
        into(kept.at[0])

    @pl.when(jnp.logical_not(keep))
    def _():
        into(sent)
        for t in range(away.shape[1]):
            encode(sent[pl.ds(t * part_tile, part_tile), :], away.at[0, t])


def hop_kernel(place_ref, part_send, part_keep, got_send, got_keep, kept, away):
    encode(part_send[0] + decode(got_send.at[0, 0]), away.at[0, 0])
    kept[0] = part_keep[0] + decode(got_keep.at[0, 0])


def finish_kernel(part, got, pair_ref, vir_ref, *refs):
    out_ref = refs[-1]
    tiles, tile = got.shape[1], got.shape[2] - TAIL
    low = is_low((tile, LANES))
    pair = pair_ref[0]
    half = tiles * tile
    for t in range(tiles):
        at = pl.ds(t * tile, tile)
        total = part[0, at, :] + decode(got.at[0, t])
        virt = jnp.where(low, vir_ref[at, 0:1], vir_ref[at, 1:2])
        update = (total / (pair - virt)).T
        out_ref[:, pl.ds(t * tile, tile)] = update[:WIDTH]
        out_ref[:, pl.ds(half + t * tile, tile)] = update[WIDTH:]


def on_device(mesh, amplitudes, integrals, pair_index, eps_occ, eps_vir):
    devices, slabs = mesh.shape["pair"], mesh.shape["slab"]
    chips = devices // CORES
    num_pairs, depth = amplitudes.shape
    rows = integrals.shape[1]
    vir = eps_vir.shape[0]
    chunks = num_pairs // WIDTH
    half = vir // slabs // 2
    part_rows = half * vir
    tile, part_tile = tile_of(rows, 384), tile_of(part_rows, 384)
    tiles, part_tiles = rows // tile, part_rows // part_tile
    me, z = lax.axis_index("pair"), lax.axis_index("slab")
    chip, core = me // CORES, me % CORES

    def to_chip(x, d):
        return lax.ppermute(x, "pair", [(i, i ^ (d * CORES)) for i in range(devices)])

    def limit(mib):
        return pltpu.CompilerParams(vmem_limit_bytes=mib * 1024 * 1024)

    def cost(flops, moved):
        return pl.CostEstimate(flops=flops, bytes_accessed=moved, transcendentals=0)

    def in_hbm(kernel):
        def call(*args):
            pin = pltpu.with_memory_space_constraint
            return kernel(*(x if x.size < 8192 else pin(x, pltpu.HBM) for x in args))

        return call

    message_shape = (tiles, tile + TAIL, LANES)
    message = pltpu.HBM(message_shape, jnp.int16)
    smem = pl.BlockSpec(memory_space=pltpu.SMEM)

    def parcel(count):
        return (count, part_tiles, part_tile + TAIL, LANES)

    ladder = pl.pallas_call(
        functools.partial(ladder_kernel, chips),
        grid=(tiles,),
        in_specs=[smem]
        + [pl.BlockSpec((tile, depth), lambda i: (i, 0))] * 2
        + [pl.BlockSpec((chips, WIDTH, depth), lambda i: (0, 0, 0))],
        out_specs=[pl.BlockSpec((1, tile + TAIL, LANES), lambda i: (i, 0, 0))] * chips,
        out_shape=[message] * chips,
        scratch_shapes=[pltpu.VMEM((chips * WIDTH, depth), jnp.bfloat16)],
        compiler_params=limit(24),
        cost_estimate=cost(
            4 * rows * depth * chips * WIDTH,
            4 * rows * depth + 2 * chips * WIDTH * depth + 2 * chips * rows * LANES,
        ),
        name="ladder",
    )
    antisym = pl.pallas_call(
        functools.partial(antisym_kernel, chips, slabs, vir),
        grid=(slabs,),
        in_specs=[smem] + [pl.BlockSpec(message_shape, lambda s: (0, 0, 0))] * chips,
        out_specs=[
            pl.BlockSpec((1, part_rows, LANES), lambda s: (s // 2, 0, 0)),
            pl.BlockSpec((1, *parcel(1)[1:]), lambda s: (s // 2, 0, 0, 0)),
        ],
        out_shape=[
            pltpu.HBM((slabs // 2, part_rows, LANES), jnp.float32),
            pltpu.HBM(parcel(slabs // 2), jnp.int16),
        ],
        scratch_shapes=[
            pltpu.VMEM((vir * vir, LANES), jnp.float32),
            pltpu.VMEM((part_rows, LANES), jnp.float32),
        ],
        compiler_params=limit(24),
        cost_estimate=cost(8 * vir * vir * LANES, 4 * vir * vir * LANES),
        name="antisym",
    )

    def hop(place, part, got):
        count = part.shape[0] // 2

        def part_spec(turned):
            return pl.BlockSpec(
                (1, part_tile, LANES), lambda i, t, place: (2 * i + (place[0] ^ turned), t, 0)
            )

        def got_spec(turned):
            return pl.BlockSpec(
                (1, 1, part_tile + TAIL, LANES),
                lambda i, t, place: (2 * i + (place[0] ^ turned), t, 0, 0),
            )

        call = pl.pallas_call(
            hop_kernel,
            grid_spec=pltpu.PrefetchScalarGridSpec(
                num_scalar_prefetch=1,
                grid=(count, part_tiles),
                in_specs=[part_spec(1), part_spec(0), got_spec(1), got_spec(0)],
                out_specs=[
                    pl.BlockSpec((1, part_tile, LANES), lambda i, t, place: (i, t, 0)),
                    pl.BlockSpec(
                        (1, 1, part_tile + TAIL, LANES), lambda i, t, place: (i, t, 0, 0)
                    ),
                ],
            ),
            out_shape=[
                pltpu.HBM((count, part_rows, LANES), jnp.float32),
                pltpu.HBM(parcel(count), jnp.int16),
            ],
            compiler_params=limit(12),
            cost_estimate=cost(8 * count * part_rows * LANES, 16 * count * part_rows * LANES),
            name="hop",
        )
        return in_hbm(call)(place, part, part, got, got)

    def finish(r, part, got, pair, virt, so_far):
        given = [] if so_far is None else [so_far]
        call = pl.pallas_call(
            finish_kernel,
            grid=(1,),
            in_specs=[
                pl.BlockSpec((1, part_rows, LANES), lambda i: (0, 0, 0)),
                pl.BlockSpec(parcel(1), lambda i: (0, 0, 0, 0)),
                pl.BlockSpec((1, 1, LANES), lambda i: (r, 0, 0)),
                pl.BlockSpec((part_rows, 2), lambda i: (0, 0)),
            ]
            + [pl.BlockSpec(memory_space=pl.ANY)] * len(given),
            out_specs=pl.BlockSpec((WIDTH, 2 * part_rows), lambda i: (r, 0)),
            out_shape=pltpu.HBM((num_pairs, 2 * part_rows), jnp.float32),
            input_output_aliases={4: 0} if given else {},
            compiler_params=limit(16),
            cost_estimate=cost(16 * part_rows * LANES, 16 * part_rows * LANES),
            name="finish",
        )
        return in_hbm(call)(part, got, pair, virt, *given)

    own_t = integrals.T
    sib_t = lax.ppermute(own_t, "pair", [(i, i ^ 1) for i in range(devices)])

    occ_ids = jnp.arange(eps_occ.shape[0], dtype=jnp.int32)

    def pick(ids):
        return jnp.sum(jnp.where(ids[:, None] == occ_ids[None, :], eps_occ[None, :], 0.0), axis=1)

    eps_pair = (pick(pair_index[:, 0]) + pick(pair_index[:, 1])).reshape(chunks, 1, WIDTH)
    eps_pair = jnp.concatenate([eps_pair, eps_pair], axis=2)
    eps_mine = lax.dynamic_slice(eps_vir.reshape(slabs, 2, half), (z, 0, 0), (1, 2, half))[0]
    eps_virt = (eps_mine[:, :, None] + eps_vir[None, None, :]).reshape(2, part_rows).T

    place = jnp.stack([chip, core, z]).astype(jnp.int32)

    same_core = [list(range(k, devices, CORES)) for k in range(CORES)]
    gathered = []
    for r in range(chunks):
        mine = amplitudes[r * WIDTH : (r + 1) * WIDTH]
        if gathered:
            mine, gathered[-1] = lax.optimization_barrier((mine, gathered[-1]))
        gathered.append(lax.all_gather(mine, "pair", axis_index_groups=same_core))

    def across(x, level):
        return lax.ppermute(x, "slab", [(i, i ^ level) for i in range(slabs)])

    def stages(r):
        sums = yield functools.partial(in_hbm(ladder), place, own_t, sib_t), gathered[r]
        arrived = [to_chip(sums[d], d) for d in range(1, chips)]
        kept, away = yield functools.partial(in_hbm(antisym), place, sums[0]), *arrived
        got, level = across(away, 1), 2
        while level < slabs:
            bit = (z // level % 2)[None].astype(jnp.int32)
            kept, away = yield functools.partial(hop, bit, kept), got
            got, level = across(away, level), 2 * level
        yield functools.partial(finish, r, kept), got

    order = []
    length = 3 + max(0, (slabs - 1).bit_length() - 1)
    for tick in range(length + chunks):
        for r in reversed(range(chunks)):
            k = tick - r
            if 0 <= k < length:
                order.append((r, k))

    running = [stages(r) for r in range(chunks)]
    results = [None] * chunks
    update = token = None
    for r, k in order:
        call, *inputs = running[r].send(results[r])
        if token is not None:
            *inputs, token = lax.optimization_barrier((*inputs, token))
        if k == length - 1:
            update = call(*inputs, eps_pair, eps_virt, update)
        else:
            results[r] = call(*inputs)
            token = results[r][-1]
    return update


def solution(mesh):
    in_specs = (P("pair", "slab"), P("slab", "pair"), P("pair", None), P(), P())
    out_specs = P("pair", "slab")
    return jax.shard_map(
        functools.partial(on_device, mesh),
        mesh=mesh,
        in_specs=in_specs,
        out_specs=out_specs,
        check_vma=False,
    )
```

```python
import functools

import jax
import jax.numpy as jnp
from jax import lax
from jax.experimental import pallas as pl
from jax.experimental.pallas import tpu as pltpu
from jax.sharding import PartitionSpec as P

CORES = 2
WIDTH = 64
LANES = 2 * WIDTH
TAIL = 16
NT = (((1,), (1,)), ((), ()))


def tile_of(rows, most):
    return max(t for t in range(16, most + 1, 16) if rows % t == 0)


def is_low(shape):
    return lax.broadcasted_iota(jnp.int32, shape, len(shape) - 1) < WIDTH


def turn(values):
    return pltpu.roll(values, WIDTH, 1)


def encode(values, out_ref):
    tile = values.shape[0]
    peak = jnp.max(jnp.abs(values), axis=0, keepdims=True)
    power = jnp.ceil(jnp.log2(jnp.maximum(peak, 1e-30) * (1.0 / 32760.0)))
    codes = jnp.round(values * jnp.exp2(-power)).astype(jnp.int32)
    out_ref[pl.ds(0, tile), :] = codes.astype(jnp.int16)
    wide = jnp.broadcast_to(power.astype(jnp.int32), (TAIL, LANES))
    out_ref[pl.ds(tile, TAIL), :] = wide.astype(jnp.int16)


def decode(ref):
    tile = ref.shape[0] - TAIL
    power = ref[pl.ds(tile, TAIL), :].astype(jnp.int32).astype(jnp.float32)[0:1, :]
    return ref[pl.ds(0, tile), :].astype(jnp.int32).astype(jnp.float32) * jnp.exp2(power)


def transpose_kernel(in_ref, out_ref):
    width = in_ref.shape[1]
    at = pl.ds(pl.multiple_of(pl.program_id(0) * width, width), width)
    out_ref[at, :] = in_ref[...].T


def ladder_kernel(chips, tile, own_ref, sib_ref, *refs):
    rows_in, outs, rhs = refs[:chips], refs[chips : 2 * chips], refs[-1]
    for d in range(chips):
        rhs[pl.ds(d * WIDTH, WIDTH), :] = rows_in[d][...]
    low = is_low((tile, LANES))
    group = min(4, chips)

    def step(i, carry):
        at = pl.ds(pl.multiple_of(i * tile, tile), tile)
        for first in range(0, chips, group):
            right = rhs[pl.ds(first * WIDTH, group * WIDTH), :]
            own = lax.dot_general(own_ref[at, :], right, NT, preferred_element_type=jnp.float32)
            sib = lax.dot_general(sib_ref[at, :], right, NT, preferred_element_type=jnp.float32)
            for k in range(0, group, 2):
                u = own[:, k * WIDTH : k * WIDTH + LANES]
                v = sib[:, k * WIDTH : k * WIDTH + LANES]
                encode(jnp.where(low, u, turn(v)), outs[first + k].at[i])
                encode(jnp.where(low, turn(u), v), outs[first + k + 1].at[i])
        return carry

    lax.fori_loop(0, own_ref.shape[0] // tile, step, 0)


def antisym_kernel(chips, slabs, vir, place_ref, *refs):
    arrived, (kept, away, cube, sent) = refs[:chips], refs[chips:]
    chip, core, z = place_ref[0], place_ref[1], place_ref[2]
    tiles, tile = arrived[0].shape[0], arrived[0].shape[1] - TAIL
    rows = tiles * tile
    low = is_low((tile, LANES))
    for d in range(chips):
        base = (chip ^ d) * (CORES * rows)
        for t in range(tiles):
            values = decode(arrived[d].at[t])
            turned = turn(values)
            at_own = pl.multiple_of(base + core * rows + t * tile, tile)
            at_sib = pl.multiple_of(base + (1 - core) * rows + t * tile, tile)
            cube[pl.ds(at_own, tile), :] = jnp.where(low, values, turned)
            cube[pl.ds(at_sib, tile), :] = jnp.where(low, turned, values)

    half = vir // slabs // 2
    low = is_low((vir, LANES))
    part_tile = away.shape[2] - TAIL

    def into(slab, out):
        def body(k, carry):
            a = slab * (2 * half) + k
            b = a + half
            here = cube[pl.ds(pl.multiple_of(a * vir, vir), vir), :]
            other = cube[pl.ds(pl.multiple_of(b * vir, vir), vir), :]
            lower = here - cube[pl.ds(a, vir, stride=vir), :]
            upper = other - cube[pl.ds(b, vir, stride=vir), :]
            out[pl.ds(pl.multiple_of(k * vir, vir), vir), :] = jnp.where(low, lower, upper)
            return carry

        lax.fori_loop(0, half, body, 0)

    for i in range(slabs // 2):
        into(2 * i + (z & 1), kept.at[i])
        into(2 * i + 1 - (z & 1), sent)
        for t in range(away.shape[1]):
            encode(sent[pl.ds(t * part_tile, part_tile), :], away.at[i, t])


def hop_kernel(bit_ref, part, got, kept, away):
    tiles, tile = got.shape[1], got.shape[2] - TAIL
    bit = bit_ref[0]
    for i in range(part.shape[0] // 2):
        keep, send = 2 * i + bit, 2 * i + 1 - bit
        for t in range(tiles):
            at = pl.ds(t * tile, tile)
            encode(part[send, at, :] + decode(got.at[send, t]), away.at[i, t])
            kept[i, at, :] = part[keep, at, :] + decode(got.at[keep, t])


def finish_kernel(part, got, pair_ref, vir_ref, *refs):
    out_ref = refs[-1]
    tiles, tile = got.shape[1], got.shape[2] - TAIL
    low = is_low((tile, LANES))
    pair = pair_ref[0]
    half = tiles * tile
    for t in range(tiles):
        at = pl.ds(t * tile, tile)
        total = part[0, at, :] + decode(got.at[0, t])
        virt = jnp.where(low, vir_ref[at, 0:1], vir_ref[at, 1:2])
        update = (total / (pair - virt)).T
        out_ref[:, pl.ds(t * tile, tile)] = update[:WIDTH]
        out_ref[:, pl.ds(half + t * tile, tile)] = update[WIDTH:]


def on_device(mesh, amplitudes, integrals, pair_index, eps_occ, eps_vir):
    devices, slabs = mesh.shape["pair"], mesh.shape["slab"]
    chips = devices // CORES
    num_pairs, depth = amplitudes.shape
    rows = integrals.shape[1]
    vir = eps_vir.shape[0]
    chunks = num_pairs // WIDTH
    half = vir // slabs // 2
    part_rows = half * vir
    tile, part_tile = tile_of(rows, 384), tile_of(part_rows, 384)
    tiles, part_tiles = rows // tile, part_rows // part_tile
    me, z = lax.axis_index("pair"), lax.axis_index("slab")
    chip, core = me // CORES, me % CORES

    def to_chip(x, d):
        return lax.ppermute(x, "pair", [(i, i ^ (d * CORES)) for i in range(devices)])

    def limit(mib):
        return pltpu.CompilerParams(vmem_limit_bytes=mib * 1024 * 1024)

    def cost(flops, moved):
        return pl.CostEstimate(flops=flops, bytes_accessed=moved, transcendentals=0)

    smem = pl.BlockSpec(memory_space=pltpu.SMEM)
    vmem = pl.BlockSpec(memory_space=pltpu.VMEM)
    message = jax.ShapeDtypeStruct((tiles, tile + TAIL, LANES), jnp.int16)

    def parcel(count):
        return (count, part_tiles, part_tile + TAIL, LANES)

    column = 128 if rows % 128 == 0 else rows
    transpose = pl.pallas_call(
        transpose_kernel,
        grid=(rows // column,),
        in_specs=[pl.BlockSpec((depth, column), lambda i: (0, i))],
        out_specs=vmem,
        out_shape=jax.ShapeDtypeStruct((rows, depth), jnp.bfloat16),
        compiler_params=limit(16),
        cost_estimate=cost(0, 4 * rows * depth),
        name="transpose",
    )
    ladder = pl.pallas_call(
        functools.partial(ladder_kernel, chips, tile),
        in_specs=[vmem] * (2 + chips),
        out_specs=[vmem] * chips,
        out_shape=[message] * chips,
        scratch_shapes=[pltpu.VMEM((chips * WIDTH, depth), jnp.bfloat16)],
        compiler_params=limit(16),
        cost_estimate=cost(
            4 * rows * depth * chips * WIDTH,
            4 * rows * depth + 2 * chips * WIDTH * depth + 2 * chips * rows * LANES,
        ),
        name="ladder",
    )
    antisym = pl.pallas_call(
        functools.partial(antisym_kernel, chips, slabs, vir),
        in_specs=[smem] + [vmem] * chips,
        out_specs=[vmem, vmem],
        out_shape=[
            jax.ShapeDtypeStruct((slabs // 2, part_rows, LANES), jnp.float32),
            jax.ShapeDtypeStruct(parcel(slabs // 2), jnp.int16),
        ],
        scratch_shapes=[
            pltpu.VMEM((vir * vir, LANES), jnp.float32),
            pltpu.VMEM((part_rows, LANES), jnp.float32),
        ],
        compiler_params=limit(16),
        cost_estimate=cost(8 * vir * vir * LANES, 4 * vir * vir * LANES),
        name="antisym",
    )

    def hop(place, part, got):
        count = part.shape[0] // 2
        return pl.pallas_call(
            hop_kernel,
            in_specs=[smem, vmem, vmem],
            out_specs=[vmem, vmem],
            out_shape=[
                jax.ShapeDtypeStruct((count, part_rows, LANES), jnp.float32),
                jax.ShapeDtypeStruct(parcel(count), jnp.int16),
            ],
            compiler_params=limit(8),
            cost_estimate=cost(8 * count * part_rows * LANES, 16 * count * part_rows * LANES),
            name="hop",
        )(place, part, got)

    def finish(r, part, got, pair, virt, so_far):
        given = [] if so_far is None else [so_far]
        call = pl.pallas_call(
            finish_kernel,
            grid=(1,),
            in_specs=[
                vmem,
                vmem,
                pl.BlockSpec((1, 1, LANES), lambda i: (r, 0, 0)),
                vmem,
            ]
            + [pl.BlockSpec(memory_space=pl.ANY)] * len(given),
            out_specs=pl.BlockSpec((WIDTH, 2 * part_rows), lambda i: (r, 0)),
            out_shape=jax.ShapeDtypeStruct((num_pairs, 2 * part_rows), jnp.float32),
            input_output_aliases={4: 0} if given else {},
            compiler_params=limit(8),
            cost_estimate=cost(16 * part_rows * LANES, 16 * part_rows * LANES),
            name="finish",
        )
        return call(part, got, pair, virt, *given)

    sib_t = transpose(lax.ppermute(integrals, "pair", [(i, i ^ 1) for i in range(devices)]))
    own_t = transpose(integrals)

    occ_ids = jnp.arange(eps_occ.shape[0], dtype=jnp.int32)

    def pick(ids):
        return jnp.sum(jnp.where(ids[:, None] == occ_ids[None, :], eps_occ[None, :], 0.0), axis=1)

    eps_pair = (pick(pair_index[:, 0]) + pick(pair_index[:, 1])).reshape(chunks, 1, WIDTH)
    eps_pair = jnp.concatenate([eps_pair, eps_pair], axis=2)
    eps_mine = lax.dynamic_slice(eps_vir.reshape(slabs, 2, half), (z, 0, 0), (1, 2, half))[0]
    eps_virt = (eps_mine[:, :, None] + eps_vir[None, None, :]).reshape(2, part_rows).T

    place = jnp.stack([chip, core, z]).astype(jnp.int32)

    gathered = []
    for r in range(chunks):
        mine = amplitudes[r * WIDTH : (r + 1) * WIDTH]
        if gathered:
            mine, *gathered[-1] = lax.optimization_barrier((mine, *gathered[-1]))
        gathered.append([mine] + [to_chip(mine, d) for d in range(1, chips)])
        if r == 0:
            own_t, *gathered[0] = lax.optimization_barrier((own_t, *gathered[0]))

    def across(x, level):
        return lax.ppermute(x, "slab", [(i, i ^ level) for i in range(slabs)])

    def stages(r):
        sums = yield functools.partial(ladder, own_t, sib_t), *gathered[r]
        arrived = [to_chip(sums[d], d) for d in range(1, chips)]
        kept, away = yield functools.partial(antisym, place, sums[0]), *arrived
        got, level = across(away, 1), 2
        while level < slabs:
            bit = (z // level % 2)[None].astype(jnp.int32)
            kept, away = yield functools.partial(hop, bit, kept), got
            got, level = across(away, level), 2 * level
        yield functools.partial(finish, r, kept), got

    length = 3 + max(0, (slabs - 1).bit_length() - 1)

    def when(stage):
        r, k = stage
        if k == 0:
            return 18 * r + 14
        return 18 * r + 38 + (k - 1) * (17 + 2 * r) + (12 if k == length - 1 else 0)

    order = sorted(((r, k) for r in range(chunks) for k in range(length)), key=when)

    running = [stages(r) for r in range(chunks)]
    results = [None] * chunks
    update = token = None
    for r, k in order:
        call, *inputs = running[r].send(results[r])
        if token is not None:
            *inputs, token = lax.optimization_barrier((*inputs, token))
        if k == length - 1:
            update = call(*inputs, eps_pair, eps_virt, update)
        else:
            results[r] = call(*inputs)
            token = results[r][-1]
    return update


def solution(mesh):
    in_specs = (P("pair", "slab"), P("slab", "pair"), P("pair", None), P(), P())
    out_specs = P("pair", "slab")
    return jax.shard_map(
        functools.partial(on_device, mesh),
        mesh=mesh,
        in_specs=in_specs,
        out_specs=out_specs,
        check_vma=False,
    )
```

```python
import functools

import jax
import jax.numpy as jnp
from jax import lax
from jax.experimental import pallas as pl
from jax.experimental.pallas import tpu as pltpu
from jax.sharding import PartitionSpec as P

CORES = 2
WIDTH = 64
LANES = 2 * WIDTH
TAIL = 16
NT = (((1,), (1,)), ((), ()))


def tile_of(rows, most):
    return max(t for t in range(16, most + 1, 16) if rows % t == 0)


def is_low(shape):
    return lax.broadcasted_iota(jnp.int32, shape, len(shape) - 1) < WIDTH


def turn(values):
    return pltpu.roll(values, WIDTH, 1)


def encode(values, out_ref):
    tile = values.shape[0]
    peak = jnp.max(jnp.abs(values), axis=0, keepdims=True)
    power = jnp.ceil(jnp.log2(jnp.maximum(peak, 1e-30) * (1.0 / 32760.0)))
    codes = jnp.round(values * jnp.exp2(-power)).astype(jnp.int32)
    out_ref[pl.ds(0, tile), :] = codes.astype(jnp.int16)
    wide = jnp.broadcast_to(power.astype(jnp.int32), (TAIL, LANES))
    out_ref[pl.ds(tile, TAIL), :] = wide.astype(jnp.int16)


def decode(ref):
    tile = ref.shape[0] - TAIL
    power = ref[pl.ds(tile, TAIL), :].astype(jnp.int32).astype(jnp.float32)[0:1, :]
    return ref[pl.ds(0, tile), :].astype(jnp.int32).astype(jnp.float32) * jnp.exp2(power)


def transpose_kernel(in_ref, out_ref):
    width = in_ref.shape[1]
    at = pl.ds(pl.multiple_of(pl.program_id(0) * width, width), width)
    out_ref[at, :] = in_ref[...].T


def ladder_kernel(chips, tile, pieces, own_ref, sib_ref, *refs):
    rows_in, outs, rhs = refs[: len(pieces)], refs[len(pieces) : -1], refs[-1]
    at = 0
    for ref, (start, count) in zip(rows_in, pieces):
        rhs[pl.ds(at, count), :] = ref[pl.ds(start, count), :]
        at += count
    low = is_low((tile, LANES))
    group = min(4, chips)

    def step(i, carry):
        at = pl.ds(pl.multiple_of(i * tile, tile), tile)
        for first in range(0, chips, group):
            right = rhs[pl.ds(first * WIDTH, group * WIDTH), :]
            own = lax.dot_general(own_ref[at, :], right, NT, preferred_element_type=jnp.float32)
            sib = lax.dot_general(sib_ref[at, :], right, NT, preferred_element_type=jnp.float32)
            for k in range(0, group, 2):
                u = own[:, k * WIDTH : k * WIDTH + LANES]
                v = sib[:, k * WIDTH : k * WIDTH + LANES]
                encode(jnp.where(low, u, turn(v)), outs[first + k].at[i])
                encode(jnp.where(low, turn(u), v), outs[first + k + 1].at[i])
        return carry

    lax.fori_loop(0, own_ref.shape[0] // tile, step, 0)


def antisym_kernel(chips, slabs, vir, place_ref, *refs):
    arrived, (parts, *away, cube, sent) = refs[:chips], refs[chips:]
    chip, core, z = place_ref[0], place_ref[1], place_ref[2]
    tiles, tile = arrived[0].shape[0], arrived[0].shape[1] - TAIL
    rows = tiles * tile
    low = is_low((tile, LANES))
    for d in range(chips):
        base = (chip ^ d) * (CORES * rows)
        for t in range(tiles):
            values = decode(arrived[d].at[t])
            turned = turn(values)
            at_own = pl.multiple_of(base + core * rows + t * tile, tile)
            at_sib = pl.multiple_of(base + (1 - core) * rows + t * tile, tile)
            cube[pl.ds(at_own, tile), :] = jnp.where(low, values, turned)
            cube[pl.ds(at_sib, tile), :] = jnp.where(low, turned, values)

    half = vir // slabs // 2
    low = is_low((vir, LANES))
    part_tile = away[0].shape[2] - TAIL

    def into(slab, out):
        def body(k, carry):
            a = slab * (2 * half) + k
            b = a + half
            here = cube[pl.ds(pl.multiple_of(a * vir, vir), vir), :]
            other = cube[pl.ds(pl.multiple_of(b * vir, vir), vir), :]
            lower = here - cube[pl.ds(a, vir, stride=vir), :]
            upper = other - cube[pl.ds(b, vir, stride=vir), :]
            out[pl.ds(pl.multiple_of(k * vir, vir), vir), :] = jnp.where(low, lower, upper)
            return carry

        lax.fori_loop(0, half, body, 0)

    for e in reversed(range(1, slabs, 2)):
        into(e ^ z, sent)
        out = away[e // 2].at[0] if len(away) > 1 else away[0].at[e // 2]
        for t in range(out.shape[0]):
            encode(sent[pl.ds(t * part_tile, part_tile), :], out.at[t])
    for e in range(0, slabs, 2):
        into(e ^ z, parts.at[e // 2])


def hop_kernel(slots, parts, *refs):
    got, out = refs[:-1], refs[-1]
    tiles, tile = out.shape[1], out.shape[2] - TAIL
    for i, (part, places) in enumerate(slots):
        for t in range(tiles):
            total = parts[part, pl.ds(t * tile, tile), :]
            for k, slot in places:
                total = total + decode(got[k].at[slot, t])
            encode(total, out.at[i, t])


def finish_kernel(places, pair_ref, vir_ref, parts, *refs):
    got, out_ref = refs[:-1], refs[-1]
    tiles, tile = got[0].shape[1], got[0].shape[2] - TAIL
    low = is_low((tile, LANES))
    pair = pair_ref[0]
    half = tiles * tile
    for t in range(tiles):
        at = pl.ds(t * tile, tile)
        total = parts[0, at, :]
        for k, slot in places:
            total = total + decode(got[k].at[slot, t])
        virt = jnp.where(low, vir_ref[at, 0:1], vir_ref[at, 1:2])
        update = (total / (pair - virt)).T
        out_ref[:, pl.ds(t * tile, tile)] = update[:WIDTH]
        out_ref[:, pl.ds(half + t * tile, tile)] = update[WIDTH:]


def on_device(mesh, amplitudes, integrals, pair_index, eps_occ, eps_vir):
    devices, slabs = mesh.shape["pair"], mesh.shape["slab"]
    chips = devices // CORES
    num_pairs, depth = amplitudes.shape
    rows = integrals.shape[1]
    vir = eps_vir.shape[0]
    chunks = num_pairs // WIDTH
    half = vir // slabs // 2
    part_rows = half * vir
    tile, part_tile = tile_of(rows, 384), tile_of(part_rows, 384)
    tiles, part_tiles = rows // tile, part_rows // part_tile
    me, z = lax.axis_index("pair"), lax.axis_index("slab")
    chip, core = me // CORES, me % CORES

    def to_chip(x, d):
        return lax.ppermute(x, "pair", [(i, i ^ (d * CORES)) for i in range(devices)])

    def limit(mib):
        return pltpu.CompilerParams(vmem_limit_bytes=mib * 1024 * 1024)

    cost = pl.CostEstimate(flops=1024, bytes_accessed=1024, transcendentals=0)

    smem = pl.BlockSpec(memory_space=pltpu.SMEM)
    vmem = pl.BlockSpec(memory_space=pltpu.VMEM)
    message = jax.ShapeDtypeStruct((tiles, tile + TAIL, LANES), jnp.int16)

    def parcel(count):
        return (count, part_tiles, part_tile + TAIL, LANES)

    column = 128 if rows % 128 == 0 else rows
    transpose = pl.pallas_call(
        transpose_kernel,
        grid=(rows // column,),
        in_specs=[pl.BlockSpec((depth, column), lambda i: (0, i))],
        out_specs=vmem,
        out_shape=jax.ShapeDtypeStruct((rows, depth), jnp.bfloat16),
        compiler_params=limit(16),
        cost_estimate=cost,
        name="transpose",
    )

    def ladder(gathered):
        arrays, pieces = zip(*[(x, (start, count)) for x, start, count in gathered])
        call = pl.pallas_call(
            functools.partial(ladder_kernel, chips, tile, pieces),
            in_specs=[vmem] * (2 + len(arrays)),
            out_specs=[vmem] * chips,
            out_shape=[message] * chips,
            scratch_shapes=[pltpu.VMEM((chips * WIDTH, depth), jnp.bfloat16)],
            compiler_params=limit(16),
            cost_estimate=cost,
            name="ladder",
        )
        return functools.partial(call, own_t, sib_t), arrays

    def antisym(parcels):
        return pl.pallas_call(
            functools.partial(antisym_kernel, chips, slabs, vir),
            in_specs=[smem] + [vmem] * chips,
            out_specs=[vmem] * (1 + parcels),
            out_shape=[jax.ShapeDtypeStruct((slabs // 2, part_rows, LANES), jnp.float32)]
            + [jax.ShapeDtypeStruct(parcel(slabs // 2 // parcels), jnp.int16)] * parcels,
            scratch_shapes=[
                pltpu.VMEM((vir * vir, LANES), jnp.float32),
                pltpu.VMEM((part_rows, LANES), jnp.float32),
            ],
            compiler_params=limit(16),
            cost_estimate=cost,
            name="antisym",
        )

    def hop(slots, got_count):
        return pl.pallas_call(
            functools.partial(hop_kernel, slots),
            in_specs=[vmem] * (1 + got_count),
            out_specs=vmem,
            out_shape=jax.ShapeDtypeStruct(parcel(len(slots)), jnp.int16),
            compiler_params=limit(8),
            cost_estimate=cost,
            name="hop",
        )

    def finish(r, parts, got, places, so_far):
        given = [] if so_far is None else [so_far]
        return pl.pallas_call(
            functools.partial(finish_kernel, places),
            grid=(1,),
            in_specs=[pl.BlockSpec((1, 1, LANES), lambda i: (r, 0, 0))]
            + [vmem] * (2 + len(got))
            + [pl.BlockSpec(memory_space=pl.ANY)] * len(given),
            out_specs=pl.BlockSpec((WIDTH, 2 * part_rows), lambda i: (r, 0)),
            out_shape=jax.ShapeDtypeStruct((num_pairs, 2 * part_rows), jnp.float32),
            input_output_aliases={3 + len(got): 0} if given else {},
            compiler_params=limit(8),
            cost_estimate=cost,
            name="finish",
        )(eps_pair, eps_virt, parts, *got, *given)

    sib_t = transpose(lax.ppermute(integrals, "pair", [(i, i ^ 1) for i in range(devices)]))
    own_t = transpose(integrals)

    occ_ids = jnp.arange(eps_occ.shape[0], dtype=jnp.int32)

    def pick(ids):
        return jnp.sum(jnp.where(ids[:, None] == occ_ids[None, :], eps_occ[None, :], 0.0), axis=1)

    eps_pair = (pick(pair_index[:, 0]) + pick(pair_index[:, 1])).reshape(chunks, 1, WIDTH)
    eps_pair = jnp.concatenate([eps_pair, eps_pair], axis=2)
    eps_mine = lax.dynamic_slice(eps_vir.reshape(slabs, 2, half), (z, 0, 0), (1, 2, half))[0]
    eps_virt = (eps_mine[:, :, None] + eps_vir[None, None, :]).reshape(2, part_rows).T

    place = jnp.stack([chip, core, z]).astype(jnp.int32)

    def gather(mine, beside=()):
        count = mine.shape[0]
        if chips != 4:
            return [[(x, 0, count)] for x in [mine] + [to_chip(mine, d) for d in range(1, chips)]]
        one, two = to_chip(mine, 1), to_chip(mine, 2)
        if beside:
            one, two, *_ = lax.optimization_barrier((one, two, *beside))
        low, high = to_chip(two[: count // 2], 1), to_chip(one[count // 2 :], 2)
        parts = [(low, 0, count // 2), (high, 0, count // 2)]
        return [[(mine, 0, count)], [(one, 0, count)], [(two, 0, count)], parts]

    def cut(pieces, start, count):
        found, at = [], 0
        for x, first, rows_of in pieces:
            begin, end = max(start, at), min(start + count, at + rows_of)
            if begin < end:
                found.append((x, first + begin - at, end - begin))
            at += rows_of
        return found

    head = gather(amplitudes[:WIDTH], (own_t,))
    arrays = [x for pieces in head for x, _, _ in pieces]
    rest = amplitudes[WIDTH:]
    rest, own_t, sib_t, *arrays = lax.optimization_barrier((rest, own_t, sib_t, *arrays))
    fresh = iter(arrays)
    head = [[(next(fresh), start, count) for _, start, count in pieces] for pieces in head]
    tail = gather(rest)

    def rows_of(r):
        if r == 0:
            return [piece for pieces in head for piece in pieces]
        return [piece for pieces in tail for piece in cut(pieces, (r - 1) * WIDTH, WIDTH)]

    def across(x, level):
        return lax.ppermute(x, "slab", [(i, i ^ level) for i in range(slabs)])

    def stages(r):
        sums = yield ladder(rows_of(r))
        arrived = [to_chip(sums[d], d) for d in range(1, chips)]
        parcels = slabs // 2 if r == chunks - 1 else 1
        parts, *away = yield functools.partial(antisym(parcels), place, sums[0]), arrived
        away = [across(x, 1) for x in reversed(away)][::-1]
        each = slabs // 2 // parcels
        held = {e: [(away[e // 2 // each], e // 2 % each)] for e in range(0, slabs, 2)}

        def listed(wanted):
            arrays = []
            for e in wanted:
                arrays += [x for x, _ in held[e] if not any(x is y for y in arrays)]
            index = {id(x): k for k, x in enumerate(arrays)}
            return arrays, [(e // 2, [(index[id(x)], i) for x, i in held[e]]) for e in wanted]

        level = 2
        while level < slabs:
            leave = [e for e in held if e & level]
            got, slots = listed(leave)
            call = hop(slots, len(got))
            (out,) = yield (lambda *args, call=call: [call(parts, *args)]), got
            out = across(out, level)
            for i, e in enumerate(leave):
                held[e ^ level].append((out, i))
                del held[e]
            level *= 2
        got, ((_, places),) = listed([0])
        yield (lambda *args: finish(r, parts, args, places, update)), got

    length = 3 + max(0, (slabs - 1).bit_length() - 1)

    def when(stage):
        r, k = stage
        if k == 0:
            return 38 + 7 * r if r else 14
        return 18 * r + 40 + (k - 1) * (17 + 2 * r) + (12 if k == length - 1 else 0)

    order = sorted(((r, k) for r in range(chunks) for k in range(length)), key=when)

    running = [stages(r) for r in range(chunks)]
    results = [None] * chunks
    update = token = None
    for r, k in order:
        call, inputs = running[r].send(results[r])
        if token is not None:
            *inputs, token = lax.optimization_barrier((*inputs, token))
        if k == length - 1:
            update = call(*inputs)
        else:
            results[r] = call(*inputs)
            token = results[r][-1]
    return update


def solution(mesh):
    in_specs = (P("pair", "slab"), P("slab", "pair"), P("pair", None), P(), P())
    out_specs = P("pair", "slab")
    return jax.shard_map(
        functools.partial(on_device, mesh),
        mesh=mesh,
        in_specs=in_specs,
        out_specs=out_specs,
        check_vma=False,
    )
```

```python
import functools

import jax
import jax.numpy as jnp
from jax import lax
from jax.experimental import pallas as pl
from jax.experimental.pallas import tpu as pltpu
from jax.sharding import PartitionSpec as P

CORES = 2
WIDTH = 64
LANES = 2 * WIDTH
TAIL = 16
NT = (((1,), (1,)), ((), ()))


def tile_of(rows, most):
    return max(t for t in range(16, most + 1, 16) if rows % t == 0)


def is_low(shape):
    return lax.broadcasted_iota(jnp.int32, shape, len(shape) - 1) < WIDTH


def turn(values):
    return pltpu.roll(values, WIDTH, 1)


def encode(values, out_ref):
    tile = values.shape[0]
    peak = jnp.max(jnp.abs(values), axis=0, keepdims=True)
    power = jnp.ceil(jnp.log2(jnp.maximum(peak, 1e-30) * (1.0 / 32760.0)))
    codes = jnp.round(values * jnp.exp2(-power)).astype(jnp.int32)
    out_ref[pl.ds(0, tile), :] = codes.astype(jnp.int16)
    wide = jnp.broadcast_to(power.astype(jnp.int32), (TAIL, LANES))
    out_ref[pl.ds(tile, TAIL), :] = wide.astype(jnp.int16)


def decode(ref):
    tile = ref.shape[0] - TAIL
    power = ref[pl.ds(tile, TAIL), :].astype(jnp.int32).astype(jnp.float32)[0:1, :]
    return ref[pl.ds(0, tile), :].astype(jnp.int32).astype(jnp.float32) * jnp.exp2(power)


def transpose_kernel(in_ref, out_ref):
    width = in_ref.shape[1]
    at = pl.ds(pl.multiple_of(pl.program_id(0) * width, width), width)
    out_ref[at, :] = in_ref[...].T


def ladder_kernel(chips, tile, pieces, own_ref, sib_ref, *refs):
    rows_in, outs, rhs = refs[: len(pieces)], refs[len(pieces) : -1], refs[-1]
    at = 0
    for ref, (start, count) in zip(rows_in, pieces):
        rhs[pl.ds(at, count), :] = ref[pl.ds(start, count), :]
        at += count
    low = is_low((tile, LANES))
    group = min(4, chips)

    def step(i, carry):
        at = pl.ds(pl.multiple_of(i * tile, tile), tile)
        for first in range(0, chips, group):
            right = rhs[pl.ds(first * WIDTH, group * WIDTH), :]
            own = lax.dot_general(own_ref[at, :], right, NT, preferred_element_type=jnp.float32)
            sib = lax.dot_general(sib_ref[at, :], right, NT, preferred_element_type=jnp.float32)
            for k in range(0, group, 2):
                u = own[:, k * WIDTH : k * WIDTH + LANES]
                v = sib[:, k * WIDTH : k * WIDTH + LANES]
                encode(jnp.where(low, u, turn(v)), outs[first + k].at[i])
                encode(jnp.where(low, turn(u), v), outs[first + k + 1].at[i])
        return carry

    lax.fori_loop(0, own_ref.shape[0] // tile, step, 0)


def antisym_kernel(chips, slabs, vir, place_ref, *refs):
    arrived, (parts, *away, cube, sent) = refs[:chips], refs[chips:]
    chip, core, z = place_ref[0], place_ref[1], place_ref[2]
    tiles, tile = arrived[0].shape[0], arrived[0].shape[1] - TAIL
    rows = tiles * tile
    low = is_low((tile, LANES))
    for d in range(chips):
        base = (chip ^ d) * (CORES * rows)
        for t in range(tiles):
            values = decode(arrived[d].at[t])
            turned = turn(values)
            at_own = pl.multiple_of(base + core * rows + t * tile, tile)
            at_sib = pl.multiple_of(base + (1 - core) * rows + t * tile, tile)
            cube[pl.ds(at_own, tile), :] = jnp.where(low, values, turned)
            cube[pl.ds(at_sib, tile), :] = jnp.where(low, turned, values)

    half = vir // slabs // 2
    low = is_low((vir, LANES))
    part_tile = away[0].shape[2] - TAIL

    def into(slab, out):
        def body(k, carry):
            a = slab * (2 * half) + k
            b = a + half
            here = cube[pl.ds(pl.multiple_of(a * vir, vir), vir), :]
            other = cube[pl.ds(pl.multiple_of(b * vir, vir), vir), :]
            lower = here - cube[pl.ds(a, vir, stride=vir), :]
            upper = other - cube[pl.ds(b, vir, stride=vir), :]
            out[pl.ds(pl.multiple_of(k * vir, vir), vir), :] = jnp.where(low, lower, upper)
            return carry

        lax.fori_loop(0, half, body, 0)

    for e in reversed(range(1, slabs, 2)):
        into(e ^ z, sent)
        out = away[e // 2].at[0] if len(away) > 1 else away[0].at[e // 2]
        for t in range(out.shape[0]):
            encode(sent[pl.ds(t * part_tile, part_tile), :], out.at[t])
    for e in range(0, slabs, 2):
        into(e ^ z, parts.at[e // 2])


def hop_kernel(slots, parts, *refs):
    got, out = refs[:-1], refs[-1]
    tiles, tile = out.shape[1], out.shape[2] - TAIL
    for i, (part, places) in enumerate(slots):
        for t in range(tiles):
            total = parts[part, pl.ds(t * tile, tile), :]
            for k, slot in places:
                total = total + decode(got[k].at[slot, t])
            encode(total, out.at[i, t])


def finish_kernel(places, pair_ref, vir_ref, parts, *refs):
    got, out_ref = refs[:-1], refs[-1]
    tiles, tile = got[0].shape[1], got[0].shape[2] - TAIL
    low = is_low((tile, LANES))
    pair = pair_ref[0]
    half = tiles * tile
    for t in range(tiles):
        at = pl.ds(t * tile, tile)
        total = parts[0, at, :]
        for k, slot in places:
            total = total + decode(got[k].at[slot, t])
        virt = jnp.where(low, vir_ref[at, 0:1], vir_ref[at, 1:2])
        update = (total / (pair - virt)).T
        out_ref[:, pl.ds(t * tile, tile)] = update[:WIDTH]
        out_ref[:, pl.ds(half + t * tile, tile)] = update[WIDTH:]


def on_device(mesh, amplitudes, integrals, pair_index, eps_occ, eps_vir):
    devices, slabs = mesh.shape["pair"], mesh.shape["slab"]
    chips = devices // CORES
    num_pairs, depth = amplitudes.shape
    rows = integrals.shape[1]
    vir = eps_vir.shape[0]
    chunks = num_pairs // WIDTH
    half = vir // slabs // 2
    part_rows = half * vir
    tile, part_tile = tile_of(rows, 384), tile_of(part_rows, 384)
    tiles, part_tiles = rows // tile, part_rows // part_tile
    me, z = lax.axis_index("pair"), lax.axis_index("slab")
    chip, core = me // CORES, me % CORES

    def to_chip(x, d):
        return lax.ppermute(x, "pair", [(i, i ^ (d * CORES)) for i in range(devices)])

    def limit(mib):
        return pltpu.CompilerParams(vmem_limit_bytes=mib * 1024 * 1024)

    cost = pl.CostEstimate(flops=1024, bytes_accessed=1024, transcendentals=0)

    smem = pl.BlockSpec(memory_space=pltpu.SMEM)
    vmem = pl.BlockSpec(memory_space=pltpu.VMEM)
    message = jax.ShapeDtypeStruct((tiles, tile + TAIL, LANES), jnp.int16)

    def parcel(count):
        return (count, part_tiles, part_tile + TAIL, LANES)

    column = 128 if rows % 128 == 0 else rows
    transpose = pl.pallas_call(
        transpose_kernel,
        grid=(rows // column,),
        in_specs=[pl.BlockSpec((depth, column), lambda i: (0, i))],
        out_specs=vmem,
        out_shape=jax.ShapeDtypeStruct((rows, depth), jnp.bfloat16),
        compiler_params=limit(16),
        cost_estimate=cost,
        name="transpose",
    )

    def ladder(gathered):
        arrays, pieces = zip(*[(x, (start, count)) for x, start, count in gathered])
        call = pl.pallas_call(
            functools.partial(ladder_kernel, chips, tile, pieces),
            in_specs=[vmem] * (2 + len(arrays)),
            out_specs=[vmem] * chips,
            out_shape=[message] * chips,
            scratch_shapes=[pltpu.VMEM((chips * WIDTH, depth), jnp.bfloat16)],
            compiler_params=limit(16),
            cost_estimate=cost,
            name="ladder",
        )
        return functools.partial(call, own_t, sib_t), arrays

    def antisym(parcels):
        return pl.pallas_call(
            functools.partial(antisym_kernel, chips, slabs, vir),
            in_specs=[smem] + [vmem] * chips,
            out_specs=[vmem] * (1 + parcels),
            out_shape=[jax.ShapeDtypeStruct((slabs // 2, part_rows, LANES), jnp.float32)]
            + [jax.ShapeDtypeStruct(parcel(slabs // 2 // parcels), jnp.int16)] * parcels,
            scratch_shapes=[
                pltpu.VMEM((vir * vir, LANES), jnp.float32),
                pltpu.VMEM((part_rows, LANES), jnp.float32),
            ],
            compiler_params=limit(16),
            cost_estimate=cost,
            name="antisym",
        )

    def hop(slots, got_count):
        return pl.pallas_call(
            functools.partial(hop_kernel, slots),
            in_specs=[vmem] * (1 + got_count),
            out_specs=vmem,
            out_shape=jax.ShapeDtypeStruct(parcel(len(slots)), jnp.int16),
            compiler_params=limit(8),
            cost_estimate=cost,
            name="hop",
        )

    def finish(r, parts, got, places, so_far):
        given = [] if so_far is None else [so_far]
        return pl.pallas_call(
            functools.partial(finish_kernel, places),
            grid=(1,),
            in_specs=[pl.BlockSpec((1, 1, LANES), lambda i: (r, 0, 0))]
            + [vmem] * (2 + len(got))
            + [pl.BlockSpec(memory_space=pl.ANY)] * len(given),
            out_specs=pl.BlockSpec((WIDTH, 2 * part_rows), lambda i: (r, 0)),
            out_shape=jax.ShapeDtypeStruct((num_pairs, 2 * part_rows), jnp.float32),
            input_output_aliases={3 + len(got): 0} if given else {},
            compiler_params=limit(8),
            cost_estimate=cost,
            name="finish",
        )(eps_pair, eps_virt, parts, *got, *given)

    sib_t = transpose(lax.ppermute(integrals, "pair", [(i, i ^ 1) for i in range(devices)]))
    own_t = transpose(integrals)

    occ_ids = jnp.arange(eps_occ.shape[0], dtype=jnp.int32)

    def pick(ids):
        return jnp.sum(jnp.where(ids[:, None] == occ_ids[None, :], eps_occ[None, :], 0.0), axis=1)

    eps_pair = (pick(pair_index[:, 0]) + pick(pair_index[:, 1])).reshape(chunks, 1, WIDTH)
    eps_pair = jnp.concatenate([eps_pair, eps_pair], axis=2)
    eps_mine = lax.dynamic_slice(eps_vir.reshape(slabs, 2, half), (z, 0, 0), (1, 2, half))[0]
    eps_virt = (eps_mine[:, :, None] + eps_vir[None, None, :]).reshape(2, part_rows).T

    place = jnp.stack([chip, core, z]).astype(jnp.int32)

    mine = amplitudes
    if chips == 4:
        one, two = to_chip(mine, 1), to_chip(mine, 2)
        one, two, own_t, sib_t, eps_pair, eps_virt = lax.optimization_barrier(
            (one, two, own_t, sib_t, eps_pair, eps_virt)
        )
        middle = num_pairs // 2
        low, high = to_chip(two[:middle], 1), to_chip(one[middle:], 2)
        gathered = [[mine], [one], [two], [low, high]]
    else:
        gathered = [[mine]] + [[to_chip(mine, d)] for d in range(1, chips)]

    def rows_of(r):
        found = []
        for arrays in gathered:
            at = 0
            for x in arrays:
                begin = max(r * WIDTH, at)
                end = min((r + 1) * WIDTH, at + x.shape[0])
                if begin < end:
                    found.append((x, begin - at, end - begin))
                at += x.shape[0]
        return found

    def across(x, level):
        return lax.ppermute(x, "slab", [(i, i ^ level) for i in range(slabs)])

    def stages(r):
        sums = yield ladder(rows_of(r))
        sums, _ = lax.optimization_barrier((sums, turns[-1]))
        arrived = [to_chip(sums[d], d) for d in range(1, chips)]
        turns.append(arrived)
        parcels = slabs // 2 if r == chunks - 1 else 1
        parts, *away = yield functools.partial(antisym(parcels), place, sums[0]), arrived
        away = [across(x, 1) for x in reversed(away)][::-1]
        each = slabs // 2 // parcels
        held = {e: [(away[e // 2 // each], e // 2 % each)] for e in range(0, slabs, 2)}

        def listed(wanted):
            arrays = []
            for e in wanted:
                arrays += [x for x, _ in held[e] if not any(x is y for y in arrays)]
            index = {id(x): k for k, x in enumerate(arrays)}
            return arrays, [(e // 2, [(index[id(x)], i) for x, i in held[e]]) for e in wanted]

        level = 2
        while level < slabs:
            leave = [e for e in held if e & level]
            got, slots = listed(leave)
            call = hop(slots, len(got))
            (out,) = yield (lambda *args, call=call: [call(parts, *args)]), got
            out = across(out, level)
            for i, e in enumerate(leave):
                held[e ^ level].append((out, i))
                del held[e]
            level *= 2
        got, ((_, places),) = listed([0])
        yield (lambda *args: finish(r, parts, args, places, update)), got

    length = 3 + max(0, (slabs - 1).bit_length() - 1)

    def when(stage):
        r, k = stage
        if k == 0:
            return 30 + 5 * r
        return 15 * r + 54 + (k - 1) * 17 + (12 if k == length - 1 else 0)

    order = sorted(((r, k) for r in range(chunks) for k in range(length)), key=when)

    turns = [[]]
    running = [stages(r) for r in range(chunks)]
    results = [None] * chunks
    update = token = None
    for r, k in order:
        call, inputs = running[r].send(results[r])
        if token is not None:
            *inputs, token = lax.optimization_barrier((*inputs, token))
        if k == length - 1:
            update = call(*inputs)
        else:
            results[r] = call(*inputs)
            token = results[r][-1]
    return update


def solution(mesh):
    in_specs = (P("pair", "slab"), P("slab", "pair"), P("pair", None), P(), P())
    out_specs = P("pair", "slab")
    return jax.shard_map(
        functools.partial(on_device, mesh),
        mesh=mesh,
        in_specs=in_specs,
        out_specs=out_specs,
        check_vma=False,
    )
```

```python
import functools

import jax
import jax.numpy as jnp
from jax import lax
from jax.experimental import pallas as pl
from jax.experimental.pallas import tpu as pltpu
from jax.sharding import PartitionSpec as P

CORES = 2
WIDTH = 64
LANES = 2 * WIDTH
TAIL = 16
NT = (((1,), (1,)), ((), ()))


def tile_of(rows, most):
    return max(t for t in range(16, most + 1, 16) if rows % t == 0)


def is_low(shape):
    return lax.broadcasted_iota(jnp.int32, shape, len(shape) - 1) < WIDTH


def turn(values):
    return pltpu.roll(values, WIDTH, 1)


def encode(values, out_ref):
    tile = values.shape[0]
    peak = jnp.max(jnp.abs(values), axis=0, keepdims=True)
    power = jnp.ceil(jnp.log2(jnp.maximum(peak, 1e-30) * (1.0 / 32760.0)))
    codes = jnp.round(values * jnp.exp2(-power)).astype(jnp.int32)
    out_ref[pl.ds(0, tile), :] = codes.astype(jnp.int16)
    wide = jnp.broadcast_to(power.astype(jnp.int32), (TAIL, LANES))
    out_ref[pl.ds(tile, TAIL), :] = wide.astype(jnp.int16)


def decode(ref):
    tile = ref.shape[0] - TAIL
    power = ref[pl.ds(tile, TAIL), :].astype(jnp.int32).astype(jnp.float32)[0:1, :]
    return ref[pl.ds(0, tile), :].astype(jnp.int32).astype(jnp.float32) * jnp.exp2(power)


def transpose_kernel(in_ref, out_ref):
    width = in_ref.shape[1]
    at = pl.ds(pl.multiple_of(pl.program_id(0) * width, width), width)
    out_ref[at, :] = in_ref[...].T


def ladder_kernel(chips, tile, pieces, own_ref, sib_ref, *refs):
    rows_in, outs, rhs = refs[: len(pieces)], refs[len(pieces) : -1], refs[-1]
    at = 0
    for ref, (start, count) in zip(rows_in, pieces):
        rhs[pl.ds(at, count), :] = ref[pl.ds(start, count), :]
        at += count
    low = is_low((tile, LANES))
    group = min(4, chips)

    def step(i, carry):
        at = pl.ds(pl.multiple_of(i * tile, tile), tile)
        for first in range(0, chips, group):
            right = rhs[pl.ds(first * WIDTH, group * WIDTH), :]
            own = lax.dot_general(own_ref[at, :], right, NT, preferred_element_type=jnp.float32)
            sib = lax.dot_general(sib_ref[at, :], right, NT, preferred_element_type=jnp.float32)
            for k in range(0, group, 2):
                u = own[:, k * WIDTH : k * WIDTH + LANES]
                v = sib[:, k * WIDTH : k * WIDTH + LANES]
                encode(jnp.where(low, u, turn(v)), outs[first + k].at[i])
                encode(jnp.where(low, turn(u), v), outs[first + k + 1].at[i])
        return carry

    lax.fori_loop(0, own_ref.shape[0] // tile, step, 0)


def antisym_kernel(chips, slabs, vir, place_ref, *refs):
    arrived, (parts, *away, cube, sent) = refs[:chips], refs[chips:]
    chip, core, z = place_ref[0], place_ref[1], place_ref[2]
    tiles, tile = arrived[0].shape[0], arrived[0].shape[1] - TAIL
    rows = tiles * tile
    low = is_low((tile, LANES))
    for d in range(chips):
        base = (chip ^ d) * (CORES * rows)
        for t in range(tiles):
            values = decode(arrived[d].at[t])
            turned = turn(values)
            at_own = pl.multiple_of(base + core * rows + t * tile, tile)
            at_sib = pl.multiple_of(base + (1 - core) * rows + t * tile, tile)
            cube[pl.ds(at_own, tile), :] = jnp.where(low, values, turned)
            cube[pl.ds(at_sib, tile), :] = jnp.where(low, turned, values)

    half = vir // slabs // 2
    low = is_low((vir, LANES))
    part_tile = away[0].shape[2] - TAIL

    def into(slab, out):
        def body(k, carry):
            a = slab * (2 * half) + k
            b = a + half
            here = cube[pl.ds(pl.multiple_of(a * vir, vir), vir), :]
            other = cube[pl.ds(pl.multiple_of(b * vir, vir), vir), :]
            lower = here - cube[pl.ds(a, vir, stride=vir), :]
            upper = other - cube[pl.ds(b, vir, stride=vir), :]
            out[pl.ds(pl.multiple_of(k * vir, vir), vir), :] = jnp.where(low, lower, upper)
            return carry

        lax.fori_loop(0, half, body, 0)

    for e in reversed(range(1, slabs, 2)):
        into(e ^ z, sent)
        out = away[e // 2].at[0] if len(away) > 1 else away[0].at[e // 2]
        for t in range(out.shape[0]):
            encode(sent[pl.ds(t * part_tile, part_tile), :], out.at[t])
    for e in range(0, slabs, 2):
        into(e ^ z, parts.at[e // 2])


def hop_kernel(slots, parts, *refs):
    got, out = refs[:-1], refs[-1]
    tiles, tile = out.shape[1], out.shape[2] - TAIL
    for i, (part, places) in enumerate(slots):
        for t in range(tiles):
            total = parts[part, pl.ds(t * tile, tile), :]
            for k, slot in places:
                total = total + decode(got[k].at[slot, t])
            encode(total, out.at[i, t])


def finish_kernel(places, count, pair_ref, vir_ref, parts, *refs):
    got, out_ref = refs[:count], refs[-1]
    tiles, tile = got[0].shape[1], got[0].shape[2] - TAIL
    low = is_low((tile, LANES))
    pair = pair_ref[0]
    half = tiles * tile
    for t in range(tiles):
        at = pl.ds(t * tile, tile)
        total = parts[0, at, :]
        for k, slot in places:
            total = total + decode(got[k].at[slot, t])
        virt = jnp.where(low, vir_ref[at, 0:1], vir_ref[at, 1:2])
        update = (total / (pair - virt)).T
        out_ref[:, pl.ds(t * tile, tile)] = update[:WIDTH]
        out_ref[:, pl.ds(half + t * tile, tile)] = update[WIDTH:]


def on_device(mesh, amplitudes, integrals, pair_index, eps_occ, eps_vir):
    devices, slabs = mesh.shape["pair"], mesh.shape["slab"]
    chips = devices // CORES
    num_pairs, depth = amplitudes.shape
    rows = integrals.shape[1]
    vir = eps_vir.shape[0]
    chunks = num_pairs // WIDTH
    half = vir // slabs // 2
    part_rows = half * vir
    tile, part_tile = tile_of(rows, 384), tile_of(part_rows, 384)
    tiles, part_tiles = rows // tile, part_rows // part_tile
    me, z = lax.axis_index("pair"), lax.axis_index("slab")
    chip, core = me // CORES, me % CORES

    def to_chip(x, d):
        return lax.ppermute(x, "pair", [(i, i ^ (d * CORES)) for i in range(devices)])

    def limit(mib):
        return pltpu.CompilerParams(vmem_limit_bytes=mib * 1024 * 1024)

    cost = pl.CostEstimate(flops=1024, bytes_accessed=1024, transcendentals=0)

    smem = pl.BlockSpec(memory_space=pltpu.SMEM)
    vmem = pl.BlockSpec(memory_space=pltpu.VMEM)
    message = jax.ShapeDtypeStruct((tiles, tile + TAIL, LANES), jnp.int16)

    def parcel(count):
        return (count, part_tiles, part_tile + TAIL, LANES)

    column = max((c for c in (384, 256, 128) if rows % c == 0), default=rows)
    transpose = pl.pallas_call(
        transpose_kernel,
        grid=(rows // column,),
        in_specs=[pl.BlockSpec((depth, column), lambda i: (0, i))],
        out_specs=vmem,
        out_shape=jax.ShapeDtypeStruct((rows, depth), jnp.bfloat16),
        compiler_params=limit(16),
        cost_estimate=cost,
        name="transpose",
    )

    def ordered(body, inputs, in_specs, out_specs, out_shape, mib, scratch=(), name=None, **more):
        given, made = len(in_specs), len(out_specs)

        def kernel(*refs):
            token_in, token_out = refs[given], refs[given + 1 + made]
            token_out[...] = token_in[...]
            outs = refs[given + 1 : given + 1 + made]
            body(*refs[:given], *outs, *refs[given + made + 2 :])

        def call(token, *args):
            return pl.pallas_call(
                kernel,
                in_specs=[*in_specs, vmem],
                out_specs=[*out_specs, vmem],
                out_shape=[*out_shape, jax.ShapeDtypeStruct(token.shape, token.dtype)],
                scratch_shapes=scratch,
                compiler_params=limit(mib),
                cost_estimate=cost,
                name=name,
                **more,
            )(*args, token)

        return call, inputs

    def ladder(gathered):
        arrays, pieces = zip(*[(x, (start, count)) for x, start, count in gathered])
        return ordered(
            functools.partial(ladder_kernel, chips, tile, pieces),
            [own_t, sib_t, *arrays],
            [vmem] * (2 + len(arrays)),
            [vmem] * chips,
            [message] * chips,
            16,
            [pltpu.VMEM((chips * WIDTH, depth), jnp.bfloat16)],
            name="ladder",
        )

    def antisym(parcels, arrived):
        return ordered(
            functools.partial(antisym_kernel, chips, slabs, vir),
            [place, *arrived],
            [smem] + [vmem] * chips,
            [vmem] * (1 + parcels),
            [jax.ShapeDtypeStruct((slabs // 2, part_rows, LANES), jnp.float32)]
            + [jax.ShapeDtypeStruct(parcel(slabs // 2 // parcels), jnp.int16)] * parcels,
            16,
            [
                pltpu.VMEM((vir * vir, LANES), jnp.float32),
                pltpu.VMEM((part_rows, LANES), jnp.float32),
            ],
            name="antisym",
        )

    def hop(slots, parts, got):
        return ordered(
            functools.partial(hop_kernel, slots),
            [parts, *got],
            [vmem] * (1 + len(got)),
            [vmem],
            [jax.ShapeDtypeStruct(parcel(len(slots)), jnp.int16)],
            8,
            name="hop",
        )

    def finish(r, parts, got, places, so_far):
        given = [] if so_far is None else [so_far]
        return ordered(
            functools.partial(finish_kernel, places, len(got)),
            [eps_pair, eps_virt, parts, *got, *given],
            [pl.BlockSpec((1, 1, LANES), lambda i: (r, 0, 0))]
            + [vmem] * (2 + len(got))
            + [pl.BlockSpec(memory_space=pl.ANY)] * len(given),
            [pl.BlockSpec((WIDTH, 2 * part_rows), lambda i: (r, 0))],
            [jax.ShapeDtypeStruct((num_pairs, 2 * part_rows), jnp.float32)],
            8,
            name="finish",
            grid=(1,),
            input_output_aliases={3 + len(got): 0} if given else {},
        )

    in_hbm = functools.partial(pltpu.with_memory_space_constraint, memory_space=pltpu.HBM)
    own_t = transpose(in_hbm(integrals))
    swapped = lax.ppermute(integrals, "pair", [(i, i ^ 1) for i in range(devices)])
    sib_t = transpose(swapped)

    occ_ids = jnp.arange(eps_occ.shape[0], dtype=jnp.int32)

    def pick(ids):
        return jnp.sum(jnp.where(ids[:, None] == occ_ids[None, :], eps_occ[None, :], 0.0), axis=1)

    eps_pair = (pick(pair_index[:, 0]) + pick(pair_index[:, 1])).reshape(chunks, 1, WIDTH)
    eps_pair = jnp.concatenate([eps_pair, eps_pair], axis=2)
    eps_mine = lax.dynamic_slice(eps_vir.reshape(slabs, 2, half), (z, 0, 0), (1, 2, half))[0]
    eps_virt = (eps_mine[:, :, None] + eps_vir[None, None, :]).reshape(2, part_rows).T

    place = jnp.stack([chip, core, z]).astype(jnp.int32)

    mine = amplitudes
    if chips == 4:
        one, two = to_chip(mine, 1), to_chip(mine, 2)
        one, two, own_t, sib_t, eps_pair, eps_virt = lax.optimization_barrier(
            (one, two, own_t, sib_t, eps_pair, eps_virt)
        )
        middle = num_pairs // 2
        low, high = to_chip(two[:middle], 1), to_chip(one[middle:], 2)
        gathered = [[mine], [one], [two], [low, high]]
    else:
        gathered = [[mine]] + [[to_chip(mine, d)] for d in range(1, chips)]

    def rows_of(r):
        found = []
        for arrays in gathered:
            at = 0
            for x in arrays:
                begin = max(r * WIDTH, at)
                end = min((r + 1) * WIDTH, at + x.shape[0])
                if begin < end:
                    found.append((x, begin - at, end - begin))
                at += x.shape[0]
        return found

    def across(x, level):
        return lax.ppermute(x, "slab", [(i, i ^ level) for i in range(slabs)])

    def stages(r):
        sums = yield ladder(rows_of(r))
        if r:
            sums, _ = lax.optimization_barrier((sums, turns[-1] + results[-1][:1]))
        arrived = [to_chip(sums[d], d) for d in range(1, chips)]
        turns.append(arrived)
        parcels = slabs // 2 if r == chunks - 1 else 1
        parts, *away = yield antisym(parcels, [sums[0], *arrived])
        away = [across(x, 1) for x in reversed(away)][::-1]
        each = slabs // 2 // parcels
        held = {e: [(away[e // 2 // each], e // 2 % each)] for e in range(0, slabs, 2)}

        def listed(wanted):
            arrays = []
            for e in wanted:
                arrays += [x for x, _ in held[e] if not any(x is y for y in arrays)]
            index = {id(x): k for k, x in enumerate(arrays)}
            return arrays, [(e // 2, [(index[id(x)], i) for x, i in held[e]]) for e in wanted]

        level = 2
        while level < slabs:
            leave = [e for e in held if e & level]
            got, slots = listed(leave)
            (out,) = yield hop(slots, parts, got)
            out = across(out, level)
            for i, e in enumerate(leave):
                held[e ^ level].append((out, i))
                del held[e]
            level *= 2
        got, ((_, places),) = listed([0])
        yield finish(r, parts, got, places, update)

    length = 3 + max(0, (slabs - 1).bit_length() - 1)

    def when(stage):
        r, k = stage
        if k == 0:
            return 30 + 5 * r
        return 15 * r + 54 + (k - 1) * 17 - (1 if k == length - 1 else 0)

    order = sorted(((r, k) for r in range(chunks) for k in range(length)), key=when)

    turns = [[]]
    running = [stages(r) for r in range(chunks)]
    results = [None] * chunks
    update, token = None, jnp.zeros((8, LANES), jnp.float32)
    for r, k in order:
        call, inputs = running[r].send(results[r])
        *results[r], token = call(token, *inputs)
        if k == length - 1:
            (update,) = results[r]
    return update


def solution(mesh):
    in_specs = (P("pair", "slab"), P("slab", "pair"), P("pair", None), P(), P())
    out_specs = P("pair", "slab")
    return jax.shard_map(
        functools.partial(on_device, mesh),
        mesh=mesh,
        in_specs=in_specs,
        out_specs=out_specs,
        check_vma=False,
    )
```

```python
import functools

import jax
import jax.numpy as jnp
from jax import lax
from jax.experimental import pallas as pl
from jax.experimental.pallas import tpu as pltpu
from jax.sharding import PartitionSpec as P

CORES = 2
WIDTH = 64
LANES = 2 * WIDTH
TAIL = 16
NT = (((1,), (1,)), ((), ()))


def tile_of(rows, most):
    return max(t for t in range(16, most + 1, 16) if rows % t == 0)


def is_low(shape):
    return lax.broadcasted_iota(jnp.int32, shape, len(shape) - 1) < WIDTH


def turn(values):
    return pltpu.roll(values, WIDTH, 1)


def encode(values, out_ref):
    tile = values.shape[0]
    peak = jnp.max(jnp.abs(values), axis=0, keepdims=True)
    power = jnp.ceil(jnp.log2(jnp.maximum(peak, 1e-30) * (1.0 / 32760.0)))
    codes = jnp.round(values * jnp.exp2(-power)).astype(jnp.int32)
    out_ref[pl.ds(0, tile), :] = codes.astype(jnp.int16)
    wide = jnp.broadcast_to(power.astype(jnp.int32), (TAIL, LANES))
    out_ref[pl.ds(tile, TAIL), :] = wide.astype(jnp.int16)


def decode(ref):
    tile = ref.shape[0] - TAIL
    power = ref[pl.ds(tile, TAIL), :].astype(jnp.int32).astype(jnp.float32)[0:1, :]
    return ref[pl.ds(0, tile), :].astype(jnp.int32).astype(jnp.float32) * jnp.exp2(power)


def transpose_kernel(in_ref, out_ref):
    width = in_ref.shape[1]
    at = pl.ds(pl.multiple_of(pl.program_id(0) * width, width), width)
    out_ref[at, :] = in_ref[...].T


def ladder_kernel(chips, tile, pieces, own_ref, sib_ref, *refs):
    rows_in, outs, rhs = refs[: len(pieces)], refs[len(pieces) : -1], refs[-1]
    at = 0
    for ref, (start, count) in zip(rows_in, pieces):
        rhs[pl.ds(at, count), :] = ref[pl.ds(start, count), :]
        at += count
    low = is_low((tile, LANES))
    group = min(4, chips)

    def step(i, carry):
        at = pl.ds(pl.multiple_of(i * tile, tile), tile)
        for first in range(0, chips, group):
            right = rhs[pl.ds(first * WIDTH, group * WIDTH), :]
            own = lax.dot_general(own_ref[at, :], right, NT, preferred_element_type=jnp.float32)
            sib = lax.dot_general(sib_ref[at, :], right, NT, preferred_element_type=jnp.float32)
            for k in range(0, group, 2):
                u = own[:, k * WIDTH : k * WIDTH + LANES]
                v = sib[:, k * WIDTH : k * WIDTH + LANES]
                encode(jnp.where(low, u, turn(v)), outs[first + k].at[i])
                encode(jnp.where(low, turn(u), v), outs[first + k + 1].at[i])
        return carry

    lax.fori_loop(0, own_ref.shape[0] // tile, step, 0)


def antisym_kernel(chips, slabs, vir, place_ref, *refs):
    arrived, (parts, *away, cube, sent) = refs[:chips], refs[chips:]
    chip, core, z = place_ref[0], place_ref[1], place_ref[2]
    tiles, tile = arrived[0].shape[0], arrived[0].shape[1] - TAIL
    rows = tiles * tile
    low = is_low((tile, LANES))
    for d in range(chips):
        base = (chip ^ d) * (CORES * rows)
        for t in range(tiles):
            values = decode(arrived[d].at[t])
            turned = turn(values)
            at_own = pl.multiple_of(base + core * rows + t * tile, tile)
            at_sib = pl.multiple_of(base + (1 - core) * rows + t * tile, tile)
            cube[pl.ds(at_own, tile), :] = jnp.where(low, values, turned)
            cube[pl.ds(at_sib, tile), :] = jnp.where(low, turned, values)

    half = vir // slabs // 2
    low = is_low((vir, LANES))
    part_tile = away[0].shape[2] - TAIL

    def into(slab, out):
        def body(k, carry):
            a = slab * (2 * half) + k
            b = a + half
            here = cube[pl.ds(pl.multiple_of(a * vir, vir), vir), :]
            other = cube[pl.ds(pl.multiple_of(b * vir, vir), vir), :]
            lower = here - cube[pl.ds(a, vir, stride=vir), :]
            upper = other - cube[pl.ds(b, vir, stride=vir), :]
            out[pl.ds(pl.multiple_of(k * vir, vir), vir), :] = jnp.where(low, lower, upper)
            return carry

        lax.fori_loop(0, half, body, 0)

    for e in reversed(range(1, slabs, 2)):
        into(e ^ z, sent)
        out = away[e // 2].at[0] if len(away) > 1 else away[0].at[e // 2]
        for t in range(out.shape[0]):
            encode(sent[pl.ds(t * part_tile, part_tile), :], out.at[t])
    for e in range(0, slabs, 2):
        into(e ^ z, parts.at[e // 2])


def hop_kernel(slots, parts, *refs):
    got, out = refs[:-1], refs[-1]
    tiles, tile = out.shape[1], out.shape[2] - TAIL
    for i, (part, places) in enumerate(slots):
        for t in range(tiles):
            total = parts[part, pl.ds(t * tile, tile), :]
            for k, slot in places:
                total = total + decode(got[k].at[slot, t])
            encode(total, out.at[i, t])


def finish_kernel(places, count, pair_ref, vir_ref, parts, *refs):
    got, out_ref = refs[:count], refs[-1]
    tiles, tile = got[0].shape[1], got[0].shape[2] - TAIL
    low = is_low((tile, LANES))
    pair = pair_ref[0]
    half = tiles * tile
    for t in range(tiles):
        at = pl.ds(t * tile, tile)
        total = parts[0, at, :]
        for k, slot in places:
            total = total + decode(got[k].at[slot, t])
        virt = jnp.where(low, vir_ref[at, 0:1], vir_ref[at, 1:2])
        update = (total / (pair - virt)).T
        out_ref[:, pl.ds(t * tile, tile)] = update[:WIDTH]
        out_ref[:, pl.ds(half + t * tile, tile)] = update[WIDTH:]


def on_device(mesh, amplitudes, integrals, pair_index, eps_occ, eps_vir):
    devices, slabs = mesh.shape["pair"], mesh.shape["slab"]
    chips = devices // CORES
    num_pairs, depth = amplitudes.shape
    rows = integrals.shape[1]
    vir = eps_vir.shape[0]
    chunks = num_pairs // WIDTH
    half = vir // slabs // 2
    part_rows = half * vir
    tile, part_tile = tile_of(rows, 384), tile_of(part_rows, 384)
    tiles, part_tiles = rows // tile, part_rows // part_tile
    me, z = lax.axis_index("pair"), lax.axis_index("slab")
    chip, core = me // CORES, me % CORES

    def to_chip(x, d):
        return lax.ppermute(x, "pair", [(i, i ^ (d * CORES)) for i in range(devices)])

    def limit(mib):
        return pltpu.CompilerParams(vmem_limit_bytes=mib * 1024 * 1024)

    def cost(flops, moved):
        return pl.CostEstimate(flops=flops, bytes_accessed=moved, transcendentals=0)

    smem = pl.BlockSpec(memory_space=pltpu.SMEM)
    vmem = pl.BlockSpec(memory_space=pltpu.VMEM)
    message = jax.ShapeDtypeStruct((tiles, tile + TAIL, LANES), jnp.int16)

    def parcel(count):
        return (count, part_tiles, part_tile + TAIL, LANES)

    column = max((c for c in (384, 256, 128) if rows % c == 0), default=rows)
    transpose = pl.pallas_call(
        transpose_kernel,
        grid=(rows // column,),
        in_specs=[pl.BlockSpec((depth, column), lambda i: (0, i))],
        out_specs=vmem,
        out_shape=jax.ShapeDtypeStruct((rows, depth), jnp.bfloat16),
        compiler_params=limit(16),
        cost_estimate=cost(0, 4 * rows * depth),
        name="transpose",
    )

    def ordered(
        body, flops, inputs, in_specs, out_specs, out_shape, mib, scratch=(), name=None, **more
    ):
        given, made = len(in_specs), len(out_specs)
        moved = sum(x.size * x.dtype.itemsize for x in (*inputs, *out_shape))

        def kernel(*refs):
            token_in, token_out = refs[given], refs[given + 1 + made]
            token_out[...] = token_in[...]
            outs = refs[given + 1 : given + 1 + made]
            body(*refs[:given], *outs, *refs[given + made + 2 :])

        def call(token, *args):
            return pl.pallas_call(
                kernel,
                in_specs=[*in_specs, vmem],
                out_specs=[*out_specs, vmem],
                out_shape=[*out_shape, jax.ShapeDtypeStruct(token.shape, token.dtype)],
                scratch_shapes=scratch,
                compiler_params=limit(mib),
                cost_estimate=cost(flops, moved),
                name=name,
                **more,
            )(*args, token)

        return call, inputs

    def ladder(gathered):
        arrays, pieces = zip(*[(x, (start, count)) for x, start, count in gathered])
        return ordered(
            functools.partial(ladder_kernel, chips, tile, pieces),
            4 * rows * depth * chips * WIDTH,
            [own_t, sib_t, *arrays],
            [vmem] * (2 + len(arrays)),
            [vmem] * chips,
            [message] * chips,
            16,
            [pltpu.VMEM((chips * WIDTH, depth), jnp.bfloat16)],
            name="ladder",
        )

    def antisym(parcels, arrived):
        return ordered(
            functools.partial(antisym_kernel, chips, slabs, vir),
            8 * vir * vir * LANES,
            [place, *arrived],
            [smem] + [vmem] * chips,
            [vmem] * (1 + parcels),
            [jax.ShapeDtypeStruct((slabs // 2, part_rows, LANES), jnp.float32)]
            + [jax.ShapeDtypeStruct(parcel(slabs // 2 // parcels), jnp.int16)] * parcels,
            16,
            [
                pltpu.VMEM((vir * vir, LANES), jnp.float32),
                pltpu.VMEM((part_rows, LANES), jnp.float32),
            ],
            name="antisym",
        )

    def hop(slots, parts, got):
        return ordered(
            functools.partial(hop_kernel, slots),
            8 * part_rows * LANES,
            [parts, *got],
            [vmem] * (1 + len(got)),
            [vmem],
            [jax.ShapeDtypeStruct(parcel(len(slots)), jnp.int16)],
            8,
            name="hop",
        )

    def finish(r, parts, got, places, so_far):
        given = [] if so_far is None else [so_far]
        return ordered(
            functools.partial(finish_kernel, places, len(got)),
            16 * part_rows * LANES,
            [eps_pair, eps_virt, parts, *got, *given],
            [pl.BlockSpec((1, 1, LANES), lambda i: (r, 0, 0))]
            + [vmem] * (2 + len(got))
            + [pl.BlockSpec(memory_space=pl.ANY)] * len(given),
            [pl.BlockSpec((WIDTH, 2 * part_rows), lambda i: (r, 0))],
            [jax.ShapeDtypeStruct((num_pairs, 2 * part_rows), jnp.float32)],
            8,
            name="finish",
            grid=(1,),
            input_output_aliases={3 + len(got): 0} if given else {},
        )

    in_hbm = functools.partial(pltpu.with_memory_space_constraint, memory_space=pltpu.HBM)
    own_t = transpose(in_hbm(integrals))
    swapped = lax.ppermute(integrals, "pair", [(i, i ^ 1) for i in range(devices)])
    sib_t = transpose(swapped)

    occ_ids = jnp.arange(eps_occ.shape[0], dtype=jnp.int32)

    def pick(ids):
        return jnp.sum(jnp.where(ids[:, None] == occ_ids[None, :], eps_occ[None, :], 0.0), axis=1)

    eps_pair = (pick(pair_index[:, 0]) + pick(pair_index[:, 1])).reshape(chunks, 1, WIDTH)
    eps_pair = jnp.concatenate([eps_pair, eps_pair], axis=2)
    eps_mine = lax.dynamic_slice(eps_vir.reshape(slabs, 2, half), (z, 0, 0), (1, 2, half))[0]
    eps_virt = (eps_mine[:, :, None] + eps_vir[None, None, :]).reshape(2, part_rows).T

    place = jnp.stack([chip, core, z]).astype(jnp.int32)

    mine = amplitudes
    if chips == 4:
        one, two = to_chip(mine, 1), to_chip(mine, 2)
        one, two, own_t, sib_t, eps_pair, eps_virt = lax.optimization_barrier(
            (one, two, own_t, sib_t, eps_pair, eps_virt)
        )
        middle = num_pairs // 2
        low, high = to_chip(two[:middle], 1), to_chip(one[middle:], 2)
        gathered = [[mine], [one], [two], [low, high]]
    else:
        gathered = [[mine]] + [[to_chip(mine, d)] for d in range(1, chips)]

    def rows_of(r):
        found = []
        for arrays in gathered:
            at = 0
            for x in arrays:
                begin = max(r * WIDTH, at)
                end = min((r + 1) * WIDTH, at + x.shape[0])
                if begin < end:
                    found.append((x, begin - at, end - begin))
                at += x.shape[0]
        return found

    def across(x, level):
        return lax.ppermute(x, "slab", [(i, i ^ level) for i in range(slabs)])

    def stages(r):
        sums = yield ladder(rows_of(r))
        if r:
            sums, _ = lax.optimization_barrier((sums, turns[-1] + results[-1][:1]))
        arrived = [to_chip(sums[d], d) for d in range(1, chips)]
        turns.append(arrived)
        parcels = slabs // 2 if r == chunks - 1 else 1
        parts, *away = yield antisym(parcels, [sums[0], *arrived])
        away = [across(x, 1) for x in reversed(away)][::-1]
        each = slabs // 2 // parcels
        held = {e: [(away[e // 2 // each], e // 2 % each)] for e in range(0, slabs, 2)}

        def listed(wanted):
            arrays = []
            for e in wanted:
                arrays += [x for x, _ in held[e] if not any(x is y for y in arrays)]
            index = {id(x): k for k, x in enumerate(arrays)}
            return arrays, [(e // 2, [(index[id(x)], i) for x, i in held[e]]) for e in wanted]

        level = 2
        while level < slabs:
            leave = [e for e in held if e & level]
            got, slots = listed(leave)
            (out,) = yield hop(slots, parts, got)
            out = across(out, level)
            for i, e in enumerate(leave):
                held[e ^ level].append((out, i))
                del held[e]
            level *= 2
        got, ((_, places),) = listed([0])
        yield finish(r, parts, got, places, update)

    length = 3 + max(0, (slabs - 1).bit_length() - 1)

    def when(stage):
        r, k = stage
        if k == 0:
            return 30 + 5 * r
        return 15 * r + 54 + (k - 1) * 17 - (1 if k == length - 1 else 0)

    order = sorted(((r, k) for r in range(chunks) for k in range(length)), key=when)

    turns = [[]]
    running = [stages(r) for r in range(chunks)]
    results = [None] * chunks
    update, token = None, jnp.zeros((8, LANES), jnp.float32)
    for r, k in order:
        call, inputs = running[r].send(results[r])
        *results[r], token = call(token, *inputs)
        if k == length - 1:
            (update,) = results[r]
    return update


def solution(mesh):
    in_specs = (P("pair", "slab"), P("slab", "pair"), P("pair", None), P(), P())
    out_specs = P("pair", "slab")
    return jax.shard_map(
        functools.partial(on_device, mesh),
        mesh=mesh,
        in_specs=in_specs,
        out_specs=out_specs,
        check_vma=False,
    )
```

```python
import functools

import jax
import jax.numpy as jnp
from jax import lax
from jax.experimental import pallas as pl
from jax.experimental.pallas import tpu as pltpu
from jax.sharding import PartitionSpec as P

CORES = 2
WIDTH = 64
LANES = 2 * WIDTH
TAIL = 16
NT = (((1,), (1,)), ((), ()))


def tile_of(rows, most):
    return max(t for t in range(16, most + 1, 16) if rows % t == 0)


def is_low(shape):
    return lax.broadcasted_iota(jnp.int32, shape, len(shape) - 1) < WIDTH


def turn(values):
    return pltpu.roll(values, WIDTH, 1)


def encode(values, out_ref):
    tile = values.shape[0]
    peak = jnp.max(jnp.abs(values), axis=0, keepdims=True)
    power = jnp.ceil(jnp.log2(jnp.maximum(peak, 1e-30) * (1.0 / 32760.0)))
    codes = jnp.round(values * jnp.exp2(-power)).astype(jnp.int32)
    out_ref[pl.ds(0, tile), :] = codes.astype(jnp.int16)
    wide = jnp.broadcast_to(power.astype(jnp.int32), (TAIL, LANES))
    out_ref[pl.ds(tile, TAIL), :] = wide.astype(jnp.int16)


def decode(ref):
    tile = ref.shape[0] - TAIL
    power = ref[pl.ds(tile, TAIL), :].astype(jnp.int32).astype(jnp.float32)[0:1, :]
    return ref[pl.ds(0, tile), :].astype(jnp.int32).astype(jnp.float32) * jnp.exp2(power)


def transpose_kernel(in_ref, out_ref):
    width = in_ref.shape[1]
    at = pl.ds(pl.multiple_of(pl.program_id(0) * width, width), width)
    out_ref[at, :] = in_ref[...].T


def ladder_kernel(chips, tile, pieces, own_ref, sib_ref, *refs):
    rows_in, outs, rhs = refs[: len(pieces)], refs[len(pieces) : -1], refs[-1]
    at = 0
    for ref, (start, count) in zip(rows_in, pieces):
        rhs[pl.ds(at, count), :] = ref[pl.ds(start, count), :]
        at += count
    low = is_low((tile, LANES))
    group = min(4, chips)

    def step(i, carry):
        at = pl.ds(pl.multiple_of(i * tile, tile), tile)
        for first in range(0, chips, group):
            right = rhs[pl.ds(first * WIDTH, group * WIDTH), :]
            own = lax.dot_general(own_ref[at, :], right, NT, preferred_element_type=jnp.float32)
            sib = lax.dot_general(sib_ref[at, :], right, NT, preferred_element_type=jnp.float32)
            for k in range(0, group, 2):
                u = own[:, k * WIDTH : k * WIDTH + LANES]
                v = sib[:, k * WIDTH : k * WIDTH + LANES]
                encode(jnp.where(low, u, turn(v)), outs[first + k].at[i])
                encode(jnp.where(low, turn(u), v), outs[first + k + 1].at[i])
        return carry

    lax.fori_loop(0, own_ref.shape[0] // tile, step, 0)


def early_ladder_kernel(chips, tile, vir, pieces, place_ref, own_ref, sib_ref, *refs):
    rows_in, (parts, away, rhs, work, sent) = refs[: len(pieces)], refs[len(pieces) :]
    chip, z = place_ref[0], place_ref[2]
    at = 0
    for ref, (start, count) in zip(rows_in, pieces):
        rhs[pl.ds(at, count), :] = ref[pl.ds(start, count), :]
        at += count
    low = is_low((tile, LANES))
    block = vir // chips
    group = own_ref.shape[0] // chips

    def step(i, carry):
        at = pl.ds(pl.multiple_of(i * tile, tile), tile)
        own = lax.dot_general(own_ref[at, :], rhs[...], NT, preferred_element_type=jnp.float32)
        sib = lax.dot_general(sib_ref[at, :], rhs[...], NT, preferred_element_type=jnp.float32)
        for d in range(0, chips, 2):
            u = own[:, d * WIDTH : d * WIDTH + LANES]
            v = sib[:, d * WIDTH : d * WIDTH + LANES]
            work[d] = jnp.where(low, u, turn(v))
            work[d + 1] = jnp.where(low, turn(u), v)
        for e in range(chips):
            column = (chip ^ z ^ e) * block
            out = sent if e % 2 else parts
            for k in range(tile // vir):
                source = pl.ds(pl.multiple_of(k * vir + column, 8), block)
                line = (i * (tile // vir) + k) * block
                for d in range(chips):
                    target = pl.ds(pl.multiple_of(d * group + line, 8), block)
                    out[e // 2, target, :] = work[d, source, :]
        return carry

    lax.fori_loop(0, own_ref.shape[0] // tile, step, 0)
    for i in range(chips // 2):
        for d in range(chips):
            encode(sent[i, pl.ds(d * group, group), :], away.at[i, d])


def sum_kernel(places, count, parts, *refs):
    got, outs = refs[:count], refs[count:]
    group = outs[0].shape[0] - TAIL
    for d, out in enumerate(outs):
        total = parts[0, pl.ds(d * group, group), :]
        for k, slot in places:
            total = total + decode(got[k].at[slot, d])
        encode(total, out)


def early_antisym_kernel(chips, side, place_ref, *refs):
    arrived, own, outs = refs[:chips], refs[chips], refs[chips + 1 : 2 * chips]
    cube, sent = refs[2 * chips :]
    chip, core, z = place_ref[0], place_ref[1], place_ref[2]
    group = own.shape[0]
    size, held = CORES * group, side // CORES
    low = is_low((group, LANES))
    for d in range(chips):
        values = decode(arrived[d])
        turned = turn(values)
        at_own = pl.multiple_of(d * size + core * group, group)
        at_sib = pl.multiple_of(d * size + (1 - core) * group, group)
        cube[pl.ds(at_own, group), :] = jnp.where(low, values, turned)
        cube[pl.ds(at_sib, group), :] = jnp.where(low, turned, values)
    low = is_low((side, LANES))
    for e in range(chips):
        this = (e ^ z ^ chip) * size
        that = (e ^ chip) * size
        out = sent if e else own
        for a in range(held):
            b = a + held
            here = cube[pl.ds(pl.multiple_of(this + a * side, 8), side), :]
            other = cube[pl.ds(pl.multiple_of(this + b * side, 8), side), :]
            lower = here - cube[pl.ds(that + a, side, stride=side), :]
            upper = other - cube[pl.ds(that + b, side, stride=side), :]
            out[pl.ds(a * side, side), :] = jnp.where(low, lower, upper)
        if e:
            encode(sent[...], outs[e - 1])


def early_finish_kernel(chips, side, pair_ref, vir_ref, own, *refs):
    got, (out_ref, cube) = refs[: chips - 1], refs[-2:]
    group, rows = own.shape[0], cube.shape[0]
    for e in range(chips):
        values = decode(got[e - 1]) if e else own[...]
        for a in range(group // side):
            target = pl.ds((a * chips + e) * side, side)
            cube[target, :] = values[a * side : (a + 1) * side]
    virt = jnp.where(is_low(cube.shape), vir_ref[:, 0:1], vir_ref[:, 1:2])
    update = (cube[...] / (pair_ref[0] - virt)).T
    out_ref[:, pl.ds(0, rows)] = update[:WIDTH]
    out_ref[:, pl.ds(rows, rows)] = update[WIDTH:]


def antisym_kernel(chips, slabs, vir, place_ref, *refs):
    arrived, (parts, *away, cube, sent) = refs[:chips], refs[chips:]
    chip, core, z = place_ref[0], place_ref[1], place_ref[2]
    tiles, tile = arrived[0].shape[0], arrived[0].shape[1] - TAIL
    rows = tiles * tile
    low = is_low((tile, LANES))
    for d in range(chips):
        base = (chip ^ d) * (CORES * rows)
        for t in range(tiles):
            values = decode(arrived[d].at[t])
            turned = turn(values)
            at_own = pl.multiple_of(base + core * rows + t * tile, tile)
            at_sib = pl.multiple_of(base + (1 - core) * rows + t * tile, tile)
            cube[pl.ds(at_own, tile), :] = jnp.where(low, values, turned)
            cube[pl.ds(at_sib, tile), :] = jnp.where(low, turned, values)

    half = vir // slabs // 2
    low = is_low((vir, LANES))
    part_tile = away[0].shape[2] - TAIL

    def into(slab, out):
        def body(k, carry):
            a = slab * (2 * half) + k
            b = a + half
            here = cube[pl.ds(pl.multiple_of(a * vir, vir), vir), :]
            other = cube[pl.ds(pl.multiple_of(b * vir, vir), vir), :]
            lower = here - cube[pl.ds(a, vir, stride=vir), :]
            upper = other - cube[pl.ds(b, vir, stride=vir), :]
            out[pl.ds(pl.multiple_of(k * vir, vir), vir), :] = jnp.where(low, lower, upper)
            return carry

        lax.fori_loop(0, half, body, 0)

    for e in reversed(range(1, slabs, 2)):
        into(e ^ z, sent)
        out = away[e // 2].at[0] if len(away) > 1 else away[0].at[e // 2]
        for t in range(out.shape[0]):
            encode(sent[pl.ds(t * part_tile, part_tile), :], out.at[t])
    for e in range(0, slabs, 2):
        into(e ^ z, parts.at[e // 2])


def hop_kernel(slots, parts, *refs):
    got, out = refs[:-1], refs[-1]
    tiles, tile = out.shape[1], out.shape[2] - TAIL
    for i, (part, places) in enumerate(slots):
        for t in range(tiles):
            total = parts[part, pl.ds(t * tile, tile), :]
            for k, slot in places:
                total = total + decode(got[k].at[slot, t])
            encode(total, out.at[i, t])


def finish_kernel(places, count, pair_ref, vir_ref, parts, *refs):
    got, out_ref = refs[:count], refs[-1]
    tiles, tile = got[0].shape[1], got[0].shape[2] - TAIL
    low = is_low((tile, LANES))
    pair = pair_ref[0]
    half = tiles * tile
    for t in range(tiles):
        at = pl.ds(t * tile, tile)
        total = parts[0, at, :]
        for k, slot in places:
            total = total + decode(got[k].at[slot, t])
        virt = jnp.where(low, vir_ref[at, 0:1], vir_ref[at, 1:2])
        update = (total / (pair - virt)).T
        out_ref[:, pl.ds(t * tile, tile)] = update[:WIDTH]
        out_ref[:, pl.ds(half + t * tile, tile)] = update[WIDTH:]


def on_device(mesh, amplitudes, integrals, pair_index, eps_occ, eps_vir):
    devices, slabs = mesh.shape["pair"], mesh.shape["slab"]
    chips = devices // CORES
    num_pairs, depth = amplitudes.shape
    rows = integrals.shape[1]
    vir = eps_vir.shape[0]
    chunks = num_pairs // WIDTH
    half = vir // slabs // 2
    part_rows = half * vir
    tile, part_tile = tile_of(rows, 384), tile_of(part_rows, 384)
    tiles, part_tiles = rows // tile, part_rows // part_tile
    me, z = lax.axis_index("pair"), lax.axis_index("slab")
    chip, core = me // CORES, me % CORES

    def to_chip(x, d):
        return lax.ppermute(x, "pair", [(i, i ^ (d * CORES)) for i in range(devices)])

    def limit(mib):
        return pltpu.CompilerParams(vmem_limit_bytes=mib * 1024 * 1024)

    def cost(flops, moved):
        return pl.CostEstimate(flops=flops, bytes_accessed=moved, transcendentals=0)

    smem = pl.BlockSpec(memory_space=pltpu.SMEM)
    vmem = pl.BlockSpec(memory_space=pltpu.VMEM)
    message = jax.ShapeDtypeStruct((tiles, tile + TAIL, LANES), jnp.int16)

    def parcel(count):
        return (count, part_tiles, part_tile + TAIL, LANES)

    column = max((c for c in (384, 256, 128) if rows % c == 0), default=rows)
    transpose = pl.pallas_call(
        transpose_kernel,
        grid=(rows // column,),
        in_specs=[pl.BlockSpec((depth, column), lambda i: (0, i))],
        out_specs=vmem,
        out_shape=jax.ShapeDtypeStruct((rows, depth), jnp.bfloat16),
        compiler_params=limit(16),
        cost_estimate=cost(0, 4 * rows * depth),
        name="transpose",
    )

    def ordered(
        body, flops, inputs, in_specs, out_specs, out_shape, mib, scratch=(), name=None, **more
    ):
        given, made = len(in_specs), len(out_specs)
        moved = sum(x.size * x.dtype.itemsize for x in (*inputs, *out_shape))

        def kernel(*refs):
            token_in, token_out = refs[given], refs[given + 1 + made]
            token_out[...] = token_in[...]
            outs = refs[given + 1 : given + 1 + made]
            body(*refs[:given], *outs, *refs[given + made + 2 :])

        def call(token, *args):
            return pl.pallas_call(
                kernel,
                in_specs=[*in_specs, vmem],
                out_specs=[*out_specs, vmem],
                out_shape=[*out_shape, jax.ShapeDtypeStruct(token.shape, token.dtype)],
                scratch_shapes=scratch,
                compiler_params=limit(mib),
                cost_estimate=cost(flops, moved),
                name=name,
                **more,
            )(*args, token)

        return call, inputs

    def ladder(gathered):
        arrays, pieces = zip(*[(x, (start, count)) for x, start, count in gathered])
        return ordered(
            functools.partial(ladder_kernel, chips, tile, pieces),
            4 * rows * depth * chips * WIDTH,
            [own_t, sib_t, *arrays],
            [vmem] * (2 + len(arrays)),
            [vmem] * chips,
            [message] * chips,
            16,
            [pltpu.VMEM((chips * WIDTH, depth), jnp.bfloat16)],
            name="ladder",
        )

    early = chips == slabs and chips >= 4 and tile % vir == 0 and vir // chips % 8 == 0
    side, group = vir // chips, rows // chips
    small = jax.ShapeDtypeStruct((group + TAIL, LANES), jnp.int16)
    grouped = (chips // 2, chips * group, LANES)

    def early_ladder(gathered):
        arrays, pieces = zip(*[(x, (start, count)) for x, start, count in gathered])
        return ordered(
            functools.partial(early_ladder_kernel, chips, tile, vir, pieces),
            4 * rows * depth * chips * WIDTH,
            [place, own_t, sib_t, *arrays],
            [smem] + [vmem] * (2 + len(arrays)),
            [vmem] * 2,
            [
                jax.ShapeDtypeStruct(grouped, jnp.float32),
                jax.ShapeDtypeStruct((chips // 2, chips, *small.shape), jnp.int16),
            ],
            20,
            [
                pltpu.VMEM((chips * WIDTH, depth), jnp.bfloat16),
                pltpu.VMEM((chips, tile, LANES), jnp.float32),
                pltpu.VMEM(grouped, jnp.float32),
            ],
            name="early_ladder",
        )

    def early_sum(places, parts, got):
        return ordered(
            functools.partial(sum_kernel, places, len(got)),
            8 * chips * group * LANES,
            [parts, *got],
            [vmem] * (1 + len(got)),
            [vmem] * chips,
            [small] * chips,
            8,
            name="early_sum",
        )

    def early_antisym(arrived):
        return ordered(
            functools.partial(early_antisym_kernel, chips, side),
            8 * vir * side * LANES,
            [place, *arrived],
            [smem] + [vmem] * chips,
            [vmem] * chips,
            [jax.ShapeDtypeStruct((group, LANES), jnp.float32)] + [small] * (chips - 1),
            12,
            [
                pltpu.VMEM((chips * side * side, LANES), jnp.float32),
                pltpu.VMEM((group, LANES), jnp.float32),
            ],
            name="early_antisym",
        )

    def antisym(parcels, arrived):
        return ordered(
            functools.partial(antisym_kernel, chips, slabs, vir),
            8 * vir * vir * LANES,
            [place, *arrived],
            [smem] + [vmem] * chips,
            [vmem] * (1 + parcels),
            [jax.ShapeDtypeStruct((slabs // 2, part_rows, LANES), jnp.float32)]
            + [jax.ShapeDtypeStruct(parcel(slabs // 2 // parcels), jnp.int16)] * parcels,
            16,
            [
                pltpu.VMEM((vir * vir, LANES), jnp.float32),
                pltpu.VMEM((part_rows, LANES), jnp.float32),
            ],
            name="antisym",
        )

    def hop(slots, parts, got):
        return ordered(
            functools.partial(hop_kernel, slots),
            8 * parts.size,
            [parts, *got],
            [vmem] * (1 + len(got)),
            [vmem],
            [jax.ShapeDtypeStruct((len(slots), *got[0].shape[1:]), jnp.int16)],
            8,
            name="hop",
        )

    def finish(r, parts, got, places, so_far):
        given = [] if so_far is None else [so_far]
        if places is None:
            body = functools.partial(early_finish_kernel, chips, side)
        else:
            body = functools.partial(finish_kernel, places, len(got))
        return ordered(
            body,
            16 * part_rows * LANES,
            [eps_pair, eps_virt, parts, *got, *given],
            [pl.BlockSpec((1, 1, LANES), lambda i: (r, 0, 0))]
            + [vmem] * (2 + len(got))
            + [pl.BlockSpec(memory_space=pl.ANY)] * len(given),
            [pl.BlockSpec((WIDTH, 2 * part_rows), lambda i: (r, 0))],
            [jax.ShapeDtypeStruct((num_pairs, 2 * part_rows), jnp.float32)],
            8,
            [] if places else [pltpu.VMEM((part_rows, LANES), jnp.float32)],
            name="finish",
            grid=(1,),
            input_output_aliases={3 + len(got): 0} if given else {},
        )

    in_hbm = functools.partial(pltpu.with_memory_space_constraint, memory_space=pltpu.HBM)
    own_t = transpose(in_hbm(integrals))
    swapped = lax.ppermute(integrals, "pair", [(i, i ^ 1) for i in range(devices)])
    sib_t = transpose(swapped)

    occ_ids = jnp.arange(eps_occ.shape[0], dtype=jnp.int32)

    def pick(ids):
        return jnp.sum(jnp.where(ids[:, None] == occ_ids[None, :], eps_occ[None, :], 0.0), axis=1)

    eps_pair = (pick(pair_index[:, 0]) + pick(pair_index[:, 1])).reshape(chunks, 1, WIDTH)
    eps_pair = jnp.concatenate([eps_pair, eps_pair], axis=2)
    eps_mine = lax.dynamic_slice(eps_vir.reshape(slabs, 2, half), (z, 0, 0), (1, 2, half))[0]
    eps_virt = (eps_mine[:, :, None] + eps_vir[None, None, :]).reshape(2, part_rows).T

    place = jnp.stack([chip, core, z]).astype(jnp.int32)

    def gather(mine, beside):
        count = mine.shape[0]
        if chips != 4:
            return [[mine]] + [[to_chip(mine, d)] for d in range(1, chips)], beside
        one, two = to_chip(mine, 1), to_chip(mine, 2)
        if beside:
            one, two, *beside = lax.optimization_barrier((one, two, *beside))
        low, high = to_chip(two[: count // 2], 1), to_chip(one[count // 2 :], 2)
        return [[mine], [one], [two], [low, high]], beside

    if early:
        head, (eps_pair, eps_virt) = gather(amplitudes[:WIDTH], (eps_pair, eps_virt))
        (head, own_t, sib_t, rest) = lax.optimization_barrier((head, own_t, sib_t, amplitudes[WIDTH:]))
        tail, _ = gather(rest, ())
        gathered = [(0, head), (WIDTH, tail)]
    else:
        tail, (own_t, sib_t, eps_pair, eps_virt) = gather(
            amplitudes, (own_t, sib_t, eps_pair, eps_virt)
        )
        gathered = [(0, tail)]

    def rows_of(r):
        found = []
        for d in range(chips):
            for base, parts in gathered:
                at = base
                for x in parts[d]:
                    begin = max(r * WIDTH, at)
                    end = min((r + 1) * WIDTH, at + x.shape[0])
                    if begin < end:
                        found.append((x, begin - at, end - begin))
                    at += x.shape[0]
        return found

    def across(x, level):
        return lax.ppermute(x, "slab", [(i, i ^ level) for i in range(slabs)])

    def halved(parts, away):
        each = slabs // 2 // len(away)
        held = {e: [(away[e // 2 // each], e // 2 % each)] for e in range(0, slabs, 2)}

        def listed(wanted):
            arrays = []
            for e in wanted:
                arrays += [x for x, _ in held[e] if not any(x is y for y in arrays)]
            index = {id(x): k for k, x in enumerate(arrays)}
            return arrays, [(e // 2, [(index[id(x)], i) for x, i in held[e]]) for e in wanted]

        level = 2
        while level < slabs:
            leave = [e for e in held if e & level]
            got, slots = listed(leave)
            (out,) = yield hop(slots, parts, got)
            out = across(out, level)
            for i, e in enumerate(leave):
                held[e ^ level].append((out, i))
                del held[e]
            level *= 2
        got, ((_, places),) = listed([0])
        return got, places

    def early_stages(r):
        parts, away = yield early_ladder(rows_of(r))
        got, places = yield from halved(parts, [across(away, 1)])
        sums = yield early_sum(places, parts, got)
        arrived = [sums[0]] + [to_chip(sums[d], d) for d in range(1, chips)]
        own, *blocks = yield early_antisym(arrived)
        got = [across(x, e + 1) for e, x in enumerate(blocks)]
        yield finish(r, own, got, None, update)

    def stages(r):
        sums = yield ladder(rows_of(r))
        if turns:
            sums, _ = lax.optimization_barrier((sums, turns[-1] + results[-1][:1]))
        arrived = [to_chip(sums[d], d) for d in range(1, chips)]
        turns.append(arrived)
        parcels = slabs // 2 if r == chunks - 1 else 1
        parts, *away = yield antisym(parcels, [sums[0], *arrived])
        if parcels > 1 and firsts:
            away, _ = lax.optimization_barrier((away, firsts[-1]))
        away = [across(x, 1) for x in reversed(away)][::-1]
        firsts.append(away)
        got, places = yield from halved(parts, away)
        yield finish(r, parts, got, places, update)

    hops = max(0, (slabs - 1).bit_length() - 1)

    def when(stage):
        r, k = stage
        if early and r == 0:
            return (20, *[46] * hops, 54, 66, 83)[k]
        if k == 0:
            return 37 + 5 * r if early else 30 + 5 * r
        return 15 * r + (45 if early else 54) + (k - 1) * 17 - (1 if k == 2 + hops else 0)

    order = [(r, k) for r in range(chunks) for k in range(3 + hops + (early and r == 0))]
    order = sorted(order, key=when)

    turns, firsts = [], []
    running = [early_stages(r) if early and r == 0 else stages(r) for r in range(chunks)]
    results = [None] * chunks
    update, token = None, jnp.zeros((8, LANES), jnp.float32)
    for r, k in order:
        call, inputs = running[r].send(results[r])
        *results[r], token = call(token, *inputs)
        if results[r][0].shape == (num_pairs, 2 * part_rows):
            update = results[r][0]
    return update


def solution(mesh):
    in_specs = (P("pair", "slab"), P("slab", "pair"), P("pair", None), P(), P())
    out_specs = P("pair", "slab")
    return jax.shard_map(
        functools.partial(on_device, mesh),
        mesh=mesh,
        in_specs=in_specs,
        out_specs=out_specs,
        check_vma=False,
    )
```

```python
import functools

import jax
import jax.numpy as jnp
from jax import lax
from jax.experimental import pallas as pl
from jax.experimental.pallas import tpu as pltpu
from jax.sharding import PartitionSpec as P

CORES = 2
WIDTH = 64
LANES = 2 * WIDTH
TAIL = 16
NT = (((1,), (1,)), ((), ()))


def tile_of(rows, most):
    return max(t for t in range(16, most + 1, 16) if rows % t == 0)


def is_low(shape):
    return lax.broadcasted_iota(jnp.int32, shape, len(shape) - 1) < WIDTH


def turn(values):
    return pltpu.roll(values, WIDTH, 1)


def encode(values, out_ref):
    tile = values.shape[0]
    peak = jnp.max(jnp.abs(values), axis=0, keepdims=True)
    power = jnp.ceil(jnp.log2(jnp.maximum(peak, 1e-30) * (1.0 / 32760.0)))
    codes = jnp.round(values * jnp.exp2(-power)).astype(jnp.int32)
    out_ref[pl.ds(0, tile), :] = codes.astype(jnp.int16)
    wide = jnp.broadcast_to(power.astype(jnp.int32), (TAIL, LANES))
    out_ref[pl.ds(tile, TAIL), :] = wide.astype(jnp.int16)


def decode(ref):
    tile = ref.shape[0] - TAIL
    power = ref[pl.ds(tile, TAIL), :].astype(jnp.int32).astype(jnp.float32)[0:1, :]
    return ref[pl.ds(0, tile), :].astype(jnp.int32).astype(jnp.float32) * jnp.exp2(power)


def transpose_kernel(in_ref, out_ref):
    width = in_ref.shape[1]
    at = pl.ds(pl.multiple_of(pl.program_id(0) * width, width), width)
    out_ref[at, :] = in_ref[...].T


def ladder_kernel(chips, tile, pieces, own_ref, sib_ref, *refs):
    rows_in, outs, rhs = refs[: len(pieces)], refs[len(pieces) : -1], refs[-1]
    at = 0
    for ref, (start, count) in zip(rows_in, pieces):
        rhs[pl.ds(at, count), :] = ref[pl.ds(start, count), :]
        at += count
    low = is_low((tile, LANES))
    group = min(4, chips)

    def step(i, carry):
        at = pl.ds(pl.multiple_of(i * tile, tile), tile)
        for first in range(0, chips, group):
            right = rhs[pl.ds(first * WIDTH, group * WIDTH), :]
            own = lax.dot_general(own_ref[at, :], right, NT, preferred_element_type=jnp.float32)
            sib = lax.dot_general(sib_ref[at, :], right, NT, preferred_element_type=jnp.float32)
            for k in range(0, group, 2):
                u = own[:, k * WIDTH : k * WIDTH + LANES]
                v = sib[:, k * WIDTH : k * WIDTH + LANES]
                encode(jnp.where(low, u, turn(v)), outs[first + k].at[i])
                encode(jnp.where(low, turn(u), v), outs[first + k + 1].at[i])
        return carry

    lax.fori_loop(0, own_ref.shape[0] // tile, step, 0)


def early_ladder_kernel(chips, tile, vir, pieces, place_ref, own_ref, sib_ref, *refs):
    rows_in, (parts, away, rhs, work, sent) = refs[: len(pieces)], refs[len(pieces) :]
    chip, z = place_ref[0], place_ref[2]
    at = 0
    for ref, (start, count) in zip(rows_in, pieces):
        rhs[pl.ds(at, count), :] = ref[pl.ds(start, count), :]
        at += count
    low = is_low((tile, LANES))
    block = vir // chips
    group = own_ref.shape[0] // chips

    def step(i, carry):
        at = pl.ds(pl.multiple_of(i * tile, tile), tile)
        own = lax.dot_general(own_ref[at, :], rhs[...], NT, preferred_element_type=jnp.float32)
        sib = lax.dot_general(sib_ref[at, :], rhs[...], NT, preferred_element_type=jnp.float32)
        for d in range(0, chips, 2):
            u = own[:, d * WIDTH : d * WIDTH + LANES]
            v = sib[:, d * WIDTH : d * WIDTH + LANES]
            work[d] = jnp.where(low, u, turn(v))
            work[d + 1] = jnp.where(low, turn(u), v)
        for e in range(chips):
            column = (chip ^ z ^ e) * block
            out = sent if e % 2 else parts
            for k in range(tile // vir):
                source = pl.ds(pl.multiple_of(k * vir + column, 8), block)
                line = (i * (tile // vir) + k) * block
                for d in range(chips):
                    target = pl.ds(pl.multiple_of(d * group + line, 8), block)
                    out[e // 2, target, :] = work[d, source, :]
        return carry

    lax.fori_loop(0, own_ref.shape[0] // tile, step, 0)
    for i in range(chips // 2):
        for d in range(chips):
            encode(sent[i, pl.ds(d * group, group), :], away.at[i, d])


def sum_kernel(places, count, parts, *refs):
    got, (own, pair, single) = refs[:count], refs[count:]
    group = own.shape[0] - TAIL
    for d, out in enumerate((own, pair.at[0], single.at[0], pair.at[1])):
        total = parts[0, pl.ds(d * group, group), :]
        for k, slot in places:
            total = total + decode(got[k].at[slot, d])
        encode(total, out)


def early_antisym_kernel(chips, side, place_ref, *refs):
    mine, pair_in, single_in, own, pair, single, cube, sent = refs
    arrived = (mine, pair_in.at[0], single_in.at[0], single_in.at[1])
    outs = (None, pair.at[0], single.at[0], pair.at[1])
    chip, core, z = place_ref[0], place_ref[1], place_ref[2]
    group = own.shape[0]
    size, held = CORES * group, side // CORES
    low = is_low((group, LANES))
    for d in range(chips):
        values = decode(arrived[d])
        turned = turn(values)
        at_own = pl.multiple_of(d * size + core * group, group)
        at_sib = pl.multiple_of(d * size + (1 - core) * group, group)
        cube[pl.ds(at_own, group), :] = jnp.where(low, values, turned)
        cube[pl.ds(at_sib, group), :] = jnp.where(low, turned, values)
    low = is_low((side, LANES))
    for e in range(chips):
        this = (e ^ z ^ chip) * size
        that = (e ^ chip) * size
        out = sent if e else own
        for a in range(held):
            b = a + held
            here = cube[pl.ds(pl.multiple_of(this + a * side, 8), side), :]
            other = cube[pl.ds(pl.multiple_of(this + b * side, 8), side), :]
            lower = here - cube[pl.ds(that + a, side, stride=side), :]
            upper = other - cube[pl.ds(that + b, side, stride=side), :]
            out[pl.ds(a * side, side), :] = jnp.where(low, lower, upper)
        if e:
            encode(sent[...], outs[e])


def early_finish_kernel(chips, side, pair_ref, vir_ref, own, pair, single, *refs):
    got, (out_ref, cube) = (pair.at[0], single.at[0], single.at[1]), refs[-2:]
    group, rows = own.shape[0], cube.shape[0]
    for e in range(chips):
        values = decode(got[e - 1]) if e else own[...]
        for a in range(group // side):
            target = pl.ds((a * chips + e) * side, side)
            cube[target, :] = values[a * side : (a + 1) * side]
    virt = jnp.where(is_low(cube.shape), vir_ref[:, 0:1], vir_ref[:, 1:2])
    update = (cube[...] / (pair_ref[0] - virt)).T
    out_ref[:, pl.ds(0, rows)] = update[:WIDTH]
    out_ref[:, pl.ds(rows, rows)] = update[WIDTH:]


def antisym_kernel(chips, slabs, vir, place_ref, *refs):
    arrived, (parts, *away, cube, sent) = refs[:chips], refs[chips:]
    chip, core, z = place_ref[0], place_ref[1], place_ref[2]
    tiles, tile = arrived[0].shape[0], arrived[0].shape[1] - TAIL
    rows = tiles * tile
    low = is_low((tile, LANES))
    for d in range(chips):
        base = (chip ^ d) * (CORES * rows)
        for t in range(tiles):
            values = decode(arrived[d].at[t])
            turned = turn(values)
            at_own = pl.multiple_of(base + core * rows + t * tile, tile)
            at_sib = pl.multiple_of(base + (1 - core) * rows + t * tile, tile)
            cube[pl.ds(at_own, tile), :] = jnp.where(low, values, turned)
            cube[pl.ds(at_sib, tile), :] = jnp.where(low, turned, values)

    half = vir // slabs // 2
    low = is_low((vir, LANES))
    part_tile = away[0].shape[2] - TAIL

    def into(slab, out):
        def body(k, carry):
            a = slab * (2 * half) + k
            b = a + half
            here = cube[pl.ds(pl.multiple_of(a * vir, vir), vir), :]
            other = cube[pl.ds(pl.multiple_of(b * vir, vir), vir), :]
            lower = here - cube[pl.ds(a, vir, stride=vir), :]
            upper = other - cube[pl.ds(b, vir, stride=vir), :]
            out[pl.ds(pl.multiple_of(k * vir, vir), vir), :] = jnp.where(low, lower, upper)
            return carry

        lax.fori_loop(0, half, body, 0)

    for e in reversed(range(1, slabs, 2)):
        into(e ^ z, sent)
        out = away[e // 2].at[0] if len(away) > 1 else away[0].at[e // 2]
        for t in range(out.shape[0]):
            encode(sent[pl.ds(t * part_tile, part_tile), :], out.at[t])
    for e in range(0, slabs, 2):
        into(e ^ z, parts.at[e // 2])


def hop_kernel(slots, parts, *refs):
    got, out = refs[:-1], refs[-1]
    tiles, tile = out.shape[1], out.shape[2] - TAIL
    for i, (part, places) in enumerate(slots):
        for t in range(tiles):
            total = parts[part, pl.ds(t * tile, tile), :]
            for k, slot in places:
                total = total + decode(got[k].at[slot, t])
            encode(total, out.at[i, t])


def finish_kernel(places, count, pair_ref, vir_ref, parts, *refs):
    got, out_ref = refs[:count], refs[-1]
    tiles, tile = got[0].shape[1], got[0].shape[2] - TAIL
    low = is_low((tile, LANES))
    pair = pair_ref[0]
    half = tiles * tile
    for t in range(tiles):
        at = pl.ds(t * tile, tile)
        total = parts[0, at, :]
        for k, slot in places:
            total = total + decode(got[k].at[slot, t])
        virt = jnp.where(low, vir_ref[at, 0:1], vir_ref[at, 1:2])
        update = (total / (pair - virt)).T
        out_ref[:, pl.ds(t * tile, tile)] = update[:WIDTH]
        out_ref[:, pl.ds(half + t * tile, tile)] = update[WIDTH:]


def on_device(mesh, amplitudes, integrals, pair_index, eps_occ, eps_vir):
    devices, slabs = mesh.shape["pair"], mesh.shape["slab"]
    chips = devices // CORES
    num_pairs, depth = amplitudes.shape
    rows = integrals.shape[1]
    vir = eps_vir.shape[0]
    chunks = num_pairs // WIDTH
    half = vir // slabs // 2
    part_rows = half * vir
    tile, part_tile = tile_of(rows, 384), tile_of(part_rows, 384)
    tiles, part_tiles = rows // tile, part_rows // part_tile
    me, z = lax.axis_index("pair"), lax.axis_index("slab")
    chip, core = me // CORES, me % CORES

    def to_chip(x, d):
        return lax.ppermute(x, "pair", [(i, i ^ (d * CORES)) for i in range(devices)])

    def limit(mib):
        return pltpu.CompilerParams(vmem_limit_bytes=mib * 1024 * 1024)

    def cost(flops, moved):
        return pl.CostEstimate(flops=flops, bytes_accessed=moved, transcendentals=0)

    smem = pl.BlockSpec(memory_space=pltpu.SMEM)
    vmem = pl.BlockSpec(memory_space=pltpu.VMEM)
    message = jax.ShapeDtypeStruct((tiles, tile + TAIL, LANES), jnp.int16)

    def parcel(count):
        return (count, part_tiles, part_tile + TAIL, LANES)

    column = max((c for c in (384, 256, 128) if rows % c == 0), default=rows)
    transpose = pl.pallas_call(
        transpose_kernel,
        grid=(rows // column,),
        in_specs=[pl.BlockSpec((depth, column), lambda i: (0, i))],
        out_specs=vmem,
        out_shape=jax.ShapeDtypeStruct((rows, depth), jnp.bfloat16),
        compiler_params=limit(16),
        cost_estimate=cost(0, 4 * rows * depth),
        name="transpose",
    )

    def ordered(
        body, flops, inputs, in_specs, out_specs, out_shape, mib, scratch=(), name=None, **more
    ):
        given, made = len(in_specs), len(out_specs)
        moved = sum(x.size * x.dtype.itemsize for x in (*inputs, *out_shape))

        def kernel(*refs):
            token_in, token_out = refs[given], refs[given + 1 + made]
            token_out[...] = token_in[...]
            outs = refs[given + 1 : given + 1 + made]
            body(*refs[:given], *outs, *refs[given + made + 2 :])

        def call(token, *args):
            return pl.pallas_call(
                kernel,
                in_specs=[*in_specs, vmem],
                out_specs=[*out_specs, vmem],
                out_shape=[*out_shape, jax.ShapeDtypeStruct(token.shape, token.dtype)],
                scratch_shapes=scratch,
                compiler_params=limit(mib),
                cost_estimate=cost(flops, moved),
                name=name,
                **more,
            )(*args, token)

        return call, inputs

    def ladder(gathered):
        arrays, pieces = zip(*[(x, (start, count)) for x, start, count in gathered])
        return ordered(
            functools.partial(ladder_kernel, chips, tile, pieces),
            4 * rows * depth * chips * WIDTH,
            [own_t, sib_t, *arrays],
            [vmem] * (2 + len(arrays)),
            [vmem] * chips,
            [message] * chips,
            16,
            [pltpu.VMEM((chips * WIDTH, depth), jnp.bfloat16)],
            name="ladder",
        )

    early = chips == slabs == 4 and tile % vir == 0 and vir // chips % 8 == 0
    side, group = vir // chips, rows // chips
    small, single, pair = (
        jax.ShapeDtypeStruct((*lead, group + TAIL, LANES), jnp.int16) for lead in ((), (1,), (2,))
    )
    grouped = (chips // 2, chips * group, LANES)

    def early_ladder(gathered):
        arrays, pieces = zip(*[(x, (start, count)) for x, start, count in gathered])
        return ordered(
            functools.partial(early_ladder_kernel, chips, tile, vir, pieces),
            4 * rows * depth * chips * WIDTH,
            [place, own_t, sib_t, *arrays],
            [smem] + [vmem] * (2 + len(arrays)),
            [vmem] * 2,
            [
                jax.ShapeDtypeStruct(grouped, jnp.float32),
                jax.ShapeDtypeStruct((chips // 2, chips, *small.shape), jnp.int16),
            ],
            20,
            [
                pltpu.VMEM((chips * WIDTH, depth), jnp.bfloat16),
                pltpu.VMEM((chips, tile, LANES), jnp.float32),
                pltpu.VMEM(grouped, jnp.float32),
            ],
            name="early_ladder",
        )

    def early_sum(places, parts, got):
        return ordered(
            functools.partial(sum_kernel, places, len(got)),
            8 * chips * group * LANES,
            [parts, *got],
            [vmem] * (1 + len(got)),
            [vmem] * 3,
            [small, pair, single],
            8,
            name="early_sum",
        )

    def early_antisym(arrived):
        return ordered(
            functools.partial(early_antisym_kernel, chips, side),
            8 * vir * side * LANES,
            [place, *arrived],
            [smem] + [vmem] * 3,
            [vmem] * 3,
            [jax.ShapeDtypeStruct((group, LANES), jnp.float32), pair, single],
            12,
            [
                pltpu.VMEM((chips * side * side, LANES), jnp.float32),
                pltpu.VMEM((group, LANES), jnp.float32),
            ],
            name="early_antisym",
        )

    def antisym(parcels, arrived):
        return ordered(
            functools.partial(antisym_kernel, chips, slabs, vir),
            8 * vir * vir * LANES,
            [place, *arrived],
            [smem] + [vmem] * chips,
            [vmem] * (1 + parcels),
            [jax.ShapeDtypeStruct((slabs // 2, part_rows, LANES), jnp.float32)]
            + [jax.ShapeDtypeStruct(parcel(slabs // 2 // parcels), jnp.int16)] * parcels,
            16,
            [
                pltpu.VMEM((vir * vir, LANES), jnp.float32),
                pltpu.VMEM((part_rows, LANES), jnp.float32),
            ],
            name="antisym",
        )

    def hop(slots, parts, got):
        return ordered(
            functools.partial(hop_kernel, slots),
            8 * parts.size,
            [parts, *got],
            [vmem] * (1 + len(got)),
            [vmem],
            [jax.ShapeDtypeStruct((len(slots), *got[0].shape[1:]), jnp.int16)],
            8,
            name="hop",
        )

    def finish(r, parts, got, places, so_far):
        given = [] if so_far is None else [so_far]
        if places is None:
            body = functools.partial(early_finish_kernel, chips, side)
        else:
            body = functools.partial(finish_kernel, places, len(got))
        return ordered(
            body,
            16 * part_rows * LANES,
            [eps_pair, eps_virt, parts, *got, *given],
            [pl.BlockSpec((1, 1, LANES), lambda i: (r, 0, 0))]
            + [vmem] * (2 + len(got))
            + [pl.BlockSpec(memory_space=pl.ANY)] * len(given),
            [pl.BlockSpec((WIDTH, 2 * part_rows), lambda i: (r, 0))],
            [jax.ShapeDtypeStruct((num_pairs, 2 * part_rows), jnp.float32)],
            8,
            [] if places else [pltpu.VMEM((part_rows, LANES), jnp.float32)],
            name="finish",
            grid=(1,),
            input_output_aliases={3 + len(got): 0} if given else {},
        )

    in_hbm = functools.partial(pltpu.with_memory_space_constraint, memory_space=pltpu.HBM)
    own_t = transpose(in_hbm(integrals))
    swapped = lax.ppermute(integrals, "pair", [(i, i ^ 1) for i in range(devices)])
    sib_t = transpose(swapped)

    occ_ids = jnp.arange(eps_occ.shape[0], dtype=jnp.int32)

    def pick(ids):
        return jnp.sum(jnp.where(ids[:, None] == occ_ids[None, :], eps_occ[None, :], 0.0), axis=1)

    eps_pair = (pick(pair_index[:, 0]) + pick(pair_index[:, 1])).reshape(chunks, 1, WIDTH)
    eps_pair = jnp.concatenate([eps_pair, eps_pair], axis=2)
    eps_mine = lax.dynamic_slice(eps_vir.reshape(slabs, 2, half), (z, 0, 0), (1, 2, half))[0]
    eps_virt = (eps_mine[:, :, None] + eps_vir[None, None, :]).reshape(2, part_rows).T

    place = jnp.stack([chip, core, z]).astype(jnp.int32)

    def gather(mine, beside):
        count = mine.shape[0]
        if chips != 4:
            return [[mine]] + [[to_chip(mine, d)] for d in range(1, chips)], beside
        one, two = to_chip(mine, 1), to_chip(mine, 2)
        if beside:
            one, two, *beside = lax.optimization_barrier((one, two, *beside))
        low, high = to_chip(two[: count // 2], 1), to_chip(one[count // 2 :], 2)
        return [[mine], [one], [two], [low, high]], beside

    if early:
        head, (own_t, eps_pair, eps_virt) = gather(
            amplitudes[:WIDTH], (own_t, eps_pair, eps_virt)
        )
        head, own_t, sib_t, rest = lax.optimization_barrier(
            (head, own_t, sib_t, amplitudes[WIDTH:])
        )
        tail, _ = gather(rest, ())
        gathered = [(0, head), (WIDTH, tail)]
    else:
        tail, (own_t, sib_t, eps_pair, eps_virt) = gather(
            amplitudes, (own_t, sib_t, eps_pair, eps_virt)
        )
        gathered = [(0, tail)]

    def rows_of(r):
        found = []
        for d in range(chips):
            for base, parts in gathered:
                at = base
                for x in parts[d]:
                    begin = max(r * WIDTH, at)
                    end = min((r + 1) * WIDTH, at + x.shape[0])
                    if begin < end:
                        found.append((x, begin - at, end - begin))
                    at += x.shape[0]
        return found

    def across(x, level):
        return lax.ppermute(x, "slab", [(i, i ^ level) for i in range(slabs)])

    def halved(parts, away):
        each = slabs // 2 // len(away)
        held = {e: [(away[e // 2 // each], e // 2 % each)] for e in range(0, slabs, 2)}

        def listed(wanted):
            arrays = []
            for e in wanted:
                arrays += [x for x, _ in held[e] if not any(x is y for y in arrays)]
            index = {id(x): k for k, x in enumerate(arrays)}
            return arrays, [(e // 2, [(index[id(x)], i) for x, i in held[e]]) for e in wanted]

        level = 2
        while level < slabs:
            leave = [e for e in held if e & level]
            got, slots = listed(leave)
            (out,) = yield hop(slots, parts, got)
            out = across(out, level)
            for i, e in enumerate(leave):
                held[e ^ level].append((out, i))
                del held[e]
            level *= 2
        got, ((_, places),) = listed([0])
        return got, places

    def by_steps(move, pair, single):
        first = move(pair, 1)
        return [first, move(jnp.concatenate([single, first[1:]]), 2)]

    def early_stages(r):
        parts, away = yield early_ladder(rows_of(r))
        got, places = yield from halved(parts, [across(away, 1)])
        mine, *sums = yield early_sum(places, parts, got)
        arrived = by_steps(to_chip, *sums)
        turns.append(turns[-1] + arrived)
        own, *blocks = yield early_antisym([mine, *arrived])
        yield finish(r, own, by_steps(across, *blocks), None, update)

    def stages(r):
        sums = yield ladder(rows_of(r))
        if turns:
            sums, _ = lax.optimization_barrier((sums, turns[-1] + results[-1][:1]))
        arrived = [to_chip(sums[d], d) for d in range(1, chips)]
        turns.append(arrived)
        parcels = slabs // 2 if r == chunks - 1 else 1
        parts, *away = yield antisym(parcels, [sums[0], *arrived])
        if parcels > 1 and firsts:
            away, _ = lax.optimization_barrier((away, firsts[-1]))
        away = [across(x, 1) for x in reversed(away)][::-1]
        firsts.append(away)
        got, places = yield from halved(parts, away)
        yield finish(r, parts, got, places, update)

    hops = max(0, (slabs - 1).bit_length() - 1)

    def when(stage):
        r, k = stage
        if early and r == 0:
            return (20, *[41] * hops, 54, 66, 83)[k]
        if k == 0:
            return 37 + 5 * r if early else 30 + 5 * r
        return 15 * r + (45 if early else 54) + (k - 1) * 17 - (1 if k == 2 + hops else 0)

    order = [(r, k) for r in range(chunks) for k in range(3 + hops + (early and r == 0))]
    order = sorted(order, key=when)

    turns, firsts = [], []
    running = [early_stages(r) if early and r == 0 else stages(r) for r in range(chunks)]
    results = [None] * chunks
    update, token = None, jnp.zeros((8, LANES), jnp.float32)
    for r, k in order:
        call, inputs = running[r].send(results[r])
        *results[r], token = call(token, *inputs)
        if results[r][0].shape == (num_pairs, 2 * part_rows):
            update = results[r][0]
    return update


def solution(mesh):
    in_specs = (P("pair", "slab"), P("slab", "pair"), P("pair", None), P(), P())
    out_specs = P("pair", "slab")
    return jax.shard_map(
        functools.partial(on_device, mesh),
        mesh=mesh,
        in_specs=in_specs,
        out_specs=out_specs,
        check_vma=False,
    )
```

```python
import functools

import jax
import jax.numpy as jnp
from jax import lax
from jax.experimental import pallas as pl
from jax.experimental.pallas import tpu as pltpu
from jax.sharding import PartitionSpec as P

CORES = 2
WIDTH = 64
LANES = 2 * WIDTH
TAIL = 16
NT = (((1,), (1,)), ((), ()))


def tile_of(rows, most):
    return max(t for t in range(16, most + 1, 16) if rows % t == 0)


def is_low(shape):
    return lax.broadcasted_iota(jnp.int32, shape, len(shape) - 1) < WIDTH


def turn(values):
    return pltpu.roll(values, WIDTH, 1)


def encode(values, out_ref):
    tile = values.shape[0]
    peak = jnp.max(jnp.abs(values), axis=0, keepdims=True)
    power = jnp.ceil(jnp.log2(jnp.maximum(peak, 1e-30) * (1.0 / 32760.0)))
    codes = jnp.round(values * jnp.exp2(-power)).astype(jnp.int32)
    out_ref[pl.ds(0, tile), :] = codes.astype(jnp.int16)
    wide = jnp.broadcast_to(power.astype(jnp.int32), (TAIL, LANES))
    out_ref[pl.ds(tile, TAIL), :] = wide.astype(jnp.int16)


def decode(ref):
    tile = ref.shape[0] - TAIL
    power = ref[pl.ds(tile, TAIL), :].astype(jnp.int32).astype(jnp.float32)[0:1, :]
    return ref[pl.ds(0, tile), :].astype(jnp.int32).astype(jnp.float32) * jnp.exp2(power)


def transpose_kernel(in_ref, out_ref):
    width = in_ref.shape[1]
    at = pl.ds(pl.multiple_of(pl.program_id(0) * width, width), width)
    out_ref[at, :] = in_ref[...].T


def ladder_kernel(chips, tile, pieces, own_ref, sib_ref, *refs):
    rows_in, outs, rhs = refs[: len(pieces)], refs[len(pieces) : -1], refs[-1]
    at = 0
    for ref, (start, count) in zip(rows_in, pieces):
        rhs[pl.ds(at, count), :] = ref[pl.ds(start, count), :]
        at += count
    low = is_low((tile, LANES))
    group = min(4, chips)

    def step(i, carry):
        at = pl.ds(pl.multiple_of(i * tile, tile), tile)
        for first in range(0, chips, group):
            right = rhs[pl.ds(first * WIDTH, group * WIDTH), :]
            own = lax.dot_general(own_ref[at, :], right, NT, preferred_element_type=jnp.float32)
            sib = lax.dot_general(sib_ref[at, :], right, NT, preferred_element_type=jnp.float32)
            for k in range(0, group, 2):
                u = own[:, k * WIDTH : k * WIDTH + LANES]
                v = sib[:, k * WIDTH : k * WIDTH + LANES]
                encode(jnp.where(low, u, turn(v)), outs[first + k].at[i])
                encode(jnp.where(low, turn(u), v), outs[first + k + 1].at[i])
        return carry

    lax.fori_loop(0, own_ref.shape[0] // tile, step, 0)


def early_ladder_kernel(chips, tile, vir, pieces, place_ref, own_ref, sib_ref, *refs):
    rows_in, (parts, away, rhs, work, sent) = refs[: len(pieces)], refs[len(pieces) :]
    chip, z = place_ref[0], place_ref[2]
    at = 0
    for ref, (start, count) in zip(rows_in, pieces):
        rhs[pl.ds(at, count), :] = ref[pl.ds(start, count), :]
        at += count
    low = is_low((tile, LANES))
    block = vir // chips
    group = own_ref.shape[0] // chips

    def step(i, carry):
        at = pl.ds(pl.multiple_of(i * tile, tile), tile)
        own = lax.dot_general(own_ref[at, :], rhs[...], NT, preferred_element_type=jnp.float32)
        sib = lax.dot_general(sib_ref[at, :], rhs[...], NT, preferred_element_type=jnp.float32)
        for d in range(0, chips, 2):
            u = own[:, d * WIDTH : d * WIDTH + LANES]
            v = sib[:, d * WIDTH : d * WIDTH + LANES]
            work[d] = jnp.where(low, u, turn(v))
            work[d + 1] = jnp.where(low, turn(u), v)
        for e in range(chips):
            column = (chip ^ z ^ e) * block
            out = sent if e % 2 else parts
            for k in range(tile // vir):
                source = pl.ds(pl.multiple_of(k * vir + column, 8), block)
                line = (i * (tile // vir) + k) * block
                for d in range(chips):
                    target = pl.ds(pl.multiple_of(d * group + line, 8), block)
                    out[e // 2, target, :] = work[d, source, :]
        return carry

    lax.fori_loop(0, own_ref.shape[0] // tile, step, 0)
    for i in range(chips // 2):
        for d in range(chips):
            encode(sent[i, pl.ds(d * group, group), :], away.at[i, d])


def sum_kernel(places, count, parts, *refs):
    got, (own, pair, single) = refs[:count], refs[count:]
    group = own.shape[0] - TAIL
    for d, out in enumerate((own, pair.at[0], single.at[0], pair.at[1])):
        total = parts[0, pl.ds(d * group, group), :]
        for k, slot in places:
            total = total + decode(got[k].at[slot, d])
        encode(total, out)


def early_antisym_kernel(chips, side, place_ref, *refs):
    mine, pair_in, single_in, own, pair, single, cube, sent = refs
    arrived = (mine, pair_in.at[0], single_in.at[0], single_in.at[1])
    outs = (None, pair.at[0], single.at[0], pair.at[1])
    chip, core, z = place_ref[0], place_ref[1], place_ref[2]
    group = own.shape[0]
    size, held = CORES * group, side // CORES
    low = is_low((group, LANES))
    for d in range(chips):
        values = decode(arrived[d])
        turned = turn(values)
        at_own = pl.multiple_of(d * size + core * group, group)
        at_sib = pl.multiple_of(d * size + (1 - core) * group, group)
        cube[pl.ds(at_own, group), :] = jnp.where(low, values, turned)
        cube[pl.ds(at_sib, group), :] = jnp.where(low, turned, values)
    low = is_low((side, LANES))
    for e in range(chips):
        this = (e ^ z ^ chip) * size
        that = (e ^ chip) * size
        out = sent if e else own
        for a in range(held):
            b = a + held
            here = cube[pl.ds(pl.multiple_of(this + a * side, 8), side), :]
            other = cube[pl.ds(pl.multiple_of(this + b * side, 8), side), :]
            lower = here - cube[pl.ds(that + a, side, stride=side), :]
            upper = other - cube[pl.ds(that + b, side, stride=side), :]
            out[pl.ds(a * side, side), :] = jnp.where(low, lower, upper)
        if e:
            encode(sent[...], outs[e])


def early_finish_kernel(chips, side, pair_ref, vir_ref, own, pair, single, *refs):
    got, (out_ref, cube) = (pair.at[0], single.at[0], single.at[1]), refs[-2:]
    group, rows = own.shape[0], cube.shape[0]
    for e in range(chips):
        values = decode(got[e - 1]) if e else own[...]
        for a in range(group // side):
            target = pl.ds((a * chips + e) * side, side)
            cube[target, :] = values[a * side : (a + 1) * side]
    virt = jnp.where(is_low(cube.shape), vir_ref[:, 0:1], vir_ref[:, 1:2])
    update = (cube[...] / (pair_ref[0] - virt)).T
    out_ref[:, pl.ds(0, rows)] = update[:WIDTH]
    out_ref[:, pl.ds(rows, rows)] = update[WIDTH:]


def antisym_kernel(chips, slabs, vir, place_ref, *refs):
    arrived, (parts, *away, cube, sent) = refs[:chips], refs[chips:]
    chip, core, z = place_ref[0], place_ref[1], place_ref[2]
    tiles, tile = arrived[0].shape[0], arrived[0].shape[1] - TAIL
    rows = tiles * tile
    low = is_low((tile, LANES))
    for d in range(chips):
        base = (chip ^ d) * (CORES * rows)
        for t in range(tiles):
            values = decode(arrived[d].at[t])
            turned = turn(values)
            at_own = pl.multiple_of(base + core * rows + t * tile, tile)
            at_sib = pl.multiple_of(base + (1 - core) * rows + t * tile, tile)
            cube[pl.ds(at_own, tile), :] = jnp.where(low, values, turned)
            cube[pl.ds(at_sib, tile), :] = jnp.where(low, turned, values)

    half = vir // slabs // 2
    low = is_low((vir, LANES))
    part_tile = away[0].shape[2] - TAIL

    def into(slab, out):
        def body(k, carry):
            a = slab * (2 * half) + k
            b = a + half
            here = cube[pl.ds(pl.multiple_of(a * vir, vir), vir), :]
            other = cube[pl.ds(pl.multiple_of(b * vir, vir), vir), :]
            lower = here - cube[pl.ds(a, vir, stride=vir), :]
            upper = other - cube[pl.ds(b, vir, stride=vir), :]
            out[pl.ds(pl.multiple_of(k * vir, vir), vir), :] = jnp.where(low, lower, upper)
            return carry

        lax.fori_loop(0, half, body, 0)

    for e in reversed(range(1, slabs, 2)):
        into(e ^ z, sent)
        out = away[e // 2].at[0] if len(away) > 1 else away[0].at[e // 2]
        for t in range(out.shape[0]):
            encode(sent[pl.ds(t * part_tile, part_tile), :], out.at[t])
    for e in range(0, slabs, 2):
        into(e ^ z, parts.at[e // 2])


def hop_kernel(slots, parts, *refs):
    got, out = refs[:-1], refs[-1]
    tiles, tile = out.shape[1], out.shape[2] - TAIL
    for i, (part, places) in enumerate(slots):
        for t in range(tiles):
            total = parts[part, pl.ds(t * tile, tile), :]
            for k, slot in places:
                total = total + decode(got[k].at[slot, t])
            encode(total, out.at[i, t])


def finish_kernel(places, count, pair_ref, vir_ref, parts, *refs):
    got, out_ref = refs[:count], refs[-1]
    tiles, tile = got[0].shape[1], got[0].shape[2] - TAIL
    low = is_low((tile, LANES))
    pair = pair_ref[0]
    half = tiles * tile
    for t in range(tiles):
        at = pl.ds(t * tile, tile)
        total = parts[0, at, :]
        for k, slot in places:
            total = total + decode(got[k].at[slot, t])
        virt = jnp.where(low, vir_ref[at, 0:1], vir_ref[at, 1:2])
        update = (total / (pair - virt)).T
        out_ref[:, pl.ds(t * tile, tile)] = update[:WIDTH]
        out_ref[:, pl.ds(half + t * tile, tile)] = update[WIDTH:]


def on_device(mesh, amplitudes, integrals, pair_index, eps_occ, eps_vir):
    devices, slabs = mesh.shape["pair"], mesh.shape["slab"]
    chips = devices // CORES
    num_pairs, depth = amplitudes.shape
    rows = integrals.shape[1]
    vir = eps_vir.shape[0]
    chunks = num_pairs // WIDTH
    half = vir // slabs // 2
    part_rows = half * vir
    tile, part_tile = tile_of(rows, 384), tile_of(part_rows, 384)
    tiles, part_tiles = rows // tile, part_rows // part_tile
    me, z = lax.axis_index("pair"), lax.axis_index("slab")
    chip, core = me // CORES, me % CORES

    def to_chip(x, d):
        return lax.ppermute(x, "pair", [(i, i ^ (d * CORES)) for i in range(devices)])

    def limit(mib):
        return pltpu.CompilerParams(vmem_limit_bytes=mib * 1024 * 1024)

    def cost(flops, moved):
        return pl.CostEstimate(flops=flops, bytes_accessed=moved, transcendentals=0)

    smem = pl.BlockSpec(memory_space=pltpu.SMEM)
    vmem = pl.BlockSpec(memory_space=pltpu.VMEM)
    message = jax.ShapeDtypeStruct((tiles, tile + TAIL, LANES), jnp.int16)

    def parcel(count):
        return (count, part_tiles, part_tile + TAIL, LANES)

    column = max((c for c in (384, 256, 128) if rows % c == 0), default=rows)
    transpose = pl.pallas_call(
        transpose_kernel,
        grid=(rows // column,),
        in_specs=[pl.BlockSpec((depth, column), lambda i: (0, i))],
        out_specs=vmem,
        out_shape=jax.ShapeDtypeStruct((rows, depth), jnp.bfloat16),
        compiler_params=limit(16),
        cost_estimate=cost(0, 4 * rows * depth),
        name="transpose",
    )

    def ordered(
        body, flops, inputs, in_specs, out_specs, out_shape, mib, scratch=(), name=None, **more
    ):
        given, made = len(in_specs), len(out_specs)
        moved = sum(x.size * x.dtype.itemsize for x in (*inputs, *out_shape))

        def kernel(*refs):
            token_in, token_out = refs[given], refs[given + 1 + made]
            token_out[...] = token_in[...]
            outs = refs[given + 1 : given + 1 + made]
            body(*refs[:given], *outs, *refs[given + made + 2 :])

        def call(token, *args):
            return pl.pallas_call(
                kernel,
                in_specs=[*in_specs, vmem],
                out_specs=[*out_specs, vmem],
                out_shape=[*out_shape, jax.ShapeDtypeStruct(token.shape, token.dtype)],
                scratch_shapes=scratch,
                compiler_params=limit(mib),
                cost_estimate=cost(flops, moved),
                name=name,
                **more,
            )(*args, token)

        return call, inputs

    def ladder(gathered):
        arrays, pieces = zip(*[(x, (start, count)) for x, start, count in gathered])
        return ordered(
            functools.partial(ladder_kernel, chips, tile, pieces),
            4 * rows * depth * chips * WIDTH,
            [own_t, sib_t, *arrays],
            [vmem] * (2 + len(arrays)),
            [vmem] * chips,
            [message] * chips,
            16,
            [pltpu.VMEM((chips * WIDTH, depth), jnp.bfloat16)],
            name="ladder",
        )

    early = chips == slabs == 4 and tile % vir == 0 and vir // chips % 8 == 0
    side, group = vir // chips, rows // chips
    small, single, pair = (
        jax.ShapeDtypeStruct((*lead, group + TAIL, LANES), jnp.int16) for lead in ((), (1,), (2,))
    )
    grouped = (chips // 2, chips * group, LANES)

    def early_ladder(gathered):
        arrays, pieces = zip(*[(x, (start, count)) for x, start, count in gathered])
        return ordered(
            functools.partial(early_ladder_kernel, chips, tile, vir, pieces),
            4 * rows * depth * chips * WIDTH,
            [place, own_t, sib_t, *arrays],
            [smem] + [vmem] * (2 + len(arrays)),
            [vmem] * 2,
            [
                jax.ShapeDtypeStruct(grouped, jnp.float32),
                jax.ShapeDtypeStruct((chips // 2, chips, *small.shape), jnp.int16),
            ],
            20,
            [
                pltpu.VMEM((chips * WIDTH, depth), jnp.bfloat16),
                pltpu.VMEM((chips, tile, LANES), jnp.float32),
                pltpu.VMEM(grouped, jnp.float32),
            ],
            name="early_ladder",
        )

    def early_sum(places, parts, got):
        return ordered(
            functools.partial(sum_kernel, places, len(got)),
            8 * chips * group * LANES,
            [parts, *got],
            [vmem] * (1 + len(got)),
            [vmem] * 3,
            [small, pair, single],
            8,
            name="early_sum",
        )

    def early_antisym(arrived):
        return ordered(
            functools.partial(early_antisym_kernel, chips, side),
            8 * vir * side * LANES,
            [place, *arrived],
            [smem] + [vmem] * 3,
            [vmem] * 3,
            [jax.ShapeDtypeStruct((group, LANES), jnp.float32), pair, single],
            12,
            [
                pltpu.VMEM((chips * side * side, LANES), jnp.float32),
                pltpu.VMEM((group, LANES), jnp.float32),
            ],
            name="early_antisym",
        )

    def antisym(parcels, arrived):
        return ordered(
            functools.partial(antisym_kernel, chips, slabs, vir),
            8 * vir * vir * LANES,
            [place, *arrived],
            [smem] + [vmem] * chips,
            [vmem] * (1 + parcels),
            [jax.ShapeDtypeStruct((slabs // 2, part_rows, LANES), jnp.float32)]
            + [jax.ShapeDtypeStruct(parcel(slabs // 2 // parcels), jnp.int16)] * parcels,
            16,
            [
                pltpu.VMEM((vir * vir, LANES), jnp.float32),
                pltpu.VMEM((part_rows, LANES), jnp.float32),
            ],
            name="antisym",
        )

    def hop(slots, parts, got):
        return ordered(
            functools.partial(hop_kernel, slots),
            8 * parts.size,
            [parts, *got],
            [vmem] * (1 + len(got)),
            [vmem],
            [jax.ShapeDtypeStruct((len(slots), *got[0].shape[1:]), jnp.int16)],
            8,
            name="hop",
        )

    def finish(r, parts, got, places, so_far):
        given = [] if so_far is None else [so_far]
        if places is None:
            body = functools.partial(early_finish_kernel, chips, side)
        else:
            body = functools.partial(finish_kernel, places, len(got))
        return ordered(
            body,
            16 * part_rows * LANES,
            [eps_pair, eps_virt, parts, *got, *given],
            [pl.BlockSpec((1, 1, LANES), lambda i: (r, 0, 0))]
            + [vmem] * (2 + len(got))
            + [pl.BlockSpec(memory_space=pl.ANY)] * len(given),
            [pl.BlockSpec((WIDTH, 2 * part_rows), lambda i: (r, 0))],
            [jax.ShapeDtypeStruct((num_pairs, 2 * part_rows), jnp.float32)],
            8,
            [] if places else [pltpu.VMEM((part_rows, LANES), jnp.float32)],
            name="finish",
            grid=(1,),
            input_output_aliases={3 + len(got): 0} if given else {},
        )

    in_hbm = functools.partial(pltpu.with_memory_space_constraint, memory_space=pltpu.HBM)
    own_t = transpose(in_hbm(integrals))
    swapped = lax.ppermute(integrals, "pair", [(i, i ^ 1) for i in range(devices)])
    sib_t = transpose(swapped)

    occ_ids = jnp.arange(eps_occ.shape[0], dtype=jnp.int32)

    def pick(ids):
        return jnp.sum(jnp.where(ids[:, None] == occ_ids[None, :], eps_occ[None, :], 0.0), axis=1)

    eps_pair = (pick(pair_index[:, 0]) + pick(pair_index[:, 1])).reshape(chunks, 1, WIDTH)
    eps_pair = jnp.concatenate([eps_pair, eps_pair], axis=2)
    eps_mine = lax.dynamic_slice(eps_vir.reshape(slabs, 2, half), (z, 0, 0), (1, 2, half))[0]
    eps_virt = (eps_mine[:, :, None] + eps_vir[None, None, :]).reshape(2, part_rows).T

    place = jnp.stack([chip, core, z]).astype(jnp.int32)

    def gather(mine, beside):
        count = mine.shape[0]
        if chips != 4:
            return [[mine]] + [[to_chip(mine, d)] for d in range(1, chips)], beside
        one, two = to_chip(mine, 1), to_chip(mine, 2)
        if beside:
            one, two, *beside = lax.optimization_barrier((one, two, *beside))
        low, high = to_chip(two[: count // 2], 1), to_chip(one[count // 2 :], 2)
        return [[mine], [one], [two], [low, high]], beside

    if early:
        head, (own_t, eps_pair, eps_virt, rest) = gather(
            amplitudes[:WIDTH], (own_t, eps_pair, eps_virt, amplitudes[WIDTH:])
        )
        tail, _ = gather(rest, ())
        gathered = [(0, head), (WIDTH, tail)]
    else:
        tail, (own_t, sib_t, eps_pair, eps_virt) = gather(
            amplitudes, (own_t, sib_t, eps_pair, eps_virt)
        )
        gathered = [(0, tail)]

    def rows_of(r):
        found = []
        for d in range(chips):
            for base, parts in gathered:
                at = base
                for x in parts[d]:
                    begin = max(r * WIDTH, at)
                    end = min((r + 1) * WIDTH, at + x.shape[0])
                    if begin < end:
                        found.append((x, begin - at, end - begin))
                    at += x.shape[0]
        return found

    def across(x, level):
        return lax.ppermute(x, "slab", [(i, i ^ level) for i in range(slabs)])

    def halved(parts, away):
        each = slabs // 2 // len(away)
        held = {e: [(away[e // 2 // each], e // 2 % each)] for e in range(0, slabs, 2)}

        def listed(wanted):
            arrays = []
            for e in wanted:
                arrays += [x for x, _ in held[e] if not any(x is y for y in arrays)]
            index = {id(x): k for k, x in enumerate(arrays)}
            return arrays, [(e // 2, [(index[id(x)], i) for x, i in held[e]]) for e in wanted]

        level = 2
        while level < slabs:
            leave = [e for e in held if e & level]
            got, slots = listed(leave)
            (out,) = yield hop(slots, parts, got)
            out = across(out, level)
            for i, e in enumerate(leave):
                held[e ^ level].append((out, i))
                del held[e]
            level *= 2
        got, ((_, places),) = listed([0])
        return got, places

    def by_steps(move, pair, single):
        first = move(pair, 1)
        return [first, move(jnp.concatenate([single, first[1:]]), 2)]

    def early_stages(r):
        parts, away = yield early_ladder(rows_of(r))
        got, places = yield from halved(parts, [across(away, 1)])
        mine, *sums = yield early_sum(places, parts, got)
        arrived = by_steps(to_chip, *sums)
        own, *blocks = yield early_antisym([mine, *arrived])
        yield finish(r, own, by_steps(across, *blocks), None, update)

    def stages(r):
        sums = yield ladder(rows_of(r))
        if turns:
            sums, _ = lax.optimization_barrier((sums, turns[-1] + results[-1][:1]))
        arrived = [to_chip(sums[d], d) for d in range(1, chips)]
        turns.append(arrived)
        parcels = slabs // 2 if r == chunks - 1 else 1
        parts, *away = yield antisym(parcels, [sums[0], *arrived])
        if parcels > 1 and firsts:
            away, _ = lax.optimization_barrier((away, firsts[-1]))
        away = [across(x, 1) for x in reversed(away)][::-1]
        firsts.append(away)
        got, places = yield from halved(parts, away)
        yield finish(r, parts, got, places, update)

    hops = max(0, (slabs - 1).bit_length() - 1)

    def when(stage):
        r, k = stage
        if early and r == 0:
            return (20, *[44] * hops, 54, 66, 83)[k]
        if k == 0:
            return 37 + 5 * r if early else 30 + 5 * r
        return 15 * r + (45 if early else 54) + (k - 1) * 17 - (1 if k == 2 + hops else 0)

    order = [(r, k) for r in range(chunks) for k in range(3 + hops + (early and r == 0))]
    order = sorted(order, key=when)

    turns, firsts = [], []
    running = [early_stages(r) if early and r == 0 else stages(r) for r in range(chunks)]
    results = [None] * chunks
    update, token = None, jnp.zeros((8, LANES), jnp.float32)
    for r, k in order:
        call, inputs = running[r].send(results[r])
        *results[r], token = call(token, *inputs)
        if results[r][0].shape == (num_pairs, 2 * part_rows):
            update = results[r][0]
    return update


def solution(mesh):
    in_specs = (P("pair", "slab"), P("slab", "pair"), P("pair", None), P(), P())
    out_specs = P("pair", "slab")
    return jax.shard_map(
        functools.partial(on_device, mesh),
        mesh=mesh,
        in_specs=in_specs,
        out_specs=out_specs,
        check_vma=False,
    )
```

```python
import functools

import jax
import jax.numpy as jnp
from jax import lax
from jax.experimental import pallas as pl
from jax.experimental.pallas import tpu as pltpu
from jax.sharding import PartitionSpec as P

CORES = 2
WIDTH = 64
LANES = 2 * WIDTH
TAIL = 16
NT = (((1,), (1,)), ((), ()))


def tile_of(rows, most):
    return max(t for t in range(16, most + 1, 16) if rows % t == 0)


def is_low(shape):
    return lax.broadcasted_iota(jnp.int32, shape, len(shape) - 1) < WIDTH


def turn(values):
    return pltpu.roll(values, WIDTH, 1)


def encode(values, out_ref):
    tile = values.shape[0]
    peak = jnp.max(jnp.abs(values), axis=0, keepdims=True)
    power = jnp.ceil(jnp.log2(jnp.maximum(peak, 1e-30) * (1.0 / 32760.0)))
    codes = jnp.round(values * jnp.exp2(-power)).astype(jnp.int32)
    out_ref[pl.ds(0, tile), :] = codes.astype(jnp.int16)
    wide = jnp.broadcast_to(power.astype(jnp.int32), (TAIL, LANES))
    out_ref[pl.ds(tile, TAIL), :] = wide.astype(jnp.int16)


def decode(ref):
    tile = ref.shape[0] - TAIL
    power = ref[pl.ds(tile, TAIL), :].astype(jnp.int32).astype(jnp.float32)[0:1, :]
    return ref[pl.ds(0, tile), :].astype(jnp.int32).astype(jnp.float32) * jnp.exp2(power)


def transpose_kernel(in_ref, out_ref):
    width = in_ref.shape[1]
    at = pl.ds(pl.multiple_of(pl.program_id(0) * width, width), width)
    out_ref[at, :] = in_ref[...].T


def ladder_kernel(chips, tile, pieces, own_ref, sib_ref, *refs):
    rows_in, outs, rhs = refs[: len(pieces)], refs[len(pieces) : -1], refs[-1]
    at = 0
    for ref, (start, count) in zip(rows_in, pieces):
        rhs[pl.ds(at, count), :] = ref[pl.ds(start, count), :]
        at += count
    low = is_low((tile, LANES))
    group = min(4, chips)

    def step(i, carry):
        at = pl.ds(pl.multiple_of(i * tile, tile), tile)
        for first in range(0, chips, group):
            right = rhs[pl.ds(first * WIDTH, group * WIDTH), :]
            own = lax.dot_general(own_ref[at, :], right, NT, preferred_element_type=jnp.float32)
            sib = lax.dot_general(sib_ref[at, :], right, NT, preferred_element_type=jnp.float32)
            for k in range(0, group, 2):
                u = own[:, k * WIDTH : k * WIDTH + LANES]
                v = sib[:, k * WIDTH : k * WIDTH + LANES]
                encode(jnp.where(low, u, turn(v)), outs[first + k].at[i])
                encode(jnp.where(low, turn(u), v), outs[first + k + 1].at[i])
        return carry

    lax.fori_loop(0, own_ref.shape[0] // tile, step, 0)


def early_ladder_kernel(chips, tile, vir, pieces, place_ref, own_ref, sib_ref, *refs):
    rows_in, (parts, away, rhs, work, sent) = refs[: len(pieces)], refs[len(pieces) :]
    chip, z = place_ref[0], place_ref[2]
    at = 0
    for ref, (start, count) in zip(rows_in, pieces):
        rhs[pl.ds(at, count), :] = ref[pl.ds(start, count), :]
        at += count
    low = is_low((tile, LANES))
    block = vir // chips
    group = own_ref.shape[0] // chips

    def step(i, carry):
        at = pl.ds(pl.multiple_of(i * tile, tile), tile)
        own = lax.dot_general(own_ref[at, :], rhs[...], NT, preferred_element_type=jnp.float32)
        sib = lax.dot_general(sib_ref[at, :], rhs[...], NT, preferred_element_type=jnp.float32)
        for d in range(0, chips, 2):
            u = own[:, d * WIDTH : d * WIDTH + LANES]
            v = sib[:, d * WIDTH : d * WIDTH + LANES]
            work[d] = jnp.where(low, u, turn(v))
            work[d + 1] = jnp.where(low, turn(u), v)
        for e in range(chips):
            column = (chip ^ z ^ e) * block
            out = sent if e % 2 else parts
            for k in range(tile // vir):
                source = pl.ds(pl.multiple_of(k * vir + column, 8), block)
                line = (i * (tile // vir) + k) * block
                for d in range(chips):
                    target = pl.ds(pl.multiple_of(d * group + line, 8), block)
                    out[e // 2, target, :] = work[d, source, :]
        return carry

    lax.fori_loop(0, own_ref.shape[0] // tile, step, 0)
    for i in range(chips // 2):
        for d in range(chips):
            encode(sent[i, pl.ds(d * group, group), :], away.at[i, d])


def sum_kernel(places, count, parts, *refs):
    got, (own, pair, single) = refs[:count], refs[count:]
    group = own.shape[0] - TAIL
    for d, out in enumerate((own, pair.at[0], single.at[0], pair.at[1])):
        total = parts[0, pl.ds(d * group, group), :]
        for k, slot in places:
            total = total + decode(got[k].at[slot, d])
        encode(total, out)


def early_antisym_kernel(chips, side, place_ref, *refs):
    mine, pair_in, single_in, own, pair, single, cube, sent = refs
    arrived = (mine, pair_in.at[0], single_in.at[0], single_in.at[1])
    outs = (None, pair.at[0], single.at[0], pair.at[1])
    chip, core, z = place_ref[0], place_ref[1], place_ref[2]
    group = own.shape[0]
    size, held = CORES * group, side // CORES
    low = is_low((group, LANES))
    for d in range(chips):
        values = decode(arrived[d])
        turned = turn(values)
        at_own = pl.multiple_of(d * size + core * group, group)
        at_sib = pl.multiple_of(d * size + (1 - core) * group, group)
        cube[pl.ds(at_own, group), :] = jnp.where(low, values, turned)
        cube[pl.ds(at_sib, group), :] = jnp.where(low, turned, values)
    low = is_low((side, LANES))
    for e in range(chips):
        this = (e ^ z ^ chip) * size
        that = (e ^ chip) * size
        out = sent if e else own
        for a in range(held):
            b = a + held
            here = cube[pl.ds(pl.multiple_of(this + a * side, 8), side), :]
            other = cube[pl.ds(pl.multiple_of(this + b * side, 8), side), :]
            lower = here - cube[pl.ds(that + a, side, stride=side), :]
            upper = other - cube[pl.ds(that + b, side, stride=side), :]
            out[pl.ds(a * side, side), :] = jnp.where(low, lower, upper)
        if e:
            encode(sent[...], outs[e])


def early_finish_kernel(chips, side, pair_ref, vir_ref, own, pair, single, *refs):
    got, (out_ref, cube) = (pair.at[0], single.at[0], single.at[1]), refs[-2:]
    group, rows = own.shape[0], cube.shape[0]
    for e in range(chips):
        values = decode(got[e - 1]) if e else own[...]
        for a in range(group // side):
            target = pl.ds((a * chips + e) * side, side)
            cube[target, :] = values[a * side : (a + 1) * side]
    virt = jnp.where(is_low(cube.shape), vir_ref[:, 0:1], vir_ref[:, 1:2])
    update = (cube[...] / (pair_ref[0] - virt)).T
    out_ref[:, pl.ds(0, rows)] = update[:WIDTH]
    out_ref[:, pl.ds(rows, rows)] = update[WIDTH:]


def antisym_kernel(chips, slabs, vir, place_ref, *refs):
    arrived, (parts, *away, cube, sent) = refs[:chips], refs[chips:]
    chip, core, z = place_ref[0], place_ref[1], place_ref[2]
    tiles, tile = arrived[0].shape[0], arrived[0].shape[1] - TAIL
    rows = tiles * tile
    low = is_low((tile, LANES))
    for d in range(chips):
        base = (chip ^ d) * (CORES * rows)
        for t in range(tiles):
            values = decode(arrived[d].at[t])
            turned = turn(values)
            at_own = pl.multiple_of(base + core * rows + t * tile, tile)
            at_sib = pl.multiple_of(base + (1 - core) * rows + t * tile, tile)
            cube[pl.ds(at_own, tile), :] = jnp.where(low, values, turned)
            cube[pl.ds(at_sib, tile), :] = jnp.where(low, turned, values)

    half = vir // slabs // 2
    low = is_low((vir, LANES))
    part_tile = away[0].shape[2] - TAIL

    def into(slab, out):
        def body(k, carry):
            a = slab * (2 * half) + k
            b = a + half
            here = cube[pl.ds(pl.multiple_of(a * vir, vir), vir), :]
            other = cube[pl.ds(pl.multiple_of(b * vir, vir), vir), :]
            lower = here - cube[pl.ds(a, vir, stride=vir), :]
            upper = other - cube[pl.ds(b, vir, stride=vir), :]
            out[pl.ds(pl.multiple_of(k * vir, vir), vir), :] = jnp.where(low, lower, upper)
            return carry

        lax.fori_loop(0, half, body, 0)

    for e in reversed(range(1, slabs, 2)):
        into(e ^ z, sent)
        out = away[e // 2].at[0] if len(away) > 1 else away[0].at[e // 2]
        for t in range(out.shape[0]):
            encode(sent[pl.ds(t * part_tile, part_tile), :], out.at[t])
    for e in range(0, slabs, 2):
        into(e ^ z, parts.at[e // 2])


def hop_kernel(slots, parts, *refs):
    got, out = refs[:-1], refs[-1]
    tiles, tile = out.shape[1], out.shape[2] - TAIL
    for i, (part, places) in enumerate(slots):
        for t in range(tiles):
            total = parts[part, pl.ds(t * tile, tile), :]
            for k, slot in places:
                total = total + decode(got[k].at[slot, t])
            encode(total, out.at[i, t])


def finish_kernel(places, count, pair_ref, vir_ref, parts, *refs):
    got, out_ref = refs[:count], refs[-1]
    tiles, tile = got[0].shape[1], got[0].shape[2] - TAIL
    low = is_low((tile, LANES))
    pair = pair_ref[0]
    half = tiles * tile
    for t in range(tiles):
        at = pl.ds(t * tile, tile)
        total = parts[0, at, :]
        for k, slot in places:
            total = total + decode(got[k].at[slot, t])
        virt = jnp.where(low, vir_ref[at, 0:1], vir_ref[at, 1:2])
        update = (total / (pair - virt)).T
        out_ref[:, pl.ds(t * tile, tile)] = update[:WIDTH]
        out_ref[:, pl.ds(half + t * tile, tile)] = update[WIDTH:]


def on_device(mesh, amplitudes, integrals, pair_index, eps_occ, eps_vir):
    devices, slabs = mesh.shape["pair"], mesh.shape["slab"]
    chips = devices // CORES
    num_pairs, depth = amplitudes.shape
    rows = integrals.shape[1]
    vir = eps_vir.shape[0]
    chunks = num_pairs // WIDTH
    half = vir // slabs // 2
    part_rows = half * vir
    tile, part_tile = tile_of(rows, 384), tile_of(part_rows, 384)
    tiles, part_tiles = rows // tile, part_rows // part_tile
    me, z = lax.axis_index("pair"), lax.axis_index("slab")
    chip, core = me // CORES, me % CORES

    def to_chip(x, d):
        return lax.ppermute(x, "pair", [(i, i ^ (d * CORES)) for i in range(devices)])

    def limit(mib):
        return pltpu.CompilerParams(vmem_limit_bytes=mib * 1024 * 1024)

    def cost(flops, moved):
        return pl.CostEstimate(flops=flops, bytes_accessed=moved, transcendentals=0)

    smem = pl.BlockSpec(memory_space=pltpu.SMEM)
    vmem = pl.BlockSpec(memory_space=pltpu.VMEM)
    message = jax.ShapeDtypeStruct((tiles, tile + TAIL, LANES), jnp.int16)

    def parcel(count):
        return (count, part_tiles, part_tile + TAIL, LANES)

    column = max((c for c in (384, 256, 128) if rows % c == 0), default=rows)
    transpose = pl.pallas_call(
        transpose_kernel,
        grid=(rows // column,),
        in_specs=[pl.BlockSpec((depth, column), lambda i: (0, i))],
        out_specs=vmem,
        out_shape=jax.ShapeDtypeStruct((rows, depth), jnp.bfloat16),
        compiler_params=limit(16),
        cost_estimate=cost(0, 4 * rows * depth),
        name="transpose",
    )

    def ordered(
        body, flops, inputs, in_specs, out_specs, out_shape, mib, scratch=(), name=None, **more
    ):
        given, made = len(in_specs), len(out_specs)
        moved = sum(x.size * x.dtype.itemsize for x in (*inputs, *out_shape))

        def kernel(*refs):
            token_in, token_out = refs[given], refs[given + 1 + made]
            token_out[...] = token_in[...]
            outs = refs[given + 1 : given + 1 + made]
            body(*refs[:given], *outs, *refs[given + made + 2 :])

        def call(token, *args):
            return pl.pallas_call(
                kernel,
                in_specs=[*in_specs, vmem],
                out_specs=[*out_specs, vmem],
                out_shape=[*out_shape, jax.ShapeDtypeStruct(token.shape, token.dtype)],
                scratch_shapes=scratch,
                compiler_params=limit(mib),
                cost_estimate=cost(flops, moved),
                name=name,
                **more,
            )(*args, token)

        return call, inputs

    def ladder(gathered):
        arrays, pieces = zip(*[(x, (start, count)) for x, start, count in gathered])
        return ordered(
            functools.partial(ladder_kernel, chips, tile, pieces),
            4 * rows * depth * chips * WIDTH,
            [own_t, sib_t, *arrays],
            [vmem] * (2 + len(arrays)),
            [vmem] * chips,
            [message] * chips,
            16,
            [pltpu.VMEM((chips * WIDTH, depth), jnp.bfloat16)],
            name="ladder",
        )

    early = chips == slabs == 4 and tile % vir == 0 and vir // chips % 8 == 0
    side, group = vir // chips, rows // chips
    small, single, pair = (
        jax.ShapeDtypeStruct((*lead, group + TAIL, LANES), jnp.int16) for lead in ((), (1,), (2,))
    )
    grouped = (chips // 2, chips * group, LANES)

    def early_ladder(gathered):
        arrays, pieces = zip(*[(x, (start, count)) for x, start, count in gathered])
        return ordered(
            functools.partial(early_ladder_kernel, chips, tile, vir, pieces),
            4 * rows * depth * chips * WIDTH,
            [place, own_t, sib_t, *arrays],
            [smem] + [vmem] * (2 + len(arrays)),
            [vmem] * 2,
            [
                jax.ShapeDtypeStruct(grouped, jnp.float32),
                jax.ShapeDtypeStruct((chips // 2, chips, *small.shape), jnp.int16),
            ],
            20,
            [
                pltpu.VMEM((chips * WIDTH, depth), jnp.bfloat16),
                pltpu.VMEM((chips, tile, LANES), jnp.float32),
                pltpu.VMEM(grouped, jnp.float32),
            ],
            name="early_ladder",
        )

    def early_sum(places, parts, got):
        return ordered(
            functools.partial(sum_kernel, places, len(got)),
            8 * chips * group * LANES,
            [parts, *got],
            [vmem] * (1 + len(got)),
            [vmem] * 3,
            [small, pair, single],
            8,
            name="early_sum",
        )

    def early_antisym(arrived):
        return ordered(
            functools.partial(early_antisym_kernel, chips, side),
            8 * vir * side * LANES,
            [place, *arrived],
            [smem] + [vmem] * 3,
            [vmem] * 3,
            [jax.ShapeDtypeStruct((group, LANES), jnp.float32), pair, single],
            12,
            [
                pltpu.VMEM((chips * side * side, LANES), jnp.float32),
                pltpu.VMEM((group, LANES), jnp.float32),
            ],
            name="early_antisym",
        )

    def antisym(parcels, arrived):
        return ordered(
            functools.partial(antisym_kernel, chips, slabs, vir),
            8 * vir * vir * LANES,
            [place, *arrived],
            [smem] + [vmem] * chips,
            [vmem] * (1 + parcels),
            [jax.ShapeDtypeStruct((slabs // 2, part_rows, LANES), jnp.float32)]
            + [jax.ShapeDtypeStruct(parcel(slabs // 2 // parcels), jnp.int16)] * parcels,
            16,
            [
                pltpu.VMEM((vir * vir, LANES), jnp.float32),
                pltpu.VMEM((part_rows, LANES), jnp.float32),
            ],
            name="antisym",
        )

    def hop(slots, parts, got):
        return ordered(
            functools.partial(hop_kernel, slots),
            8 * parts.size,
            [parts, *got],
            [vmem] * (1 + len(got)),
            [vmem],
            [jax.ShapeDtypeStruct((len(slots), *got[0].shape[1:]), jnp.int16)],
            8,
            name="hop",
        )

    def finish(r, parts, got, places, so_far):
        given = [] if so_far is None else [so_far]
        if places is None:
            body = functools.partial(early_finish_kernel, chips, side)
        else:
            body = functools.partial(finish_kernel, places, len(got))
        return ordered(
            body,
            16 * part_rows * LANES,
            [eps_pair, eps_virt, parts, *got, *given],
            [pl.BlockSpec((1, 1, LANES), lambda i: (r, 0, 0))]
            + [vmem] * (2 + len(got))
            + [pl.BlockSpec(memory_space=pl.ANY)] * len(given),
            [pl.BlockSpec((WIDTH, 2 * part_rows), lambda i: (r, 0))],
            [jax.ShapeDtypeStruct((num_pairs, 2 * part_rows), jnp.float32)],
            8,
            [] if places else [pltpu.VMEM((part_rows, LANES), jnp.float32)],
            name="finish",
            grid=(1,),
            input_output_aliases={3 + len(got): 0} if given else {},
        )

    in_hbm = functools.partial(pltpu.with_memory_space_constraint, memory_space=pltpu.HBM)
    own_t = transpose(in_hbm(integrals))
    swapped = lax.ppermute(integrals, "pair", [(i, i ^ 1) for i in range(devices)])
    sib_t = transpose(swapped)

    occ_ids = jnp.arange(eps_occ.shape[0], dtype=jnp.int32)

    def pick(ids):
        return jnp.sum(jnp.where(ids[:, None] == occ_ids[None, :], eps_occ[None, :], 0.0), axis=1)

    eps_pair = (pick(pair_index[:, 0]) + pick(pair_index[:, 1])).reshape(chunks, 1, WIDTH)
    eps_pair = jnp.concatenate([eps_pair, eps_pair], axis=2)
    eps_mine = lax.dynamic_slice(eps_vir.reshape(slabs, 2, half), (z, 0, 0), (1, 2, half))[0]
    eps_virt = (eps_mine[:, :, None] + eps_vir[None, None, :]).reshape(2, part_rows).T

    place = jnp.stack([chip, core, z]).astype(jnp.int32)

    def gather(mine, beside):
        count = mine.shape[0]
        if chips != 4:
            return [[mine]] + [[to_chip(mine, d)] for d in range(1, chips)], beside
        one, two = to_chip(mine, 1), to_chip(mine, 2)
        if beside:
            one, two, *beside = lax.optimization_barrier((one, two, *beside))
        low, high = to_chip(two[: count // 2], 1), to_chip(one[count // 2 :], 2)
        return [[mine], [one], [two], [low, high]], beside

    if early:
        head, (own_t, eps_pair, eps_virt) = gather(
            amplitudes[:WIDTH], (own_t, eps_pair, eps_virt)
        )
        head, own_t, sib_t, rest = lax.optimization_barrier(
            (head, own_t, sib_t, amplitudes[WIDTH:])
        )
        tail, _ = gather(rest, ())
        gathered = [(0, head), (WIDTH, tail)]
    else:
        tail, (own_t, sib_t, eps_pair, eps_virt) = gather(
            amplitudes, (own_t, sib_t, eps_pair, eps_virt)
        )
        gathered = [(0, tail)]

    def rows_of(r):
        found = []
        for d in range(chips):
            for base, parts in gathered:
                at = base
                for x in parts[d]:
                    begin = max(r * WIDTH, at)
                    end = min((r + 1) * WIDTH, at + x.shape[0])
                    if begin < end:
                        found.append((x, begin - at, end - begin))
                    at += x.shape[0]
        return found

    def across(x, level):
        return lax.ppermute(x, "slab", [(i, i ^ level) for i in range(slabs)])

    def halved(parts, away):
        each = slabs // 2 // len(away)
        held = {e: [(away[e // 2 // each], e // 2 % each)] for e in range(0, slabs, 2)}

        def listed(wanted):
            arrays = []
            for e in wanted:
                arrays += [x for x, _ in held[e] if not any(x is y for y in arrays)]
            index = {id(x): k for k, x in enumerate(arrays)}
            return arrays, [(e // 2, [(index[id(x)], i) for x, i in held[e]]) for e in wanted]

        level = 2
        while level < slabs:
            leave = [e for e in held if e & level]
            got, slots = listed(leave)
            (out,) = yield hop(slots, parts, got)
            out = across(out, level)
            for i, e in enumerate(leave):
                held[e ^ level].append((out, i))
                del held[e]
            level *= 2
        got, ((_, places),) = listed([0])
        return got, places

    def by_steps(move, pair, single):
        first = move(pair, 1)
        return [first, move(jnp.concatenate([single, first[1:]]), 2)]

    def early_stages(r):
        parts, away = yield early_ladder(rows_of(r))
        got, places = yield from halved(parts, [across(away, 1)])
        mine, *sums = yield early_sum(places, parts, got)
        arrived = by_steps(to_chip, *sums)
        steps.append(arrived[0])
        yield None
        own, *blocks = yield early_antisym([mine, *arrived])
        yield finish(r, own, by_steps(across, *blocks), None, update)

    def stages(r):
        sums = yield ladder(rows_of(r))
        if turns:
            sums, _ = lax.optimization_barrier((sums, turns[-1] + results[-1][:1]))
        arrived = [to_chip(sums[d], d) for d in range(1, chips)]
        if steps:
            arrived, _ = lax.optimization_barrier((arrived, steps[:1]))
        turns.append(arrived)
        parcels = slabs // 2 if r == chunks - 1 else 1
        parts, *away = yield antisym(parcels, [sums[0], *arrived])
        if parcels > 1 and firsts:
            away, _ = lax.optimization_barrier((away, firsts[-1]))
        away = [across(x, 1) for x in reversed(away)][::-1]
        firsts.append(away)
        got, places = yield from halved(parts, away)
        yield finish(r, parts, got, places, update)

    hops = max(0, (slabs - 1).bit_length() - 1)

    def when(stage):
        r, k = stage
        if early and r == 0:
            return (20, *[41] * hops, 54, 55, 66, 90)[k]
        if k == 0:
            return 37 + 5 * r if early else 30 + 5 * r
        start = 15 * r + (45 if early else 54)
        return start + (k - 1) * (14 if early else 17) - (1 if k == 2 + hops else 0)

    order = [(r, k) for r in range(chunks) for k in range(3 + hops + 2 * (early and r == 0))]
    order = sorted(order, key=when)

    turns, firsts, steps = [], [], []
    running = [early_stages(r) if early and r == 0 else stages(r) for r in range(chunks)]
    results = [None] * chunks
    update, token = None, jnp.zeros((8, LANES), jnp.float32)
    for r, k in order:
        step = running[r].send(results[r])
        if step is None:
            continue
        call, inputs = step
        *results[r], token = call(token, *inputs)
        if results[r][0].shape == (num_pairs, 2 * part_rows):
            update = results[r][0]
    return update


def solution(mesh):
    in_specs = (P("pair", "slab"), P("slab", "pair"), P("pair", None), P(), P())
    out_specs = P("pair", "slab")
    return jax.shard_map(
        functools.partial(on_device, mesh),
        mesh=mesh,
        in_specs=in_specs,
        out_specs=out_specs,
        check_vma=False,
    )
```

```python
import functools

import jax
import jax.numpy as jnp
from jax import lax
from jax.experimental import pallas as pl
from jax.experimental.pallas import tpu as pltpu
from jax.sharding import PartitionSpec as P

CORES = 2
WIDTH = 64
LANES = 2 * WIDTH
TAIL = 16
NT = (((1,), (1,)), ((), ()))


def tile_of(rows, most):
    return max(t for t in range(16, most + 1, 16) if rows % t == 0)


def is_low(shape):
    return lax.broadcasted_iota(jnp.int32, shape, len(shape) - 1) < WIDTH


def turn(values):
    return pltpu.roll(values, WIDTH, 1)


def encode(values, out_ref):
    tile = values.shape[0]
    peak = jnp.max(jnp.abs(values), axis=0, keepdims=True)
    power = jnp.ceil(jnp.log2(jnp.maximum(peak, 1e-30) * (1.0 / 32760.0)))
    codes = jnp.round(values * jnp.exp2(-power)).astype(jnp.int32)
    out_ref[pl.ds(0, tile), :] = codes.astype(jnp.int16)
    wide = jnp.broadcast_to(power.astype(jnp.int32), (TAIL, LANES))
    out_ref[pl.ds(tile, TAIL), :] = wide.astype(jnp.int16)


def decode(ref):
    tile = ref.shape[0] - TAIL
    power = ref[pl.ds(tile, TAIL), :].astype(jnp.int32).astype(jnp.float32)[0:1, :]
    return ref[pl.ds(0, tile), :].astype(jnp.int32).astype(jnp.float32) * jnp.exp2(power)


def transpose_kernel(in_ref, out_ref):
    width = in_ref.shape[1]
    at = pl.ds(pl.multiple_of(pl.program_id(0) * width, width), width)
    out_ref[at, :] = in_ref[...].T


def ladder_kernel(chips, tile, pieces, own_ref, sib_ref, *refs):
    rows_in, outs, rhs = refs[: len(pieces)], refs[len(pieces) : -1], refs[-1]
    at = 0
    for ref, (start, count) in zip(rows_in, pieces):
        rhs[pl.ds(at, count), :] = ref[pl.ds(start, count), :]
        at += count
    low = is_low((tile, LANES))
    group = min(4, chips)

    def step(i, carry):
        at = pl.ds(pl.multiple_of(i * tile, tile), tile)
        for first in range(0, chips, group):
            right = rhs[pl.ds(first * WIDTH, group * WIDTH), :]
            own = lax.dot_general(own_ref[at, :], right, NT, preferred_element_type=jnp.float32)
            sib = lax.dot_general(sib_ref[at, :], right, NT, preferred_element_type=jnp.float32)
            for k in range(0, group, 2):
                u = own[:, k * WIDTH : k * WIDTH + LANES]
                v = sib[:, k * WIDTH : k * WIDTH + LANES]
                encode(jnp.where(low, u, turn(v)), outs[first + k].at[i])
                encode(jnp.where(low, turn(u), v), outs[first + k + 1].at[i])
        return carry

    lax.fori_loop(0, own_ref.shape[0] // tile, step, 0)


def early_ladder_kernel(chips, tile, vir, pieces, place_ref, own_ref, sib_ref, *refs):
    rows_in, (parts, *away, rhs, work, sent) = refs[: len(pieces)], refs[len(pieces) :]
    chip, z = place_ref[0], place_ref[2]
    at = 0
    for ref, (start, count) in zip(rows_in, pieces):
        rhs[pl.ds(at, count), :] = ref[pl.ds(start, count), :]
        at += count
    low = is_low((tile, LANES))
    block = vir // chips
    group = own_ref.shape[0] // chips

    def step(i, carry):
        at = pl.ds(pl.multiple_of(i * tile, tile), tile)
        own = lax.dot_general(own_ref[at, :], rhs[...], NT, preferred_element_type=jnp.float32)
        sib = lax.dot_general(sib_ref[at, :], rhs[...], NT, preferred_element_type=jnp.float32)
        for d in range(0, chips, 2):
            u = own[:, d * WIDTH : d * WIDTH + LANES]
            v = sib[:, d * WIDTH : d * WIDTH + LANES]
            work[d] = jnp.where(low, u, turn(v))
            work[d + 1] = jnp.where(low, turn(u), v)
        for e in range(chips):
            column = (chip ^ z ^ e) * block
            out = sent if e % 2 else parts
            for k in range(tile // vir):
                source = pl.ds(pl.multiple_of(k * vir + column, 8), block)
                line = (i * (tile // vir) + k) * block
                for d in range(chips):
                    target = pl.ds(pl.multiple_of(d * group + line, 8), block)
                    out[e // 2, target, :] = work[d, source, :]
        return carry

    lax.fori_loop(0, own_ref.shape[0] // tile, step, 0)
    for i in range(chips // 2):
        for d in range(chips):
            encode(sent[i, pl.ds(d * group, group), :], away[i].at[0, d])


def sum_kernel(places, count, parts, *refs):
    got, (own, pair, single) = refs[:count], refs[count:]
    group = own.shape[0] - TAIL
    for d, out in enumerate((own, pair.at[0], single.at[0], pair.at[1])):
        total = parts[0, pl.ds(d * group, group), :]
        for k, slot in places:
            total = total + decode(got[k].at[slot, d])
        encode(total, out)


def early_antisym_kernel(chips, side, place_ref, *refs):
    mine, pair_in, single_in, own, pair, single, cube, sent = refs
    arrived = (mine, pair_in.at[0], single_in.at[0], single_in.at[1])
    outs = (None, pair.at[0], single.at[0], pair.at[1])
    chip, core, z = place_ref[0], place_ref[1], place_ref[2]
    group = own.shape[0]
    size, held = CORES * group, side // CORES
    low = is_low((group, LANES))
    for d in range(chips):
        values = decode(arrived[d])
        turned = turn(values)
        at_own = pl.multiple_of(d * size + core * group, group)
        at_sib = pl.multiple_of(d * size + (1 - core) * group, group)
        cube[pl.ds(at_own, group), :] = jnp.where(low, values, turned)
        cube[pl.ds(at_sib, group), :] = jnp.where(low, turned, values)
    low = is_low((side, LANES))
    for e in range(chips):
        this = (e ^ z ^ chip) * size
        that = (e ^ chip) * size
        out = sent if e else own
        for a in range(held):
            b = a + held
            here = cube[pl.ds(pl.multiple_of(this + a * side, 8), side), :]
            other = cube[pl.ds(pl.multiple_of(this + b * side, 8), side), :]
            lower = here - cube[pl.ds(that + a, side, stride=side), :]
            upper = other - cube[pl.ds(that + b, side, stride=side), :]
            out[pl.ds(a * side, side), :] = jnp.where(low, lower, upper)
        if e:
            encode(sent[...], outs[e])


def early_finish_kernel(chips, side, pair_ref, vir_ref, own, pair, single, *refs):
    got, (out_ref, cube) = (pair.at[0], single.at[0], single.at[1]), refs[-2:]
    group, rows = own.shape[0], cube.shape[0]
    for e in range(chips):
        values = decode(got[e - 1]) if e else own[...]
        for a in range(group // side):
            target = pl.ds((a * chips + e) * side, side)
            cube[target, :] = values[a * side : (a + 1) * side]
    virt = jnp.where(is_low(cube.shape), vir_ref[:, 0:1], vir_ref[:, 1:2])
    update = (cube[...] / (pair_ref[0] - virt)).T
    out_ref[:, pl.ds(0, rows)] = update[:WIDTH]
    out_ref[:, pl.ds(rows, rows)] = update[WIDTH:]


def antisym_kernel(chips, slabs, vir, place_ref, *refs):
    arrived, (parts, *away, cube, sent) = refs[:chips], refs[chips:]
    chip, core, z = place_ref[0], place_ref[1], place_ref[2]
    tiles, tile = arrived[0].shape[0], arrived[0].shape[1] - TAIL
    rows = tiles * tile
    low = is_low((tile, LANES))
    for d in range(chips):
        base = (chip ^ d) * (CORES * rows)
        for t in range(tiles):
            values = decode(arrived[d].at[t])
            turned = turn(values)
            at_own = pl.multiple_of(base + core * rows + t * tile, tile)
            at_sib = pl.multiple_of(base + (1 - core) * rows + t * tile, tile)
            cube[pl.ds(at_own, tile), :] = jnp.where(low, values, turned)
            cube[pl.ds(at_sib, tile), :] = jnp.where(low, turned, values)

    half = vir // slabs // 2
    low = is_low((vir, LANES))
    part_tile = away[0].shape[2] - TAIL

    def into(slab, out):
        def body(k, carry):
            a = slab * (2 * half) + k
            b = a + half
            here = cube[pl.ds(pl.multiple_of(a * vir, vir), vir), :]
            other = cube[pl.ds(pl.multiple_of(b * vir, vir), vir), :]
            lower = here - cube[pl.ds(a, vir, stride=vir), :]
            upper = other - cube[pl.ds(b, vir, stride=vir), :]
            out[pl.ds(pl.multiple_of(k * vir, vir), vir), :] = jnp.where(low, lower, upper)
            return carry

        lax.fori_loop(0, half, body, 0)

    for e in reversed(range(1, slabs, 2)):
        into(e ^ z, sent)
        out = away[e // 2].at[0] if len(away) > 1 else away[0].at[e // 2]
        for t in range(out.shape[0]):
            encode(sent[pl.ds(t * part_tile, part_tile), :], out.at[t])
    for e in range(0, slabs, 2):
        into(e ^ z, parts.at[e // 2])


def hop_kernel(slots, parts, *refs):
    got, out = refs[:-1], refs[-1]
    tiles, tile = out.shape[1], out.shape[2] - TAIL
    for i, (part, places) in enumerate(slots):
        for t in range(tiles):
            total = parts[part, pl.ds(t * tile, tile), :]
            for k, slot in places:
                total = total + decode(got[k].at[slot, t])
            encode(total, out.at[i, t])


def finish_kernel(places, count, pair_ref, vir_ref, parts, *refs):
    got, out_ref = refs[:count], refs[-1]
    tiles, tile = got[0].shape[1], got[0].shape[2] - TAIL
    low = is_low((tile, LANES))
    pair = pair_ref[0]
    half = tiles * tile
    for t in range(tiles):
        at = pl.ds(t * tile, tile)
        total = parts[0, at, :]
        for k, slot in places:
            total = total + decode(got[k].at[slot, t])
        virt = jnp.where(low, vir_ref[at, 0:1], vir_ref[at, 1:2])
        update = (total / (pair - virt)).T
        out_ref[:, pl.ds(t * tile, tile)] = update[:WIDTH]
        out_ref[:, pl.ds(half + t * tile, tile)] = update[WIDTH:]


def on_device(mesh, amplitudes, integrals, pair_index, eps_occ, eps_vir):
    devices, slabs = mesh.shape["pair"], mesh.shape["slab"]
    chips = devices // CORES
    num_pairs, depth = amplitudes.shape
    rows = integrals.shape[1]
    vir = eps_vir.shape[0]
    chunks = num_pairs // WIDTH
    half = vir // slabs // 2
    part_rows = half * vir
    tile, part_tile = tile_of(rows, 384), tile_of(part_rows, 384)
    tiles, part_tiles = rows // tile, part_rows // part_tile
    me, z = lax.axis_index("pair"), lax.axis_index("slab")
    chip, core = me // CORES, me % CORES

    def to_chip(x, d):
        return lax.ppermute(x, "pair", [(i, i ^ (d * CORES)) for i in range(devices)])

    def limit(mib):
        return pltpu.CompilerParams(vmem_limit_bytes=mib * 1024 * 1024)

    def cost(flops, moved):
        return pl.CostEstimate(flops=flops, bytes_accessed=moved, transcendentals=0)

    smem = pl.BlockSpec(memory_space=pltpu.SMEM)
    vmem = pl.BlockSpec(memory_space=pltpu.VMEM)
    message = jax.ShapeDtypeStruct((tiles, tile + TAIL, LANES), jnp.int16)

    def parcel(count):
        return (count, part_tiles, part_tile + TAIL, LANES)

    column = max((c for c in (384, 256, 128) if rows % c == 0), default=rows)
    transpose = pl.pallas_call(
        transpose_kernel,
        grid=(rows // column,),
        in_specs=[pl.BlockSpec((depth, column), lambda i: (0, i))],
        out_specs=vmem,
        out_shape=jax.ShapeDtypeStruct((rows, depth), jnp.bfloat16),
        compiler_params=limit(16),
        cost_estimate=cost(0, 4 * rows * depth),
        name="transpose",
    )

    def ordered(
        body, flops, inputs, in_specs, out_specs, out_shape, mib, scratch=(), name=None, **more
    ):
        given, made = len(in_specs), len(out_specs)
        moved = sum(x.size * x.dtype.itemsize for x in (*inputs, *out_shape))

        def kernel(*refs):
            token_in, token_out = refs[given], refs[given + 1 + made]
            token_out[...] = token_in[...]
            outs = refs[given + 1 : given + 1 + made]
            body(*refs[:given], *outs, *refs[given + made + 2 :])

        def call(token, *args):
            return pl.pallas_call(
                kernel,
                in_specs=[*in_specs, vmem],
                out_specs=[*out_specs, vmem],
                out_shape=[*out_shape, jax.ShapeDtypeStruct(token.shape, token.dtype)],
                scratch_shapes=scratch,
                compiler_params=limit(mib),
                cost_estimate=cost(flops, moved),
                name=name,
                **more,
            )(*args, token)

        return call, inputs

    def ladder(gathered):
        arrays, pieces = zip(*[(x, (start, count)) for x, start, count in gathered])
        return ordered(
            functools.partial(ladder_kernel, chips, tile, pieces),
            4 * rows * depth * chips * WIDTH,
            [own_t, sib_t, *arrays],
            [vmem] * (2 + len(arrays)),
            [vmem] * chips,
            [message] * chips,
            16,
            [pltpu.VMEM((chips * WIDTH, depth), jnp.bfloat16)],
            name="ladder",
        )

    early = chips == slabs == 4 and tile % vir == 0 and vir // chips % 8 == 0
    side, group = vir // chips, rows // chips
    small, single, pair = (
        jax.ShapeDtypeStruct((*lead, group + TAIL, LANES), jnp.int16) for lead in ((), (1,), (2,))
    )
    grouped = (chips // 2, chips * group, LANES)

    def early_ladder(gathered):
        arrays, pieces = zip(*[(x, (start, count)) for x, start, count in gathered])
        return ordered(
            functools.partial(early_ladder_kernel, chips, tile, vir, pieces),
            4 * rows * depth * chips * WIDTH,
            [place, own_t, sib_t, *arrays],
            [smem] + [vmem] * (2 + len(arrays)),
            [vmem] * (1 + chips // 2),
            [jax.ShapeDtypeStruct(grouped, jnp.float32)]
            + [jax.ShapeDtypeStruct((1, chips, *small.shape), jnp.int16)] * (chips // 2),
            20,
            [
                pltpu.VMEM((chips * WIDTH, depth), jnp.bfloat16),
                pltpu.VMEM((chips, tile, LANES), jnp.float32),
                pltpu.VMEM(grouped, jnp.float32),
            ],
            name="early_ladder",
        )

    def early_sum(places, parts, got):
        return ordered(
            functools.partial(sum_kernel, places, len(got)),
            8 * chips * group * LANES,
            [parts, *got],
            [vmem] * (1 + len(got)),
            [vmem] * 3,
            [small, pair, single],
            8,
            name="early_sum",
        )

    def early_antisym(arrived):
        return ordered(
            functools.partial(early_antisym_kernel, chips, side),
            8 * vir * side * LANES,
            [place, *arrived],
            [smem] + [vmem] * 3,
            [vmem] * 3,
            [jax.ShapeDtypeStruct((group, LANES), jnp.float32), pair, single],
            12,
            [
                pltpu.VMEM((chips * side * side, LANES), jnp.float32),
                pltpu.VMEM((group, LANES), jnp.float32),
            ],
            name="early_antisym",
        )

    def antisym(parcels, arrived):
        return ordered(
            functools.partial(antisym_kernel, chips, slabs, vir),
            8 * vir * vir * LANES,
            [place, *arrived],
            [smem] + [vmem] * chips,
            [vmem] * (1 + parcels),
            [jax.ShapeDtypeStruct((slabs // 2, part_rows, LANES), jnp.float32)]
            + [jax.ShapeDtypeStruct(parcel(slabs // 2 // parcels), jnp.int16)] * parcels,
            16,
            [
                pltpu.VMEM((vir * vir, LANES), jnp.float32),
                pltpu.VMEM((part_rows, LANES), jnp.float32),
            ],
            name="antisym",
        )

    def hop(slots, parts, got):
        return ordered(
            functools.partial(hop_kernel, slots),
            8 * parts.size,
            [parts, *got],
            [vmem] * (1 + len(got)),
            [vmem],
            [jax.ShapeDtypeStruct((len(slots), *got[0].shape[1:]), jnp.int16)],
            8,
            name="hop",
        )

    def finish(r, parts, got, places, so_far):
        given = [] if so_far is None else [so_far]
        if places is None:
            body = functools.partial(early_finish_kernel, chips, side)
        else:
            body = functools.partial(finish_kernel, places, len(got))
        return ordered(
            body,
            16 * part_rows * LANES,
            [eps_pair, eps_virt, parts, *got, *given],
            [pl.BlockSpec((1, 1, LANES), lambda i: (r, 0, 0))]
            + [vmem] * (2 + len(got))
            + [pl.BlockSpec(memory_space=pl.ANY)] * len(given),
            [pl.BlockSpec((WIDTH, 2 * part_rows), lambda i: (r, 0))],
            [jax.ShapeDtypeStruct((num_pairs, 2 * part_rows), jnp.float32)],
            8,
            [] if places else [pltpu.VMEM((part_rows, LANES), jnp.float32)],
            name="finish",
            grid=(1,),
            input_output_aliases={3 + len(got): 0} if given else {},
        )

    in_hbm = functools.partial(pltpu.with_memory_space_constraint, memory_space=pltpu.HBM)
    own_t = transpose(in_hbm(integrals))
    swapped = lax.ppermute(integrals, "pair", [(i, i ^ 1) for i in range(devices)])
    sib_t = transpose(swapped)

    occ_ids = jnp.arange(eps_occ.shape[0], dtype=jnp.int32)

    def pick(ids):
        return jnp.sum(jnp.where(ids[:, None] == occ_ids[None, :], eps_occ[None, :], 0.0), axis=1)

    eps_pair = (pick(pair_index[:, 0]) + pick(pair_index[:, 1])).reshape(chunks, 1, WIDTH)
    eps_pair = jnp.concatenate([eps_pair, eps_pair], axis=2)
    eps_mine = lax.dynamic_slice(eps_vir.reshape(slabs, 2, half), (z, 0, 0), (1, 2, half))[0]
    eps_virt = (eps_mine[:, :, None] + eps_vir[None, None, :]).reshape(2, part_rows).T

    place = jnp.stack([chip, core, z]).astype(jnp.int32)

    def gather(mine, beside):
        count = mine.shape[0]
        if chips != 4:
            return [[mine]] + [[to_chip(mine, d)] for d in range(1, chips)], beside
        one, two = to_chip(mine, 1), to_chip(mine, 2)
        if beside:
            one, two, *beside = lax.optimization_barrier((one, two, *beside))
        low, high = to_chip(two[: count // 2], 1), to_chip(one[count // 2 :], 2)
        return [[mine], [one], [two], [low, high]], beside

    if early:
        head, (own_t, eps_pair, eps_virt) = gather(
            amplitudes[:WIDTH], (own_t, eps_pair, eps_virt)
        )
        head, own_t, sib_t, rest = lax.optimization_barrier(
            (head, own_t, sib_t, amplitudes[WIDTH:])
        )
        tail, _ = gather(rest, ())
        gathered = [(0, head), (WIDTH, tail)]
    else:
        tail, (own_t, sib_t, eps_pair, eps_virt) = gather(
            amplitudes, (own_t, sib_t, eps_pair, eps_virt)
        )
        gathered = [(0, tail)]

    def rows_of(r):
        found = []
        for d in range(chips):
            for base, parts in gathered:
                at = base
                for x in parts[d]:
                    begin = max(r * WIDTH, at)
                    end = min((r + 1) * WIDTH, at + x.shape[0])
                    if begin < end:
                        found.append((x, begin - at, end - begin))
                    at += x.shape[0]
        return found

    def across(x, level):
        return lax.ppermute(x, "slab", [(i, i ^ level) for i in range(slabs)])

    def halved(parts, away):
        each = slabs // 2 // len(away)
        held = {e: [(away[e // 2 // each], e // 2 % each)] for e in range(0, slabs, 2)}

        def listed(wanted):
            arrays = []
            for e in wanted:
                arrays += [x for x, _ in held[e] if not any(x is y for y in arrays)]
            index = {id(x): k for k, x in enumerate(arrays)}
            return arrays, [(e // 2, [(index[id(x)], i) for x, i in held[e]]) for e in wanted]

        level = 2
        while level < slabs:
            leave = [e for e in held if e & level]
            got, slots = listed(leave)
            (out,) = yield hop(slots, parts, got)
            out = across(out, level)
            for i, e in enumerate(leave):
                held[e ^ level].append((out, i))
                del held[e]
            level *= 2
        got, ((_, places),) = listed([0])
        return got, places

    def by_steps(move, pair, single):
        first = move(pair, 1)
        return [first, move(jnp.concatenate([single, first[1:]]), 2)]

    def early_stages(r):
        parts, *away = yield early_ladder(rows_of(r))
        away = [across(x, 1) for x in reversed(away)][::-1]
        got, places = yield from halved(parts, away)
        mine, *sums = yield early_sum(places, parts, got)
        arrived = by_steps(to_chip, *sums)
        steps.extend(arrived)
        own, *blocks = yield early_antisym([mine, *arrived])
        blocks = by_steps(across, *blocks)
        firsts.append(blocks[:1])
        seconds.extend(blocks[1:])
        yield None
        yield finish(r, own, blocks, None, update)

    def stages(r):
        sums = yield ladder(rows_of(r))
        if turns:
            sums, _ = lax.optimization_barrier((sums, turns[-1] + steps + results[-1][:1]))
        arrived = [to_chip(sums[d], d) for d in range(1, chips)]
        turns.append(arrived)
        parcels = slabs // 2 if r == chunks - 1 else 1
        parts, *away = yield antisym(parcels, [sums[0], *arrived])
        if firsts and (early or parcels > 1):
            away, _ = lax.optimization_barrier((away, firsts[-1] + (seconds if parcels > 1 else [])))
        away = [across(x, 1) for x in reversed(away)][::-1]
        firsts.append(away)
        got, places = yield from halved(parts, away)
        yield finish(r, parts, got, places, update)

    hops = max(0, (slabs - 1).bit_length() - 1)

    def when(stage):
        r, k = stage
        if early and r == 0:
            return (20, *[41] * hops, 44, 58, 59, 83)[k]
        if k == 0:
            return 37 + 5 * r if early else 30 + 5 * r
        return 15 * r + (45 if early else 54) + (k - 1) * 17 - (1 if k == 2 + hops else 0)

    order = [(r, k) for r in range(chunks) for k in range(3 + hops + 2 * (early and r == 0))]
    order = sorted(order, key=when)

    turns, firsts, seconds, steps = [], [], [], []
    running = [early_stages(r) if early and r == 0 else stages(r) for r in range(chunks)]
    results = [None] * chunks
    update, token = None, jnp.zeros((8, LANES), jnp.float32)
    for r, k in order:
        step = running[r].send(results[r])
        if step is None:
            continue
        call, inputs = step
        *results[r], token = call(token, *inputs)
        if results[r][0].shape == (num_pairs, 2 * part_rows):
            update = results[r][0]
    return update


def solution(mesh):
    in_specs = (P("pair", "slab"), P("slab", "pair"), P("pair", None), P(), P())
    out_specs = P("pair", "slab")
    return jax.shard_map(
        functools.partial(on_device, mesh),
        mesh=mesh,
        in_specs=in_specs,
        out_specs=out_specs,
        check_vma=False,
    )
```

```python
import functools

import jax
import jax.numpy as jnp
from jax import lax
from jax.experimental import pallas as pl
from jax.experimental.pallas import tpu as pltpu
from jax.sharding import PartitionSpec as P

CORES = 2
WIDTH = 64
LANES = 2 * WIDTH
TAIL = 16
NT = (((1,), (1,)), ((), ()))


def tile_of(rows, most):
    return max(t for t in range(16, most + 1, 16) if rows % t == 0)


def is_low(shape):
    return lax.broadcasted_iota(jnp.int32, shape, len(shape) - 1) < WIDTH


def turn(values):
    return pltpu.roll(values, WIDTH, 1)


def encode(values, out_ref):
    tile = values.shape[0]
    peak = jnp.max(jnp.abs(values), axis=0, keepdims=True)
    power = jnp.ceil(jnp.log2(jnp.maximum(peak, 1e-30) * (1.0 / 32760.0)))
    codes = jnp.round(values * jnp.exp2(-power)).astype(jnp.int32)
    out_ref[pl.ds(0, tile), :] = codes.astype(jnp.int16)
    wide = jnp.broadcast_to(power.astype(jnp.int32), (TAIL, LANES))
    out_ref[pl.ds(tile, TAIL), :] = wide.astype(jnp.int16)


def decode(ref):
    tile = ref.shape[0] - TAIL
    power = ref[pl.ds(tile, TAIL), :].astype(jnp.int32).astype(jnp.float32)[0:1, :]
    return ref[pl.ds(0, tile), :].astype(jnp.int32).astype(jnp.float32) * jnp.exp2(power)


def transpose_kernel(in_ref, out_ref):
    width = in_ref.shape[1]
    at = pl.ds(pl.multiple_of(pl.program_id(0) * width, width), width)
    out_ref[at, :] = in_ref[...].T


def ladder_kernel(chips, tile, pieces, own_ref, sib_ref, *refs):
    rows_in, outs, rhs = refs[: len(pieces)], refs[len(pieces) : -1], refs[-1]
    at = 0
    for ref, (start, count) in zip(rows_in, pieces):
        rhs[pl.ds(at, count), :] = ref[pl.ds(start, count), :]
        at += count
    low = is_low((tile, LANES))
    group = min(4, chips)

    def step(i, carry):
        at = pl.ds(pl.multiple_of(i * tile, tile), tile)
        for first in range(0, chips, group):
            right = rhs[pl.ds(first * WIDTH, group * WIDTH), :]
            own = lax.dot_general(own_ref[at, :], right, NT, preferred_element_type=jnp.float32)
            sib = lax.dot_general(sib_ref[at, :], right, NT, preferred_element_type=jnp.float32)
            for k in range(0, group, 2):
                u = own[:, k * WIDTH : k * WIDTH + LANES]
                v = sib[:, k * WIDTH : k * WIDTH + LANES]
                encode(jnp.where(low, u, turn(v)), outs[first + k].at[i])
                encode(jnp.where(low, turn(u), v), outs[first + k + 1].at[i])
        return carry

    lax.fori_loop(0, own_ref.shape[0] // tile, step, 0)


def early_ladder_kernel(chips, tile, vir, pieces, place_ref, own_ref, sib_ref, *refs):
    rows_in, (parts, *away, rhs, work, sent) = refs[: len(pieces)], refs[len(pieces) :]
    chip, z = place_ref[0], place_ref[2]
    at = 0
    for ref, (start, count) in zip(rows_in, pieces):
        rhs[pl.ds(at, count), :] = ref[pl.ds(start, count), :]
        at += count
    low = is_low((tile, LANES))
    block = vir // chips
    group = own_ref.shape[0] // chips

    def step(i, carry):
        at = pl.ds(pl.multiple_of(i * tile, tile), tile)
        own = lax.dot_general(own_ref[at, :], rhs[...], NT, preferred_element_type=jnp.float32)
        sib = lax.dot_general(sib_ref[at, :], rhs[...], NT, preferred_element_type=jnp.float32)
        for d in range(0, chips, 2):
            u = own[:, d * WIDTH : d * WIDTH + LANES]
            v = sib[:, d * WIDTH : d * WIDTH + LANES]
            work[d] = jnp.where(low, u, turn(v))
            work[d + 1] = jnp.where(low, turn(u), v)
        for e in range(chips):
            column = (chip ^ z ^ e) * block
            out = sent if e % 2 else parts
            for k in range(tile // vir):
                source = pl.ds(pl.multiple_of(k * vir + column, 8), block)
                line = (i * (tile // vir) + k) * block
                for d in range(chips):
                    target = pl.ds(pl.multiple_of(d * group + line, 8), block)
                    out[e // 2, target, :] = work[d, source, :]
        return carry

    lax.fori_loop(0, own_ref.shape[0] // tile, step, 0)
    for i in range(chips // 2):
        for d in range(chips):
            encode(sent[i, pl.ds(d * group, group), :], away[i].at[0, d])


def sum_kernel(places, count, parts, *refs):
    got, (own, pair, single) = refs[:count], refs[count:]
    group = own.shape[0] - TAIL
    for d, out in enumerate((own, pair.at[0], single.at[0], pair.at[1])):
        total = parts[0, pl.ds(d * group, group), :]
        for k, slot in places:
            total = total + decode(got[k].at[slot, d])
        encode(total, out)


def early_antisym_kernel(chips, side, place_ref, *refs):
    mine, pair_in, single_in, own, pair, single, cube, sent = refs
    arrived = (mine, pair_in.at[0], single_in.at[0], single_in.at[1])
    outs = (None, pair.at[0], single.at[0], pair.at[1])
    chip, core, z = place_ref[0], place_ref[1], place_ref[2]
    group = own.shape[0]
    size, held = CORES * group, side // CORES
    low = is_low((group, LANES))
    for d in range(chips):
        values = decode(arrived[d])
        turned = turn(values)
        at_own = pl.multiple_of(d * size + core * group, group)
        at_sib = pl.multiple_of(d * size + (1 - core) * group, group)
        cube[pl.ds(at_own, group), :] = jnp.where(low, values, turned)
        cube[pl.ds(at_sib, group), :] = jnp.where(low, turned, values)
    low = is_low((side, LANES))
    for e in range(chips):
        this = (e ^ z ^ chip) * size
        that = (e ^ chip) * size
        out = sent if e else own
        for a in range(held):
            b = a + held
            here = cube[pl.ds(pl.multiple_of(this + a * side, 8), side), :]
            other = cube[pl.ds(pl.multiple_of(this + b * side, 8), side), :]
            lower = here - cube[pl.ds(that + a, side, stride=side), :]
            upper = other - cube[pl.ds(that + b, side, stride=side), :]
            out[pl.ds(a * side, side), :] = jnp.where(low, lower, upper)
        if e:
            encode(sent[...], outs[e])


def early_finish_kernel(chips, side, pair_ref, vir_ref, own, pair, single, *refs):
    got, (out_ref, cube) = (pair.at[0], single.at[0], single.at[1]), refs[-2:]
    group, rows = own.shape[0], cube.shape[0]
    for e in range(chips):
        values = decode(got[e - 1]) if e else own[...]
        for a in range(group // side):
            target = pl.ds((a * chips + e) * side, side)
            cube[target, :] = values[a * side : (a + 1) * side]
    virt = jnp.where(is_low(cube.shape), vir_ref[:, 0:1], vir_ref[:, 1:2])
    update = (cube[...] / (pair_ref[0] - virt)).T
    out_ref[:, pl.ds(0, rows)] = update[:WIDTH]
    out_ref[:, pl.ds(rows, rows)] = update[WIDTH:]


def antisym_kernel(chips, slabs, vir, place_ref, *refs):
    arrived, (parts, *away, cube, sent) = refs[:chips], refs[chips:]
    chip, core, z = place_ref[0], place_ref[1], place_ref[2]
    tiles, tile = arrived[0].shape[0], arrived[0].shape[1] - TAIL
    rows = tiles * tile
    low = is_low((tile, LANES))
    for d in range(chips):
        base = (chip ^ d) * (CORES * rows)
        for t in range(tiles):
            values = decode(arrived[d].at[t])
            turned = turn(values)
            at_own = pl.multiple_of(base + core * rows + t * tile, tile)
            at_sib = pl.multiple_of(base + (1 - core) * rows + t * tile, tile)
            cube[pl.ds(at_own, tile), :] = jnp.where(low, values, turned)
            cube[pl.ds(at_sib, tile), :] = jnp.where(low, turned, values)

    half = vir // slabs // 2
    low = is_low((vir, LANES))
    part_tile = away[0].shape[2] - TAIL

    def into(slab, out):
        def body(k, carry):
            a = slab * (2 * half) + k
            b = a + half
            here = cube[pl.ds(pl.multiple_of(a * vir, vir), vir), :]
            other = cube[pl.ds(pl.multiple_of(b * vir, vir), vir), :]
            lower = here - cube[pl.ds(a, vir, stride=vir), :]
            upper = other - cube[pl.ds(b, vir, stride=vir), :]
            out[pl.ds(pl.multiple_of(k * vir, vir), vir), :] = jnp.where(low, lower, upper)
            return carry

        lax.fori_loop(0, half, body, 0)

    for e in reversed(range(1, slabs, 2)):
        into(e ^ z, sent)
        out = away[e // 2].at[0] if len(away) > 1 else away[0].at[e // 2]
        for t in range(out.shape[0]):
            encode(sent[pl.ds(t * part_tile, part_tile), :], out.at[t])
    for e in range(0, slabs, 2):
        into(e ^ z, parts.at[e // 2])


def hop_kernel(slots, parts, *refs):
    got, out = refs[:-1], refs[-1]
    tiles, tile = out.shape[1], out.shape[2] - TAIL
    for i, (part, places) in enumerate(slots):
        for t in range(tiles):
            total = parts[part, pl.ds(t * tile, tile), :]
            for k, slot in places:
                total = total + decode(got[k].at[slot, t])
            encode(total, out.at[i, t])


def finish_kernel(places, count, pair_ref, vir_ref, parts, *refs):
    got, out_ref = refs[:count], refs[-1]
    tiles, tile = got[0].shape[1], got[0].shape[2] - TAIL
    low = is_low((tile, LANES))
    pair = pair_ref[0]
    half = tiles * tile
    for t in range(tiles):
        at = pl.ds(t * tile, tile)
        total = parts[0, at, :]
        for k, slot in places:
            total = total + decode(got[k].at[slot, t])
        virt = jnp.where(low, vir_ref[at, 0:1], vir_ref[at, 1:2])
        update = (total / (pair - virt)).T
        out_ref[:, pl.ds(t * tile, tile)] = update[:WIDTH]
        out_ref[:, pl.ds(half + t * tile, tile)] = update[WIDTH:]


def on_device(mesh, amplitudes, integrals, pair_index, eps_occ, eps_vir):
    devices, slabs = mesh.shape["pair"], mesh.shape["slab"]
    chips = devices // CORES
    num_pairs, depth = amplitudes.shape
    rows = integrals.shape[1]
    vir = eps_vir.shape[0]
    chunks = num_pairs // WIDTH
    half = vir // slabs // 2
    part_rows = half * vir
    tile, part_tile = tile_of(rows, 384), tile_of(part_rows, 384)
    tiles, part_tiles = rows // tile, part_rows // part_tile
    me, z = lax.axis_index("pair"), lax.axis_index("slab")
    chip, core = me // CORES, me % CORES

    def to_chip(x, d):
        return lax.ppermute(x, "pair", [(i, i ^ (d * CORES)) for i in range(devices)])

    def limit(mib):
        return pltpu.CompilerParams(vmem_limit_bytes=mib * 1024 * 1024)

    def cost(flops, moved):
        return pl.CostEstimate(flops=flops, bytes_accessed=moved, transcendentals=0)

    smem = pl.BlockSpec(memory_space=pltpu.SMEM)
    vmem = pl.BlockSpec(memory_space=pltpu.VMEM)
    message = jax.ShapeDtypeStruct((tiles, tile + TAIL, LANES), jnp.int16)

    def parcel(count):
        return (count, part_tiles, part_tile + TAIL, LANES)

    column = max((c for c in (384, 256, 128) if rows % c == 0), default=rows)
    transpose = pl.pallas_call(
        transpose_kernel,
        grid=(rows // column,),
        in_specs=[pl.BlockSpec((depth, column), lambda i: (0, i))],
        out_specs=vmem,
        out_shape=pltpu.VMEM((rows, depth), jnp.bfloat16),
        compiler_params=limit(16),
        cost_estimate=cost(0, 4 * rows * depth),
        name="transpose",
    )

    def ordered(
        body, flops, inputs, in_specs, out_specs, out_shape, mib, scratch=(), name=None, **more
    ):
        given, made = len(in_specs), len(out_specs)
        moved = sum(x.size * x.dtype.itemsize for x in (*inputs, *out_shape))

        def kernel(*refs):
            token_in, token_out = refs[given], refs[given + 1 + made]
            token_out[...] = token_in[...]
            outs = refs[given + 1 : given + 1 + made]
            body(*refs[:given], *outs, *refs[given + made + 2 :])

        def call(token, *args):
            return pl.pallas_call(
                kernel,
                in_specs=[*in_specs, vmem],
                out_specs=[*out_specs, vmem],
                out_shape=[
                    pltpu.VMEM(x.shape, x.dtype) if spec is vmem else x
                    for x, spec in zip((*out_shape, token), (*out_specs, vmem))
                ],
                scratch_shapes=scratch,
                compiler_params=limit(mib),
                cost_estimate=cost(flops, moved),
                name=name,
                **more,
            )(*(in_vmem(x) if spec is vmem else x for x, spec in zip((*args, token), (*in_specs, vmem))))

        return call, inputs

    def ladder(gathered):
        arrays, pieces = zip(*[(x, (start, count)) for x, start, count in gathered])
        return ordered(
            functools.partial(ladder_kernel, chips, tile, pieces),
            4 * rows * depth * chips * WIDTH,
            [own_t, sib_t, *arrays],
            [vmem] * (2 + len(arrays)),
            [vmem] * chips,
            [message] * chips,
            16,
            [pltpu.VMEM((chips * WIDTH, depth), jnp.bfloat16)],
            name="ladder",
        )

    early = chips == slabs == 4 and tile % vir == 0 and vir // chips % 8 == 0
    side, group = vir // chips, rows // chips
    small, single, pair = (
        jax.ShapeDtypeStruct((*lead, group + TAIL, LANES), jnp.int16) for lead in ((), (1,), (2,))
    )
    grouped = (chips // 2, chips * group, LANES)

    def early_ladder(gathered):
        arrays, pieces = zip(*[(x, (start, count)) for x, start, count in gathered])
        return ordered(
            functools.partial(early_ladder_kernel, chips, tile, vir, pieces),
            4 * rows * depth * chips * WIDTH,
            [place, own_t, sib_t, *arrays],
            [smem] + [vmem] * (2 + len(arrays)),
            [vmem] * (1 + chips // 2),
            [jax.ShapeDtypeStruct(grouped, jnp.float32)]
            + [jax.ShapeDtypeStruct((1, chips, *small.shape), jnp.int16)] * (chips // 2),
            20,
            [
                pltpu.VMEM((chips * WIDTH, depth), jnp.bfloat16),
                pltpu.VMEM((chips, tile, LANES), jnp.float32),
                pltpu.VMEM(grouped, jnp.float32),
            ],
            name="early_ladder",
        )

    def early_sum(places, parts, got):
        return ordered(
            functools.partial(sum_kernel, places, len(got)),
            8 * chips * group * LANES,
            [parts, *got],
            [vmem] * (1 + len(got)),
            [vmem] * 3,
            [small, pair, single],
            8,
            name="early_sum",
        )

    def early_antisym(arrived):
        return ordered(
            functools.partial(early_antisym_kernel, chips, side),
            8 * vir * side * LANES,
            [place, *arrived],
            [smem] + [vmem] * 3,
            [vmem] * 3,
            [jax.ShapeDtypeStruct((group, LANES), jnp.float32), pair, single],
            12,
            [
                pltpu.VMEM((chips * side * side, LANES), jnp.float32),
                pltpu.VMEM((group, LANES), jnp.float32),
            ],
            name="early_antisym",
        )

    def antisym(parcels, arrived):
        return ordered(
            functools.partial(antisym_kernel, chips, slabs, vir),
            8 * vir * vir * LANES,
            [place, *arrived],
            [smem] + [vmem] * chips,
            [vmem] * (1 + parcels),
            [jax.ShapeDtypeStruct((slabs // 2, part_rows, LANES), jnp.float32)]
            + [jax.ShapeDtypeStruct(parcel(slabs // 2 // parcels), jnp.int16)] * parcels,
            16,
            [
                pltpu.VMEM((vir * vir, LANES), jnp.float32),
                pltpu.VMEM((part_rows, LANES), jnp.float32),
            ],
            name="antisym",
        )

    def hop(slots, parts, got):
        return ordered(
            functools.partial(hop_kernel, slots),
            8 * parts.size,
            [parts, *got],
            [vmem] * (1 + len(got)),
            [vmem],
            [jax.ShapeDtypeStruct((len(slots), *got[0].shape[1:]), jnp.int16)],
            8,
            name="hop",
        )

    def finish(r, parts, got, places, so_far):
        given = [] if so_far is None else [so_far]
        if places is None:
            body = functools.partial(early_finish_kernel, chips, side)
        else:
            body = functools.partial(finish_kernel, places, len(got))
        return ordered(
            body,
            16 * part_rows * LANES,
            [eps_pair, eps_virt, parts, *got, *given],
            [pl.BlockSpec((1, 1, LANES), lambda i: (r, 0, 0))]
            + [vmem] * (2 + len(got))
            + [pl.BlockSpec(memory_space=pl.ANY)] * len(given),
            [pl.BlockSpec((WIDTH, 2 * part_rows), lambda i: (r, 0))],
            [jax.ShapeDtypeStruct((num_pairs, 2 * part_rows), jnp.float32)],
            8,
            [] if places else [pltpu.VMEM((part_rows, LANES), jnp.float32)],
            name="finish",
            grid=(1,),
            input_output_aliases={3 + len(got): 0} if given else {},
        )

    in_vmem = functools.partial(pltpu.with_memory_space_constraint, memory_space=pltpu.VMEM)
    in_hbm = functools.partial(pltpu.with_memory_space_constraint, memory_space=pltpu.HBM)
    own_t = transpose(in_hbm(integrals))
    swapped = lax.ppermute(integrals, "pair", [(i, i ^ 1) for i in range(devices)])
    sib_t = transpose(swapped)

    occ_ids = jnp.arange(eps_occ.shape[0], dtype=jnp.int32)

    def pick(ids):
        return jnp.sum(jnp.where(ids[:, None] == occ_ids[None, :], eps_occ[None, :], 0.0), axis=1)

    eps_pair = (pick(pair_index[:, 0]) + pick(pair_index[:, 1])).reshape(chunks, 1, WIDTH)
    eps_pair = jnp.concatenate([eps_pair, eps_pair], axis=2)
    eps_mine = lax.dynamic_slice(eps_vir.reshape(slabs, 2, half), (z, 0, 0), (1, 2, half))[0]
    eps_virt = (eps_mine[:, :, None] + eps_vir[None, None, :]).reshape(2, part_rows).T

    place = jnp.stack([chip, core, z]).astype(jnp.int32)

    def gather(mine, beside):
        count = mine.shape[0]
        if chips != 4:
            return [[mine]] + [[to_chip(mine, d)] for d in range(1, chips)], beside
        one, two = to_chip(mine, 1), to_chip(mine, 2)
        if beside:
            one, two, *beside = lax.optimization_barrier((one, two, *beside))
        low, high = to_chip(two[: count // 2], 1), to_chip(one[count // 2 :], 2)
        return [[mine], [one], [two], [low, high]], beside

    if early:
        head, (own_t, eps_pair, eps_virt) = gather(
            amplitudes[:WIDTH], (own_t, eps_pair, eps_virt)
        )
        head, own_t, sib_t, rest = lax.optimization_barrier(
            (head, own_t, sib_t, amplitudes[WIDTH:])
        )
        tail, _ = gather(rest, ())
        gathered = [(0, head), (WIDTH, tail)]
    else:
        tail, (own_t, sib_t, eps_pair, eps_virt) = gather(
            amplitudes, (own_t, sib_t, eps_pair, eps_virt)
        )
        gathered = [(0, tail)]

    def rows_of(r):
        found = []
        for d in range(chips):
            for base, parts in gathered:
                at = base
                for x in parts[d]:
                    begin = max(r * WIDTH, at)
                    end = min((r + 1) * WIDTH, at + x.shape[0])
                    if begin < end:
                        found.append((x, begin - at, end - begin))
                    at += x.shape[0]
        return found

    def across(x, level):
        return lax.ppermute(x, "slab", [(i, i ^ level) for i in range(slabs)])

    def halved(parts, away):
        each = slabs // 2 // len(away)
        held = {e: [(away[e // 2 // each], e // 2 % each)] for e in range(0, slabs, 2)}

        def listed(wanted):
            arrays = []
            for e in wanted:
                arrays += [x for x, _ in held[e] if not any(x is y for y in arrays)]
            index = {id(x): k for k, x in enumerate(arrays)}
            return arrays, [(e // 2, [(index[id(x)], i) for x, i in held[e]]) for e in wanted]

        level = 2
        while level < slabs:
            leave = [e for e in held if e & level]
            got, slots = listed(leave)
            (out,) = yield hop(slots, parts, got)
            out = across(out, level)
            for i, e in enumerate(leave):
                held[e ^ level].append((out, i))
                del held[e]
            level *= 2
        got, ((_, places),) = listed([0])
        return got, places

    def by_steps(move, pair, single):
        first = move(pair, 1)
        return [first, move(jnp.concatenate([single, first[1:]]), 2)]

    def early_stages(r):
        parts, *away = yield early_ladder(rows_of(r))
        away = [across(x, 1) for x in reversed(away)][::-1]
        got, places = yield from halved(parts, away)
        mine, *sums = yield early_sum(places, parts, got)
        arrived = by_steps(to_chip, *sums)
        steps.extend(arrived)
        own, *blocks = yield early_antisym([mine, *arrived])
        blocks = by_steps(across, *blocks)
        firsts.append(blocks[:1])
        seconds.extend(blocks[1:])
        yield None
        yield finish(r, own, blocks, None, update)

    def stages(r):
        sums = yield ladder(rows_of(r))
        if turns:
            sums, _ = lax.optimization_barrier((sums, turns[-1] + steps + results[-1][:1]))
        arrived = [to_chip(sums[d], d) for d in range(1, chips)]
        turns.append(arrived)
        parcels = slabs // 2 if r == chunks - 1 else 1
        parts, *away = yield antisym(parcels, [sums[0], *arrived])
        if firsts and (early or parcels > 1):
            away, _ = lax.optimization_barrier((away, firsts[-1] + (seconds if parcels > 1 else [])))
        away = [across(x, 1) for x in reversed(away)][::-1]
        firsts.append(away)
        got, places = yield from halved(parts, away)
        yield finish(r, parts, got, places, update)

    hops = max(0, (slabs - 1).bit_length() - 1)

    def when(stage):
        r, k = stage
        if early and r == 0:
            return (20, *[41] * hops, 44, 58, 59, 83)[k]
        if k == 0:
            return 37 + 5 * r if early else 30 + 5 * r
        return 15 * r + (45 if early else 54) + (k - 1) * 17 - (1 if k == 2 + hops else 0)

    order = [(r, k) for r in range(chunks) for k in range(3 + hops + 2 * (early and r == 0))]
    order = sorted(order, key=when)

    turns, firsts, seconds, steps = [], [], [], []
    running = [early_stages(r) if early and r == 0 else stages(r) for r in range(chunks)]
    results = [None] * chunks
    update, token = None, jnp.zeros((8, LANES), jnp.float32)
    for r, k in order:
        step = running[r].send(results[r])
        if step is None:
            continue
        call, inputs = step
        *results[r], token = call(token, *inputs)
        if results[r][0].shape == (num_pairs, 2 * part_rows):
            update = results[r][0]
    return update


def solution(mesh):
    in_specs = (P("pair", "slab"), P("slab", "pair"), P("pair", None), P(), P())
    out_specs = P("pair", "slab")
    return jax.shard_map(
        functools.partial(on_device, mesh),
        mesh=mesh,
        in_specs=in_specs,
        out_specs=out_specs,
        check_vma=False,
    )
```

```python
import functools

import jax
import jax.numpy as jnp
from jax import lax
from jax.experimental import pallas as pl
from jax.experimental.pallas import tpu as pltpu
from jax.sharding import PartitionSpec as P

CORES = 2
WIDTH = 64
LANES = 2 * WIDTH
TAIL = 16
NT = (((1,), (1,)), ((), ()))


def tile_of(rows, most):
    return max(t for t in range(16, most + 1, 16) if rows % t == 0)


def is_low(shape):
    return lax.broadcasted_iota(jnp.int32, shape, len(shape) - 1) < WIDTH


def turn(values):
    return pltpu.roll(values, WIDTH, 1)


def encode(values, out_ref):
    tile = values.shape[0]
    peak = jnp.max(jnp.abs(values), axis=0, keepdims=True)
    power = jnp.ceil(jnp.log2(jnp.maximum(peak, 1e-30) * (1.0 / 32760.0)))
    codes = jnp.round(values * jnp.exp2(-power)).astype(jnp.int32)
    out_ref[pl.ds(0, tile), :] = codes.astype(jnp.int16)
    wide = jnp.broadcast_to(power.astype(jnp.int32), (TAIL, LANES))
    out_ref[pl.ds(tile, TAIL), :] = wide.astype(jnp.int16)


def decode(ref):
    tile = ref.shape[0] - TAIL
    power = ref[pl.ds(tile, TAIL), :].astype(jnp.int32).astype(jnp.float32)[0:1, :]
    return ref[pl.ds(0, tile), :].astype(jnp.int32).astype(jnp.float32) * jnp.exp2(power)


def transpose_kernel(in_ref, out_ref):
    width = in_ref.shape[1]
    at = pl.ds(pl.multiple_of(pl.program_id(0) * width, width), width)
    out_ref[at, :] = in_ref[...].T


def ladder_kernel(chips, tile, pieces, own_ref, sib_ref, *refs):
    rows_in, outs, rhs = refs[: len(pieces)], refs[len(pieces) : -1], refs[-1]
    at = 0
    for ref, (start, count) in zip(rows_in, pieces):
        rhs[pl.ds(at, count), :] = ref[pl.ds(start, count), :]
        at += count
    low = is_low((tile, LANES))
    group = min(4, chips)

    def step(i, carry):
        at = pl.ds(pl.multiple_of(i * tile, tile), tile)
        for first in range(0, chips, group):
            right = rhs[pl.ds(first * WIDTH, group * WIDTH), :]
            own = lax.dot_general(own_ref[at, :], right, NT, preferred_element_type=jnp.float32)
            sib = lax.dot_general(sib_ref[at, :], right, NT, preferred_element_type=jnp.float32)
            for k in range(0, group, 2):
                u = own[:, k * WIDTH : k * WIDTH + LANES]
                v = sib[:, k * WIDTH : k * WIDTH + LANES]
                encode(jnp.where(low, u, turn(v)), outs[first + k].at[i])
                encode(jnp.where(low, turn(u), v), outs[first + k + 1].at[i])
        return carry

    lax.fori_loop(0, own_ref.shape[0] // tile, step, 0)


def early_ladder_kernel(chips, tile, vir, pieces, place_ref, own_ref, sib_ref, *refs):
    rows_in, (parts, *away, rhs, work, sent) = refs[: len(pieces)], refs[len(pieces) :]
    chip, z = place_ref[0], place_ref[2]
    at = 0
    for ref, (start, count) in zip(rows_in, pieces):
        rhs[pl.ds(at, count), :] = ref[pl.ds(start, count), :]
        at += count
    low = is_low((tile, LANES))
    block = vir // chips
    group = own_ref.shape[0] // chips

    def step(i, carry):
        at = pl.ds(pl.multiple_of(i * tile, tile), tile)
        own = lax.dot_general(own_ref[at, :], rhs[...], NT, preferred_element_type=jnp.float32)
        sib = lax.dot_general(sib_ref[at, :], rhs[...], NT, preferred_element_type=jnp.float32)
        for d in range(0, chips, 2):
            u = own[:, d * WIDTH : d * WIDTH + LANES]
            v = sib[:, d * WIDTH : d * WIDTH + LANES]
            work[d] = jnp.where(low, u, turn(v))
            work[d + 1] = jnp.where(low, turn(u), v)
        for e in range(chips):
            column = (chip ^ z ^ e) * block
            out = sent if e % 2 else parts
            for k in range(tile // vir):
                source = pl.ds(pl.multiple_of(k * vir + column, 8), block)
                line = (i * (tile // vir) + k) * block
                for d in range(chips):
                    target = pl.ds(pl.multiple_of(d * group + line, 8), block)
                    out[e // 2, target, :] = work[d, source, :]
        return carry

    lax.fori_loop(0, own_ref.shape[0] // tile, step, 0)
    for i in range(chips // 2):
        for d in range(chips):
            encode(sent[i, pl.ds(d * group, group), :], away[i].at[0, d])


def sum_kernel(places, count, parts, *refs):
    got, (own, pair, single) = refs[:count], refs[count:]
    group = own.shape[0] - TAIL
    for d, out in enumerate((own, pair.at[0], single.at[0], pair.at[1])):
        total = parts[0, pl.ds(d * group, group), :]
        for k, slot in places:
            total = total + decode(got[k].at[slot, d])
        encode(total, out)


def early_antisym_kernel(chips, side, place_ref, *refs):
    mine, pair_in, single_in, own, pair, single, cube, sent = refs
    arrived = (mine, pair_in.at[0], single_in.at[0], single_in.at[1])
    outs = (None, pair.at[0], single.at[0], pair.at[1])
    chip, core, z = place_ref[0], place_ref[1], place_ref[2]
    group = own.shape[0]
    size, held = CORES * group, side // CORES
    low = is_low((group, LANES))
    for d in range(chips):
        values = decode(arrived[d])
        turned = turn(values)
        at_own = pl.multiple_of(d * size + core * group, group)
        at_sib = pl.multiple_of(d * size + (1 - core) * group, group)
        cube[pl.ds(at_own, group), :] = jnp.where(low, values, turned)
        cube[pl.ds(at_sib, group), :] = jnp.where(low, turned, values)
    low = is_low((side, LANES))
    for e in range(chips):
        this = (e ^ z ^ chip) * size
        that = (e ^ chip) * size
        out = sent if e else own
        for a in range(held):
            b = a + held
            here = cube[pl.ds(pl.multiple_of(this + a * side, 8), side), :]
            other = cube[pl.ds(pl.multiple_of(this + b * side, 8), side), :]
            lower = here - cube[pl.ds(that + a, side, stride=side), :]
            upper = other - cube[pl.ds(that + b, side, stride=side), :]
            out[pl.ds(a * side, side), :] = jnp.where(low, lower, upper)
        if e:
            encode(sent[...], outs[e])


def early_finish_kernel(chips, side, pair_ref, vir_ref, own, pair, single, *refs):
    got, (out_ref, cube) = (pair.at[0], single.at[0], single.at[1]), refs[-2:]
    group, rows = own.shape[0], cube.shape[0]
    for e in range(chips):
        values = decode(got[e - 1]) if e else own[...]
        for a in range(group // side):
            target = pl.ds((a * chips + e) * side, side)
            cube[target, :] = values[a * side : (a + 1) * side]
    virt = jnp.where(is_low(cube.shape), vir_ref[:, 0:1], vir_ref[:, 1:2])
    update = (cube[...] / (pair_ref[0] - virt)).T
    out_ref[:, pl.ds(0, rows)] = update[:WIDTH]
    out_ref[:, pl.ds(rows, rows)] = update[WIDTH:]


def antisym_kernel(chips, slabs, vir, place_ref, *refs):
    arrived, (parts, *away, cube, sent) = refs[:chips], refs[chips:]
    chip, core, z = place_ref[0], place_ref[1], place_ref[2]
    tiles, tile = arrived[0].shape[0], arrived[0].shape[1] - TAIL
    rows = tiles * tile
    low = is_low((tile, LANES))
    for d in range(chips):
        base = (chip ^ d) * (CORES * rows)
        for t in range(tiles):
            values = decode(arrived[d].at[t])
            turned = turn(values)
            at_own = pl.multiple_of(base + core * rows + t * tile, tile)
            at_sib = pl.multiple_of(base + (1 - core) * rows + t * tile, tile)
            cube[pl.ds(at_own, tile), :] = jnp.where(low, values, turned)
            cube[pl.ds(at_sib, tile), :] = jnp.where(low, turned, values)

    half = vir // slabs // 2
    low = is_low((vir, LANES))
    part_tile = away[0].shape[2] - TAIL

    def into(slab, out):
        def body(k, carry):
            a = slab * (2 * half) + k
            b = a + half
            here = cube[pl.ds(pl.multiple_of(a * vir, vir), vir), :]
            other = cube[pl.ds(pl.multiple_of(b * vir, vir), vir), :]
            lower = here - cube[pl.ds(a, vir, stride=vir), :]
            upper = other - cube[pl.ds(b, vir, stride=vir), :]
            out[pl.ds(pl.multiple_of(k * vir, vir), vir), :] = jnp.where(low, lower, upper)
            return carry

        lax.fori_loop(0, half, body, 0)

    for e in reversed(range(1, slabs, 2)):
        into(e ^ z, sent)
        out = away[e // 2].at[0] if len(away) > 1 else away[0].at[e // 2]
        for t in range(out.shape[0]):
            encode(sent[pl.ds(t * part_tile, part_tile), :], out.at[t])
    for e in range(0, slabs, 2):
        into(e ^ z, parts.at[e // 2])


def hop_kernel(slots, parts, *refs):
    got, out = refs[:-1], refs[-1]
    tiles, tile = out.shape[1], out.shape[2] - TAIL
    for i, (part, places) in enumerate(slots):
        for t in range(tiles):
            total = parts[part, pl.ds(t * tile, tile), :]
            for k, slot in places:
                total = total + decode(got[k].at[slot, t])
            encode(total, out.at[i, t])


def finish_kernel(places, count, pair_ref, vir_ref, parts, *refs):
    got, out_ref = refs[:count], refs[-1]
    tiles, tile = got[0].shape[1], got[0].shape[2] - TAIL
    low = is_low((tile, LANES))
    pair = pair_ref[0]
    half = tiles * tile
    for t in range(tiles):
        at = pl.ds(t * tile, tile)
        total = parts[0, at, :]
        for k, slot in places:
            total = total + decode(got[k].at[slot, t])
        virt = jnp.where(low, vir_ref[at, 0:1], vir_ref[at, 1:2])
        update = (total / (pair - virt)).T
        out_ref[:, pl.ds(t * tile, tile)] = update[:WIDTH]
        out_ref[:, pl.ds(half + t * tile, tile)] = update[WIDTH:]


def on_device(mesh, amplitudes, integrals, pair_index, eps_occ, eps_vir):
    devices, slabs = mesh.shape["pair"], mesh.shape["slab"]
    chips = devices // CORES
    num_pairs, depth = amplitudes.shape
    rows = integrals.shape[1]
    vir = eps_vir.shape[0]
    chunks = num_pairs // WIDTH
    half = vir // slabs // 2
    part_rows = half * vir
    tile, part_tile = tile_of(rows, 384), tile_of(part_rows, 384)
    tiles, part_tiles = rows // tile, part_rows // part_tile
    me, z = lax.axis_index("pair"), lax.axis_index("slab")
    chip, core = me // CORES, me % CORES

    def to_chip(x, d):
        return lax.ppermute(x, "pair", [(i, i ^ (d * CORES)) for i in range(devices)])

    def limit(mib):
        return pltpu.CompilerParams(vmem_limit_bytes=mib * 1024 * 1024)

    def cost(flops, moved):
        return pl.CostEstimate(flops=flops, bytes_accessed=moved, transcendentals=0)

    smem = pl.BlockSpec(memory_space=pltpu.SMEM)
    vmem = pl.BlockSpec(memory_space=pltpu.VMEM)
    message = jax.ShapeDtypeStruct((tiles, tile + TAIL, LANES), jnp.int16)

    def parcel(count):
        return (count, part_tiles, part_tile + TAIL, LANES)

    column = max((c for c in (384, 256, 128) if rows % c == 0), default=rows)
    transpose = pl.pallas_call(
        transpose_kernel,
        grid=(rows // column,),
        in_specs=[pl.BlockSpec((depth, column), lambda i: (0, i))],
        out_specs=vmem,
        out_shape=jax.ShapeDtypeStruct((rows, depth), jnp.bfloat16),
        compiler_params=limit(16),
        cost_estimate=cost(0, 4 * rows * depth),
        name="transpose",
    )

    def ordered(
        body, flops, inputs, in_specs, out_specs, out_shape, mib, scratch=(), name=None, **more
    ):
        given, made = len(in_specs), len(out_specs)
        moved = sum(x.size * x.dtype.itemsize for x in (*inputs, *out_shape))

        def kernel(*refs):
            token_in, token_out = refs[given], refs[given + 1 + made]
            token_out[...] = token_in[...]
            outs = refs[given + 1 : given + 1 + made]
            body(*refs[:given], *outs, *refs[given + made + 2 :])

        def call(token, *args):
            return pl.pallas_call(
                kernel,
                in_specs=[*in_specs, vmem],
                out_specs=[*out_specs, vmem],
                out_shape=[*out_shape, jax.ShapeDtypeStruct(token.shape, token.dtype)],
                scratch_shapes=scratch,
                compiler_params=limit(mib),
                cost_estimate=cost(flops, moved),
                name=name,
                **more,
            )(*args, token)

        return call, inputs

    def ladder(gathered):
        arrays, pieces = zip(*[(x, (start, count)) for x, start, count in gathered])
        return ordered(
            functools.partial(ladder_kernel, chips, tile, pieces),
            4 * rows * depth * chips * WIDTH,
            [own_t, sib_t, *arrays],
            [vmem] * (2 + len(arrays)),
            [vmem] * chips,
            [message] * chips,
            16,
            [pltpu.VMEM((chips * WIDTH, depth), jnp.bfloat16)],
            name="ladder",
        )

    early = chips == slabs == 4 and tile % vir == 0 and vir // chips % 8 == 0
    side, group = vir // chips, rows // chips
    small, single, pair = (
        jax.ShapeDtypeStruct((*lead, group + TAIL, LANES), jnp.int16) for lead in ((), (1,), (2,))
    )
    grouped = (chips // 2, chips * group, LANES)

    def early_ladder(gathered):
        arrays, pieces = zip(*[(x, (start, count)) for x, start, count in gathered])
        return ordered(
            functools.partial(early_ladder_kernel, chips, tile, vir, pieces),
            4 * rows * depth * chips * WIDTH,
            [place, own_t, sib_t, *arrays],
            [smem] + [vmem] * (2 + len(arrays)),
            [vmem] * (1 + chips // 2),
            [jax.ShapeDtypeStruct(grouped, jnp.float32)]
            + [jax.ShapeDtypeStruct((1, chips, *small.shape), jnp.int16)] * (chips // 2),
            20,
            [
                pltpu.VMEM((chips * WIDTH, depth), jnp.bfloat16),
                pltpu.VMEM((chips, tile, LANES), jnp.float32),
                pltpu.VMEM(grouped, jnp.float32),
            ],
            name="early_ladder",
        )

    def early_sum(places, parts, got):
        return ordered(
            functools.partial(sum_kernel, places, len(got)),
            8 * chips * group * LANES,
            [parts, *got],
            [vmem] * (1 + len(got)),
            [vmem] * 3,
            [small, pair, single],
            8,
            name="early_sum",
        )

    def early_antisym(arrived):
        return ordered(
            functools.partial(early_antisym_kernel, chips, side),
            8 * vir * side * LANES,
            [place, *arrived],
            [smem] + [vmem] * 3,
            [vmem] * 3,
            [jax.ShapeDtypeStruct((group, LANES), jnp.float32), pair, single],
            12,
            [
                pltpu.VMEM((chips * side * side, LANES), jnp.float32),
                pltpu.VMEM((group, LANES), jnp.float32),
            ],
            name="early_antisym",
        )

    def antisym(parcels, arrived):
        return ordered(
            functools.partial(antisym_kernel, chips, slabs, vir),
            8 * vir * vir * LANES,
            [place, *arrived],
            [smem] + [vmem] * chips,
            [vmem] * (1 + parcels),
            [jax.ShapeDtypeStruct((slabs // 2, part_rows, LANES), jnp.float32)]
            + [jax.ShapeDtypeStruct(parcel(slabs // 2 // parcels), jnp.int16)] * parcels,
            16,
            [
                pltpu.VMEM((vir * vir, LANES), jnp.float32),
                pltpu.VMEM((part_rows, LANES), jnp.float32),
            ],
            name="antisym",
        )

    def hop(slots, parts, got):
        return ordered(
            functools.partial(hop_kernel, slots),
            8 * parts.size,
            [parts, *got],
            [vmem] * (1 + len(got)),
            [vmem],
            [jax.ShapeDtypeStruct((len(slots), *got[0].shape[1:]), jnp.int16)],
            8,
            name="hop",
        )

    def finish(r, parts, got, places, so_far):
        given = [] if so_far is None else [so_far]
        if places is None:
            body = functools.partial(early_finish_kernel, chips, side)
        else:
            body = functools.partial(finish_kernel, places, len(got))
        return ordered(
            body,
            16 * part_rows * LANES,
            [eps_pair, eps_virt, parts, *got, *given],
            [pl.BlockSpec((1, 1, LANES), lambda i: (r, 0, 0))]
            + [vmem] * (2 + len(got))
            + [pl.BlockSpec(memory_space=pl.ANY)] * len(given),
            [pl.BlockSpec((WIDTH, 2 * part_rows), lambda i: (r, 0))],
            [jax.ShapeDtypeStruct((num_pairs, 2 * part_rows), jnp.float32)],
            8,
            [] if places else [pltpu.VMEM((part_rows, LANES), jnp.float32)],
            name="finish",
            grid=(1,),
            input_output_aliases={3 + len(got): 0} if given else {},
        )

    in_hbm = functools.partial(pltpu.with_memory_space_constraint, memory_space=pltpu.HBM)
    swapped = lax.ppermute(integrals, "pair", [(i, i ^ 1) for i in range(devices)])
    sib_t = transpose(swapped)

    occ_ids = jnp.arange(eps_occ.shape[0], dtype=jnp.int32)

    def pick(ids):
        return jnp.sum(jnp.where(ids[:, None] == occ_ids[None, :], eps_occ[None, :], 0.0), axis=1)

    eps_pair = (pick(pair_index[:, 0]) + pick(pair_index[:, 1])).reshape(chunks, 1, WIDTH)
    eps_pair = jnp.concatenate([eps_pair, eps_pair], axis=2)
    eps_mine = lax.dynamic_slice(eps_vir.reshape(slabs, 2, half), (z, 0, 0), (1, 2, half))[0]
    eps_virt = (eps_mine[:, :, None] + eps_vir[None, None, :]).reshape(2, part_rows).T

    place = jnp.stack([chip, core, z]).astype(jnp.int32)
    token = jnp.zeros((8, LANES), jnp.float32)
    rest = amplitudes[WIDTH:]

    ready, eps_pair, eps_virt, place, token, rest = lax.optimization_barrier(
        (integrals, eps_pair, eps_virt, place, token, rest)
    )
    own_t = transpose(in_hbm(ready))

    def gather(mine, beside):
        count = mine.shape[0]
        if chips != 4:
            return [[mine]] + [[to_chip(mine, d)] for d in range(1, chips)], beside
        one, two = to_chip(mine, 1), to_chip(mine, 2)
        if beside:
            one, two, *beside = lax.optimization_barrier((one, two, *beside))
        low, high = to_chip(two[: count // 2], 1), to_chip(one[count // 2 :], 2)
        return [[mine], [one], [two], [low, high]], beside

    if early:
        head, (own_t,) = gather(amplitudes[:WIDTH], (own_t,))
        head, own_t, sib_t, rest = lax.optimization_barrier((head, own_t, sib_t, rest))
        tail, _ = gather(rest, ())
        gathered = [(0, head), (WIDTH, tail)]
    else:
        tail, (own_t, sib_t, eps_pair, eps_virt) = gather(
            amplitudes, (own_t, sib_t, eps_pair, eps_virt)
        )
        gathered = [(0, tail)]

    def rows_of(r):
        found = []
        for d in range(chips):
            for base, parts in gathered:
                at = base
                for x in parts[d]:
                    begin = max(r * WIDTH, at)
                    end = min((r + 1) * WIDTH, at + x.shape[0])
                    if begin < end:
                        found.append((x, begin - at, end - begin))
                    at += x.shape[0]
        return found

    def across(x, level):
        return lax.ppermute(x, "slab", [(i, i ^ level) for i in range(slabs)])

    def halved(parts, away):
        each = slabs // 2 // len(away)
        held = {e: [(away[e // 2 // each], e // 2 % each)] for e in range(0, slabs, 2)}

        def listed(wanted):
            arrays = []
            for e in wanted:
                arrays += [x for x, _ in held[e] if not any(x is y for y in arrays)]
            index = {id(x): k for k, x in enumerate(arrays)}
            return arrays, [(e // 2, [(index[id(x)], i) for x, i in held[e]]) for e in wanted]

        level = 2
        while level < slabs:
            leave = [e for e in held if e & level]
            got, slots = listed(leave)
            (out,) = yield hop(slots, parts, got)
            out = across(out, level)
            for i, e in enumerate(leave):
                held[e ^ level].append((out, i))
                del held[e]
            level *= 2
        got, ((_, places),) = listed([0])
        return got, places

    def by_steps(move, pair, single):
        first = move(pair, 1)
        return [first, move(jnp.concatenate([single, first[1:]]), 2)]

    def early_stages(r):
        parts, *away = yield early_ladder(rows_of(r))
        away = [across(x, 1) for x in reversed(away)][::-1]
        got, places = yield from halved(parts, away)
        mine, *sums = yield early_sum(places, parts, got)
        arrived = by_steps(to_chip, *sums)
        steps.extend(arrived)
        own, *blocks = yield early_antisym([mine, *arrived])
        blocks = by_steps(across, *blocks)
        firsts.append(blocks[:1])
        seconds.extend(blocks[1:])
        yield None
        yield finish(r, own, blocks, None, update)

    def stages(r):
        sums = yield ladder(rows_of(r))
        if turns:
            sums, _ = lax.optimization_barrier((sums, turns[-1] + steps + results[-1][:1]))
        arrived = [to_chip(sums[d], d) for d in range(1, chips)]
        turns.append(arrived)
        parcels = slabs // 2 if r == chunks - 1 else 1
        parts, *away = yield antisym(parcels, [sums[0], *arrived])
        if firsts and (early or parcels > 1):
            away, _ = lax.optimization_barrier((away, firsts[-1] + (seconds if parcels > 1 else [])))
        away = [across(x, 1) for x in reversed(away)][::-1]
        firsts.append(away)
        got, places = yield from halved(parts, away)
        yield finish(r, parts, got, places, update)

    hops = max(0, (slabs - 1).bit_length() - 1)

    def when(stage):
        r, k = stage
        if early and r == 0:
            return (20, *[41] * hops, 44, 58, 59, 83)[k]
        if k == 0:
            return 37 + 5 * r if early else 30 + 5 * r
        return 15 * r + (45 if early else 54) + (k - 1) * 17 - (1 if k == 2 + hops else 0)

    order = [(r, k) for r in range(chunks) for k in range(3 + hops + 2 * (early and r == 0))]
    order = sorted(order, key=when)

    turns, firsts, seconds, steps = [], [], [], []
    running = [early_stages(r) if early and r == 0 else stages(r) for r in range(chunks)]
    results = [None] * chunks
    update = None
    for r, k in order:
        step = running[r].send(results[r])
        if step is None:
            continue
        call, inputs = step
        *results[r], token = call(token, *inputs)
        if results[r][0].shape == (num_pairs, 2 * part_rows):
            update = results[r][0]
    return update


def solution(mesh):
    in_specs = (P("pair", "slab"), P("slab", "pair"), P("pair", None), P(), P())
    out_specs = P("pair", "slab")
    return jax.shard_map(
        functools.partial(on_device, mesh),
        mesh=mesh,
        in_specs=in_specs,
        out_specs=out_specs,
        check_vma=False,
    )
```

```python
import functools

import jax
import jax.numpy as jnp
from jax import lax
from jax.experimental import pallas as pl
from jax.experimental.pallas import tpu as pltpu
from jax.sharding import PartitionSpec as P

CORES = 2
WIDTH = 64
LANES = 2 * WIDTH
TAIL = 16
NT = (((1,), (1,)), ((), ()))


def tile_of(rows, most):
    return max(t for t in range(16, most + 1, 16) if rows % t == 0)


def is_low(shape):
    return lax.broadcasted_iota(jnp.int32, shape, len(shape) - 1) < WIDTH


def turn(values):
    return pltpu.roll(values, WIDTH, 1)


def encode(values, out_ref):
    tile = values.shape[0]
    peak = jnp.max(jnp.abs(values), axis=0, keepdims=True)
    power = jnp.ceil(jnp.log2(jnp.maximum(peak, 1e-30) * (1.0 / 32760.0)))
    codes = jnp.round(values * jnp.exp2(-power)).astype(jnp.int32)
    out_ref[pl.ds(0, tile), :] = codes.astype(jnp.int16)
    wide = jnp.broadcast_to(power.astype(jnp.int32), (TAIL, LANES))
    out_ref[pl.ds(tile, TAIL), :] = wide.astype(jnp.int16)


def decode(ref):
    tile = ref.shape[0] - TAIL
    power = ref[pl.ds(tile, TAIL), :].astype(jnp.int32).astype(jnp.float32)[0:1, :]
    return ref[pl.ds(0, tile), :].astype(jnp.int32).astype(jnp.float32) * jnp.exp2(power)


def transpose_kernel(in_ref, out_ref):
    width = in_ref.shape[1]
    at = pl.ds(pl.multiple_of(pl.program_id(0) * width, width), width)
    out_ref[at, :] = in_ref[...].T


def ladder_kernel(chips, tile, pieces, own_ref, sib_ref, *refs):
    rows_in, outs, rhs = refs[: len(pieces)], refs[len(pieces) : -1], refs[-1]
    at = 0
    for ref, (start, count) in zip(rows_in, pieces):
        rhs[pl.ds(at, count), :] = ref[pl.ds(start, count), :]
        at += count
    low = is_low((tile, LANES))
    group = min(4, chips)

    def step(i, carry):
        at = pl.ds(pl.multiple_of(i * tile, tile), tile)
        for first in range(0, chips, group):
            right = rhs[pl.ds(first * WIDTH, group * WIDTH), :]
            own = lax.dot_general(own_ref[at, :], right, NT, preferred_element_type=jnp.float32)
            sib = lax.dot_general(sib_ref[at, :], right, NT, preferred_element_type=jnp.float32)
            for k in range(0, group, 2):
                u = own[:, k * WIDTH : k * WIDTH + LANES]
                v = sib[:, k * WIDTH : k * WIDTH + LANES]
                encode(jnp.where(low, u, turn(v)), outs[first + k].at[i])
                encode(jnp.where(low, turn(u), v), outs[first + k + 1].at[i])
        return carry

    lax.fori_loop(0, own_ref.shape[0] // tile, step, 0)


def early_ladder_kernel(chips, tile, vir, pieces, place_ref, own_ref, sib_ref, *refs):
    rows_in, (parts, *away, rhs, work, sent) = refs[: len(pieces)], refs[len(pieces) :]
    chip, z = place_ref[0], place_ref[2]
    at = 0
    for ref, (start, count) in zip(rows_in, pieces):
        rhs[pl.ds(at, count), :] = ref[pl.ds(start, count), :]
        at += count
    low = is_low((tile, LANES))
    block = vir // chips
    group = own_ref.shape[0] // chips

    def step(i, carry):
        at = pl.ds(pl.multiple_of(i * tile, tile), tile)
        own = lax.dot_general(own_ref[at, :], rhs[...], NT, preferred_element_type=jnp.float32)
        sib = lax.dot_general(sib_ref[at, :], rhs[...], NT, preferred_element_type=jnp.float32)
        for d in range(0, chips, 2):
            u = own[:, d * WIDTH : d * WIDTH + LANES]
            v = sib[:, d * WIDTH : d * WIDTH + LANES]
            work[d] = jnp.where(low, u, turn(v))
            work[d + 1] = jnp.where(low, turn(u), v)
        for e in range(chips):
            column = (chip ^ z ^ e) * block
            out = sent if e % 2 else parts
            for k in range(tile // vir):
                source = pl.ds(pl.multiple_of(k * vir + column, 8), block)
                line = (i * (tile // vir) + k) * block
                for d in range(chips):
                    target = pl.ds(pl.multiple_of(d * group + line, 8), block)
                    out[e // 2, target, :] = work[d, source, :]
        return carry

    lax.fori_loop(0, own_ref.shape[0] // tile, step, 0)
    for i in range(chips // 2):
        for d in range(chips):
            encode(sent[i, pl.ds(d * group, group), :], away[i].at[0, d])


def sum_kernel(places, count, parts, *refs):
    got, (own, pair, single) = refs[:count], refs[count:]
    group = own.shape[0] - TAIL
    for d, out in enumerate((own, pair.at[0], single.at[0], pair.at[1])):
        total = parts[0, pl.ds(d * group, group), :]
        for k, slot in places:
            total = total + decode(got[k].at[slot, d])
        encode(total, out)


def early_antisym_kernel(chips, side, place_ref, *refs):
    mine, pair_in, single_in, own, pair, single, cube, sent = refs
    arrived = (mine, pair_in.at[0], single_in.at[0], single_in.at[1])
    outs = (None, pair.at[0], single.at[0], pair.at[1])
    chip, core, z = place_ref[0], place_ref[1], place_ref[2]
    group = own.shape[0]
    size, held = CORES * group, side // CORES
    low = is_low((group, LANES))
    for d in range(chips):
        values = decode(arrived[d])
        turned = turn(values)
        at_own = pl.multiple_of(d * size + core * group, group)
        at_sib = pl.multiple_of(d * size + (1 - core) * group, group)
        cube[pl.ds(at_own, group), :] = jnp.where(low, values, turned)
        cube[pl.ds(at_sib, group), :] = jnp.where(low, turned, values)
    low = is_low((side, LANES))
    for e in range(chips):
        this = (e ^ z ^ chip) * size
        that = (e ^ chip) * size
        out = sent if e else own
        for a in range(held):
            b = a + held
            here = cube[pl.ds(pl.multiple_of(this + a * side, 8), side), :]
            other = cube[pl.ds(pl.multiple_of(this + b * side, 8), side), :]
            lower = here - cube[pl.ds(that + a, side, stride=side), :]
            upper = other - cube[pl.ds(that + b, side, stride=side), :]
            out[pl.ds(a * side, side), :] = jnp.where(low, lower, upper)
        if e:
            encode(sent[...], outs[e])


def early_finish_kernel(chips, side, pair_ref, vir_ref, own, pair, single, *refs):
    got, (out_ref, cube) = (pair.at[0], single.at[0], single.at[1]), refs[-2:]
    group, rows = own.shape[0], cube.shape[0]
    for e in range(chips):
        values = decode(got[e - 1]) if e else own[...]
        for a in range(group // side):
            target = pl.ds((a * chips + e) * side, side)
            cube[target, :] = values[a * side : (a + 1) * side]
    virt = jnp.where(is_low(cube.shape), vir_ref[:, 0:1], vir_ref[:, 1:2])
    update = (cube[...] / (pair_ref[0] - virt)).T
    out_ref[:, pl.ds(0, rows)] = update[:WIDTH]
    out_ref[:, pl.ds(rows, rows)] = update[WIDTH:]


def antisym_kernel(chips, slabs, vir, place_ref, *refs):
    arrived, (parts, *away, cube, sent) = refs[:chips], refs[chips:]
    chip, core, z = place_ref[0], place_ref[1], place_ref[2]
    tiles, tile = arrived[0].shape[0], arrived[0].shape[1] - TAIL
    rows = tiles * tile
    low = is_low((tile, LANES))
    for d in range(chips):
        base = (chip ^ d) * (CORES * rows)
        for t in range(tiles):
            values = decode(arrived[d].at[t])
            turned = turn(values)
            at_own = pl.multiple_of(base + core * rows + t * tile, tile)
            at_sib = pl.multiple_of(base + (1 - core) * rows + t * tile, tile)
            cube[pl.ds(at_own, tile), :] = jnp.where(low, values, turned)
            cube[pl.ds(at_sib, tile), :] = jnp.where(low, turned, values)

    half = vir // slabs // 2
    low = is_low((vir, LANES))
    part_tile = away[0].shape[2] - TAIL

    def into(slab, out):
        def body(k, carry):
            a = slab * (2 * half) + k
            b = a + half
            here = cube[pl.ds(pl.multiple_of(a * vir, vir), vir), :]
            other = cube[pl.ds(pl.multiple_of(b * vir, vir), vir), :]
            lower = here - cube[pl.ds(a, vir, stride=vir), :]
            upper = other - cube[pl.ds(b, vir, stride=vir), :]
            out[pl.ds(pl.multiple_of(k * vir, vir), vir), :] = jnp.where(low, lower, upper)
            return carry

        lax.fori_loop(0, half, body, 0)

    for e in reversed(range(1, slabs, 2)):
        into(e ^ z, sent)
        out = away[e // 2].at[0] if len(away) > 1 else away[0].at[e // 2]
        for t in range(out.shape[0]):
            encode(sent[pl.ds(t * part_tile, part_tile), :], out.at[t])
    for e in range(0, slabs, 2):
        into(e ^ z, parts.at[e // 2])


def hop_kernel(slots, parts, *refs):
    got, out = refs[:-1], refs[-1]
    tiles, tile = out.shape[1], out.shape[2] - TAIL
    for i, (part, places) in enumerate(slots):
        for t in range(tiles):
            total = parts[part, pl.ds(t * tile, tile), :]
            for k, slot in places:
                total = total + decode(got[k].at[slot, t])
            encode(total, out.at[i, t])


def finish_kernel(places, count, pair_ref, vir_ref, parts, *refs):
    got, out_ref = refs[:count], refs[-1]
    tiles, tile = got[0].shape[1], got[0].shape[2] - TAIL
    low = is_low((tile, LANES))
    pair = pair_ref[0]
    half = tiles * tile
    for t in range(tiles):
        at = pl.ds(t * tile, tile)
        total = parts[0, at, :]
        for k, slot in places:
            total = total + decode(got[k].at[slot, t])
        virt = jnp.where(low, vir_ref[at, 0:1], vir_ref[at, 1:2])
        update = (total / (pair - virt)).T
        out_ref[:, pl.ds(t * tile, tile)] = update[:WIDTH]
        out_ref[:, pl.ds(half + t * tile, tile)] = update[WIDTH:]


def on_device(mesh, amplitudes, integrals, pair_index, eps_occ, eps_vir):
    devices, slabs = mesh.shape["pair"], mesh.shape["slab"]
    chips = devices // CORES
    num_pairs, depth = amplitudes.shape
    rows = integrals.shape[1]
    vir = eps_vir.shape[0]
    chunks = num_pairs // WIDTH
    half = vir // slabs // 2
    part_rows = half * vir
    tile, part_tile = tile_of(rows, 384), tile_of(part_rows, 384)
    tiles, part_tiles = rows // tile, part_rows // part_tile
    me, z = lax.axis_index("pair"), lax.axis_index("slab")
    chip, core = me // CORES, me % CORES

    def to_chip(x, d):
        return lax.ppermute(x, "pair", [(i, i ^ (d * CORES)) for i in range(devices)])

    def limit(mib):
        return pltpu.CompilerParams(vmem_limit_bytes=mib * 1024 * 1024)

    def cost(flops, moved):
        return pl.CostEstimate(flops=flops, bytes_accessed=moved, transcendentals=0)

    smem = pl.BlockSpec(memory_space=pltpu.SMEM)
    vmem = pl.BlockSpec(memory_space=pltpu.VMEM)
    message = jax.ShapeDtypeStruct((tiles, tile + TAIL, LANES), jnp.int16)

    def parcel(count):
        return (count, part_tiles, part_tile + TAIL, LANES)

    column = max((c for c in (384, 256, 128) if rows % c == 0), default=rows)
    transpose = pl.pallas_call(
        transpose_kernel,
        grid=(rows // column,),
        in_specs=[pl.BlockSpec((depth, column), lambda i: (0, i))],
        out_specs=vmem,
        out_shape=jax.ShapeDtypeStruct((rows, depth), jnp.bfloat16),
        compiler_params=limit(16),
        cost_estimate=cost(0, 4 * rows * depth),
        name="transpose",
    )

    def ordered(
        body, flops, inputs, in_specs, out_specs, out_shape, mib, scratch=(), name=None, **more
    ):
        given, made = len(in_specs), len(out_specs)
        moved = sum(x.size * x.dtype.itemsize for x in (*inputs, *out_shape))

        def kernel(*refs):
            token_in, token_out = refs[given], refs[given + 1 + made]
            token_out[...] = token_in[...]
            outs = refs[given + 1 : given + 1 + made]
            body(*refs[:given], *outs, *refs[given + made + 2 :])

        def call(token, *args):
            return pl.pallas_call(
                kernel,
                in_specs=[*in_specs, vmem],
                out_specs=[*out_specs, vmem],
                out_shape=[*out_shape, jax.ShapeDtypeStruct(token.shape, token.dtype)],
                scratch_shapes=scratch,
                compiler_params=limit(mib),
                cost_estimate=cost(flops, moved),
                name=name,
                **more,
            )(*args, token)

        return call, inputs

    def ladder(gathered):
        arrays, pieces = zip(*[(x, (start, count)) for x, start, count in gathered])
        return ordered(
            functools.partial(ladder_kernel, chips, tile, pieces),
            4 * rows * depth * chips * WIDTH,
            [own_t, sib_t, *arrays],
            [vmem] * (2 + len(arrays)),
            [vmem] * chips,
            [message] * chips,
            16,
            [pltpu.VMEM((chips * WIDTH, depth), jnp.bfloat16)],
            name="ladder",
        )

    early = chips == slabs == 4 and tile % vir == 0 and vir // chips % 8 == 0
    side, group = vir // chips, rows // chips
    small, single, pair = (
        jax.ShapeDtypeStruct((*lead, group + TAIL, LANES), jnp.int16) for lead in ((), (1,), (2,))
    )
    grouped = (chips // 2, chips * group, LANES)

    def early_ladder(gathered):
        arrays, pieces = zip(*[(x, (start, count)) for x, start, count in gathered])
        return ordered(
            functools.partial(early_ladder_kernel, chips, tile, vir, pieces),
            4 * rows * depth * chips * WIDTH,
            [place, own_t, sib_t, *arrays],
            [smem] + [vmem] * (2 + len(arrays)),
            [vmem] * (1 + chips // 2),
            [jax.ShapeDtypeStruct(grouped, jnp.float32)]
            + [jax.ShapeDtypeStruct((1, chips, *small.shape), jnp.int16)] * (chips // 2),
            20,
            [
                pltpu.VMEM((chips * WIDTH, depth), jnp.bfloat16),
                pltpu.VMEM((chips, tile, LANES), jnp.float32),
                pltpu.VMEM(grouped, jnp.float32),
            ],
            name="early_ladder",
        )

    def early_sum(places, parts, got):
        return ordered(
            functools.partial(sum_kernel, places, len(got)),
            8 * chips * group * LANES,
            [parts, *got],
            [vmem] * (1 + len(got)),
            [vmem] * 3,
            [small, pair, single],
            8,
            name="early_sum",
        )

    def early_antisym(arrived):
        return ordered(
            functools.partial(early_antisym_kernel, chips, side),
            8 * vir * side * LANES,
            [place, *arrived],
            [smem] + [vmem] * 3,
            [vmem] * 3,
            [jax.ShapeDtypeStruct((group, LANES), jnp.float32), pair, single],
            12,
            [
                pltpu.VMEM((chips * side * side, LANES), jnp.float32),
                pltpu.VMEM((group, LANES), jnp.float32),
            ],
            name="early_antisym",
        )

    def antisym(parcels, arrived):
        return ordered(
            functools.partial(antisym_kernel, chips, slabs, vir),
            8 * vir * vir * LANES,
            [place, *arrived],
            [smem] + [vmem] * chips,
            [vmem] * (1 + parcels),
            [jax.ShapeDtypeStruct((slabs // 2, part_rows, LANES), jnp.float32)]
            + [jax.ShapeDtypeStruct(parcel(slabs // 2 // parcels), jnp.int16)] * parcels,
            16,
            [
                pltpu.VMEM((vir * vir, LANES), jnp.float32),
                pltpu.VMEM((part_rows, LANES), jnp.float32),
            ],
            name="antisym",
        )

    def hop(slots, parts, got):
        return ordered(
            functools.partial(hop_kernel, slots),
            8 * parts.size,
            [parts, *got],
            [vmem] * (1 + len(got)),
            [vmem],
            [jax.ShapeDtypeStruct((len(slots), *got[0].shape[1:]), jnp.int16)],
            8,
            name="hop",
        )

    def finish(r, parts, got, places, so_far):
        given = [] if so_far is None else [so_far]
        if places is None:
            body = functools.partial(early_finish_kernel, chips, side)
        else:
            body = functools.partial(finish_kernel, places, len(got))
        return ordered(
            body,
            16 * part_rows * LANES,
            [eps_pair, eps_virt, parts, *got, *given],
            [pl.BlockSpec((1, 1, LANES), lambda i: (r, 0, 0))]
            + [vmem] * (2 + len(got))
            + [pl.BlockSpec(memory_space=pl.ANY)] * len(given),
            [pl.BlockSpec((WIDTH, 2 * part_rows), lambda i: (r, 0))],
            [jax.ShapeDtypeStruct((num_pairs, 2 * part_rows), jnp.float32)],
            8,
            [] if places else [pltpu.VMEM((part_rows, LANES), jnp.float32)],
            name="finish",
            grid=(1,),
            input_output_aliases={3 + len(got): 0} if given else {},
        )

    in_hbm = functools.partial(pltpu.with_memory_space_constraint, memory_space=pltpu.HBM)
    swapped = lax.ppermute(integrals, "pair", [(i, i ^ 1) for i in range(devices)])
    sib_t = transpose(swapped)

    occ_ids = jnp.arange(eps_occ.shape[0], dtype=jnp.int32)

    def pick(ids):
        return jnp.sum(jnp.where(ids[:, None] == occ_ids[None, :], eps_occ[None, :], 0.0), axis=1)

    eps_pair = (pick(pair_index[:, 0]) + pick(pair_index[:, 1])).reshape(chunks, 1, WIDTH)
    eps_pair = jnp.concatenate([eps_pair, eps_pair], axis=2)
    eps_mine = lax.dynamic_slice(eps_vir.reshape(slabs, 2, half), (z, 0, 0), (1, 2, half))[0]
    eps_virt = (eps_mine[:, :, None] + eps_vir[None, None, :]).reshape(2, part_rows).T

    place = jnp.stack([chip, core, z]).astype(jnp.int32)
    token = jnp.zeros((8, LANES), jnp.float32)
    rest = amplitudes[WIDTH:]

    ready, eps_pair, eps_virt, place, token, rest = lax.optimization_barrier(
        (integrals, eps_pair, eps_virt, place, token, rest)
    )
    own_t = transpose(in_hbm(ready))

    def gather(mine, beside):
        count = mine.shape[0]
        if chips != 4:
            return [[mine]] + [[to_chip(mine, d)] for d in range(1, chips)], beside
        one, two = to_chip(mine, 1), to_chip(mine, 2)
        if beside:
            one, two, *beside = lax.optimization_barrier((one, two, *beside))
        low, high = to_chip(two[: count // 2], 1), to_chip(one[count // 2 :], 2)
        return [[mine], [one], [two], [low, high]], beside

    if early:
        head, (own_t,) = gather(amplitudes[:WIDTH], (own_t,))
        head, own_t, sib_t, rest = lax.optimization_barrier((head, own_t, sib_t, rest))
        tail, _ = gather(rest, ())
        gathered = [(0, head), (WIDTH, tail)]
    else:
        tail, (own_t, sib_t, eps_pair, eps_virt) = gather(
            amplitudes, (own_t, sib_t, eps_pair, eps_virt)
        )
        gathered = [(0, tail)]

    def rows_of(r):
        found = []
        for d in range(chips):
            for base, parts in gathered:
                at = base
                for x in parts[d]:
                    begin = max(r * WIDTH, at)
                    end = min((r + 1) * WIDTH, at + x.shape[0])
                    if begin < end:
                        found.append((x, begin - at, end - begin))
                    at += x.shape[0]
        return found

    def across(x, level):
        return lax.ppermute(x, "slab", [(i, i ^ level) for i in range(slabs)])

    def halved(parts, away):
        each = slabs // 2 // len(away)
        held = {e: [(away[e // 2 // each], e // 2 % each)] for e in range(0, slabs, 2)}

        def listed(wanted):
            arrays = []
            for e in wanted:
                arrays += [x for x, _ in held[e] if not any(x is y for y in arrays)]
            index = {id(x): k for k, x in enumerate(arrays)}
            return arrays, [(e // 2, [(index[id(x)], i) for x, i in held[e]]) for e in wanted]

        level = 2
        while level < slabs:
            leave = [e for e in held if e & level]
            got, slots = listed(leave)
            (out,) = yield hop(slots, parts, got)
            out = across(out, level)
            for i, e in enumerate(leave):
                held[e ^ level].append((out, i))
                del held[e]
            level *= 2
        got, ((_, places),) = listed([0])
        return got, places

    def by_steps(move, pair, single):
        first = move(pair, 1)
        return [first, move(jnp.concatenate([single, first[1:]]), 2)]

    def early_stages(r):
        parts, *away = yield early_ladder(rows_of(r))
        away = [across(x, 1) for x in reversed(away)][::-1]
        got, places = yield from halved(parts, away)
        if turns:
            got, _ = lax.optimization_barrier((got, turns[-1]))
        mine, *sums = yield early_sum(places, parts, got)
        arrived = by_steps(to_chip, *sums)
        steps.extend(arrived)
        own, *blocks = yield early_antisym([mine, *arrived])
        blocks = by_steps(across, *blocks)
        seconds.extend(blocks[1:])
        yield None
        yield finish(r, own, blocks, None, update)

    def stages(r):
        sums = yield ladder(rows_of(r))
        if turns:
            sums, _ = lax.optimization_barrier((sums, turns[-1] + steps + results[-1][:1]))
        arrived = [to_chip(sums[d], d) for d in range(1, chips)]
        turns.append(arrived)
        yield None
        parcels = slabs // 2 if r == chunks - 1 else 1
        parts, *away = yield antisym(parcels, [sums[0], *arrived])
        if firsts and (early or parcels > 1):
            away, _ = lax.optimization_barrier((away, firsts[-1] + (seconds if parcels > 1 else [])))
        away = [across(x, 1) for x in reversed(away)][::-1]
        firsts.append(away)
        got, places = yield from halved(parts, away)
        yield finish(r, parts, got, places, update)

    hops = max(0, (slabs - 1).bit_length() - 1)

    def when(stage):
        r, k = stage
        if early and r == 0:
            return (20, *[41] * hops, 48, 62, 63, 83)[k]
        if k == 0:
            return 37 + 5 * r if early else 30 + 5 * r
        if k == 1:
            return (47.5 if r == 1 else 64) if early else 53 + r / chunks
        start = 15 * r + (45 if early else 54)
        return start + (k - 2) * (14 if early and r == 1 else 17) - (1 if k == 3 + hops else 0)

    order = [(r, k) for r in range(chunks) for k in range(4 + hops + (early and r == 0))]
    order = sorted(order, key=when)

    turns, firsts, seconds, steps = [], [], [], []
    running = [early_stages(r) if early and r == 0 else stages(r) for r in range(chunks)]
    results = [None] * chunks
    update = None
    for r, k in order:
        step = running[r].send(results[r])
        if step is None:
            continue
        call, inputs = step
        *results[r], token = call(token, *inputs)
        if results[r][0].shape == (num_pairs, 2 * part_rows):
            update = results[r][0]
    return update


def solution(mesh):
    in_specs = (P("pair", "slab"), P("slab", "pair"), P("pair", None), P(), P())
    out_specs = P("pair", "slab")
    return jax.shard_map(
        functools.partial(on_device, mesh),
        mesh=mesh,
        in_specs=in_specs,
        out_specs=out_specs,
        check_vma=False,
    )
```
